32 devices in a mesh: expert: 8 (over z, x), mp: 4 (over y, core).
Axes of the slice: x: 2, y: 2, z: 4, core: 2. Of those that a mesh axis runs over, the one named last changes fastest.
Arguments:
- features: bfloat16 [9456, 768], P('expert'), may hold values from -6 to 6
- norm_gains: float32 [2, 768], P(None, ('expert', 'mp')), may hold values from 0.25 to 1.75
- norm_shifts: float32 [2, 768], P(None, ('expert', 'mp')), may hold values from -0.6 to 0.6
- attention_bias: float32 [2, 768], P(None, ('expert', 'mp')), may hold values from -0.6 to 0.6
- output_bias: float32 [768], P(('expert', 'mp')), may hold values from -0.6 to 0.6
- project_weight: float32 [768, 3, 768], P('expert', None, 'mp'), may hold values from -0.21875 to 0.21875
- merge_weight: float32 [768, 768], P('mp', 'expert'), may hold values from -0.625 to 0.625
- router_weight: float32 [768, 8], P('expert'), may hold values from -0.15625 to 0.15625
- router_noise: float32 [9456, 8], P('expert'), may hold values from -1.8 to 1.8
- routes: int32 [9456, 2], P('expert'), may hold values from 0 to 7, as said below
- slot_numbers: int32 [9456, 2], P('expert'), may hold values from 0 to 442, as said below
- expand_weight: float32 [8, 768, 3072], P('expert', None, 'mp'), may hold values from -0.21875 to 0.21875
- expand_bias: float32 [8, 3072], P('expert', 'mp'), may hold values from -0.6 to 0.6
- contract_weight: float32 [8, 3072, 768], P('expert', 'mp'), may hold values from -0.15625 to 0.15625
- contract_bias: float32 [8, 768], P('expert'), may hold values from -0.6 to 0.6
- cotangent: float32 [9456, 768], P('expert'), may hold values from -6 to 6
Outputs:
- block_output: bfloat16 [9456, 768], P('expert', 'mp')
- feature_grad: float32 [9456, 768], P('expert')
- gain_grad: float32 [2, 768], P(None, ('expert', 'mp'))
- shift_grad: float32 [2, 768], P(None, ('expert', 'mp'))
- attention_bias_grad: float32 [2, 768], P(None, ('expert', 'mp'))
- output_bias_grad: float32 [768], P(('expert', 'mp'))
- project_grad: float32 [768, 3, 768], P('expert', None, 'mp')
- merge_grad: float32 [768, 768], P('mp', 'expert')
- router_grad: float32 [768, 8], P('expert')
- expand_grad: float32 [8, 768, 3072], P('expert', None, 'mp')
- expand_bias_grad: float32 [8, 3072], P('expert', 'mp')
- contract_grad: float32 [8, 3072, 768], P('expert', 'mp')
- contract_bias_grad: float32 [8, 768], P('expert')
The draws below stay inside these ranges and needn't reach their ends.
Inputs may be any that keep to these rules, and one draw needn't show every extreme that they name: `routes`: in each aligned block of 1182 rows (the tokens of one index of the expert axis) the two entries of a row differ, every expert is named at least once and at most 443 times, and some expert is named exactly 443 times. `slot_numbers`: in each aligned block of 1182 rows, the routes that name one expert carry distinct slot numbers 0 to their count minus one.
All inputs are finite; a program needn't handle non-finite values.
Results may differ from the reference program's by a relative error of at most 0.02.
Values may be sent and summed in bfloat16 or wider, within the bound.
A program may use at most 192 MiB of HBM per device.

```python
import jax
import jax.numpy as jnp
import numpy as np
from jax import lax

D = 768
HEADS = 12
HEAD = 64
FF = 3072
TOP = 2
SEQ = 197
TOK_DEV = 1182
TOKENS = 9456
EXPERTS = 8
CAP = 443
N_EXPERT = 8


def route_table(key):
    base_key = jax.random.fold_in(key, 4711)
    full_count = EXPERTS // 4
    remaining = 2 * TOK_DEV - full_count * CAP
    share_each, extra_count = divmod(remaining, EXPERTS - full_count)
    profile = jnp.asarray(np.array([CAP] * full_count + [share_each + 1] * extra_count + [share_each] * (EXPERTS - full_count - extra_count), dtype=np.int32))
    blocks = TOKENS // TOK_DEV
    step_most = max(2, share_each // 2 + 1)

    def one_block(block_key):
        block_keys = jax.random.split(block_key, 4)
        order = jax.random.permutation(block_keys[0], EXPERTS).astype(jnp.int32)
        counts = jnp.zeros((EXPERTS,), jnp.int32).at[order].set(profile)
        keeper = order[0]

        def shuffle(turn_index, counts):
            turn_key = jax.random.fold_in(block_keys[1], turn_index)
            chosen_pair = jax.random.randint(turn_key, (2,), 0, EXPERTS)
            amount = jax.random.randint(jax.random.fold_in(turn_key, 1), (), 1, step_most)
            giving = chosen_pair[0]
            taking = chosen_pair[1]
            amount = jnp.minimum(amount, jnp.minimum(counts[giving] - 1, CAP - counts[taking]))
            allowed = (giving != taking) & (giving != keeper) & (taking != keeper) & (amount > 0)
            amount = jnp.where(allowed, amount, 0).astype(jnp.int32)
            return counts.at[giving].add(-amount).at[taking].add(amount)
        counts = lax.fori_loop(0, 4 * EXPERTS, shuffle, counts)
        labels = jnp.repeat(jnp.arange(EXPERTS, dtype=jnp.int32), counts, total_repeat_length=2 * TOK_DEV)
        starts = jnp.cumsum(counts) - counts
        positions = jnp.arange(2 * TOK_DEV, dtype=jnp.int32) - starts[labels]
        pair_experts = jnp.stack([labels[:TOK_DEV], labels[TOK_DEV:]], axis=1)
        pair_slots = jnp.stack([positions[:TOK_DEV], positions[TOK_DEV:]], axis=1)
        flipped = jax.random.randint(block_keys[2], (TOK_DEV, 1), 0, 2)
        pair_experts = jnp.where(flipped == 1, pair_experts[:, ::-1], pair_experts)
        pair_slots = jnp.where(flipped == 1, pair_slots[:, ::-1], pair_slots)
        token_order = jax.random.permutation(block_keys[3], TOK_DEV)
        return (pair_experts[token_order], pair_slots[token_order])
    all_routes, all_slots = jax.vmap(one_block)(jax.random.split(base_key, blocks))
    return (all_routes.reshape(TOKENS, 2).astype(jnp.int32), all_slots.reshape(TOKENS, 2).astype(jnp.int32))


def draw_routes(key, part):
    return route_table(key)[0]


def draw_slot_numbers(key, part):
    return route_table(key)[1]


def level_of(own_key, dims, pieces, low, top_value):
    level, own = 1.0, jax.random.fold_in(own_key, 6)
    for position, blocks in pieces:
        steps = jnp.exp(jax.random.uniform(jax.random.fold_in(own, position), (blocks,), jnp.float32, low / len(pieces), top_value / len(pieces)))
        level = level * jnp.repeat(steps, dims[position] // blocks).reshape([-1 if axis == position else 1 for axis in range(len(dims))])
    return level


def scatter_about(key, extent, width, bound, cuts=(), held_as=jnp.bfloat16):
    values = jax.random.normal(key, extent, jnp.float32) * width
    if len(cuts) > 0:
        values = level_of(key, extent, cuts, -0.22, 0.18) * values
    return jnp.clip(values, min=-bound, max=bound).astype(held_as)


def setup_inputs(seed: int = 0) -> dict:
    key_list = jax.random.split(jax.random.key(seed), 17)
    features = scatter_about(key_list[0], (TOKENS, D), 1.0, 6.0, ((0, 8),))
    norm_gains = jnp.clip(1.0 + 0.15 * jax.random.normal(key_list[1], (2, D), jnp.float32), 0.25, 1.75)
    norm_shifts = scatter_about(key_list[2], (2, D), 0.1, 0.6, ((1, 32),), jnp.float32)
    attention_bias = scatter_about(key_list[3], (2, D), 0.1, 0.6, ((1, 32),), jnp.float32)
    output_bias = scatter_about(key_list[4], (D,), 0.1, 0.6, ((0, 32),), jnp.float32)
    project_weight = scatter_about(key_list[5], (D, 3, D), D ** -0.5, 0.21875, ((0, 8), (2, 4)), jnp.float32)
    merge_weight = scatter_about(key_list[6], (D, D), (D // 8) ** -0.5, 0.625, ((0, 4), (1, 8)), jnp.float32)
    router_weight = scatter_about(key_list[7], (D, EXPERTS), (2 * D) ** -0.5, 0.15625, ((0, 8),), jnp.float32)
    router_noise = scatter_about(key_list[8], (TOKENS, EXPERTS), 0.3, 1.8, ((0, 8),), jnp.float32)
    routes = draw_routes(jax.random.fold_in(key_list[16], 71), 0)
    slot_numbers = draw_slot_numbers(jax.random.fold_in(key_list[16], 71), 0)
    expand_weight = scatter_about(key_list[11], (EXPERTS, D, FF), D ** -0.5, 0.21875, ((0, 8), (2, 4)), jnp.float32)
    expand_bias = scatter_about(key_list[12], (EXPERTS, FF), 0.1, 0.6, ((0, 8), (1, 4)), jnp.float32)
    contract_weight = scatter_about(key_list[13], (EXPERTS, FF, D), (FF // 2) ** -0.5, 0.15625, ((0, 8), (1, 4)), jnp.float32)
    contract_bias = scatter_about(key_list[14], (EXPERTS, D), 0.1, 0.6, ((0, 8),), jnp.float32)
    cotangent = scatter_about(key_list[15], (TOKENS, D), 1.0, 6.0, ((0, 8),), jnp.float32)
    return dict(features=features, norm_gains=norm_gains, norm_shifts=norm_shifts, attention_bias=attention_bias, output_bias=output_bias, project_weight=project_weight, merge_weight=merge_weight, router_weight=router_weight, router_noise=router_noise, routes=routes, slot_numbers=slot_numbers, expand_weight=expand_weight, expand_bias=expand_bias, contract_weight=contract_weight, contract_bias=contract_bias, cotangent=cotangent)


@jax.custom_vjp
def low(v):
    return lax.optimization_barrier(v.astype(jnp.bfloat16)).astype(jnp.float32)

@jax.custom_vjp
def low_back(v):
    return v

def low_keep(v):
    return (low(v), None)

def low_pass(kept, grad):
    return (grad,)

def back_keep(v):
    return (v, None)

def back_low(kept, grad):
    return (low(grad),)
low.defvjp(low_keep, low_pass)
low_back.defvjp(back_keep, back_low)
highest = lax.Precision.HIGHEST
eps_norm = 1e-06

def layer_norm(value, gain, shift):
    mean_value = lax.optimization_barrier(jnp.mean(value, axis=-1, keepdims=True))
    centred = value - mean_value
    variance = lax.optimization_barrier(jnp.mean(centred * centred, axis=-1, keepdims=True))
    return centred * lax.rsqrt(variance + eps_norm) * gain + shift

def attend(rows, project_low, query_bias, value_bias, merge_low):
    count = rows.shape[0]
    images = count // SEQ
    mixed = jnp.einsum('td,dcf->ctf', rows, project_low, precision=highest)
    query = low(low_back(mixed[0] + query_bias)).reshape(images, SEQ, HEADS, HEAD)
    key_rows = low(low_back(mixed[1])).reshape(images, SEQ, HEADS, HEAD)
    values = low(low_back(mixed[2] + value_bias)).reshape(images, SEQ, HEADS, HEAD)
    scores = low_back(jnp.einsum('bqhe,bkhe->bhqk', query, key_rows, precision=highest) * HEAD ** (-0.5))
    attn_weights = jax.nn.softmax(scores, axis=-1)
    attended = jnp.einsum('bhqk,bkhe->bqhe', low(attn_weights), values, precision=highest).reshape(count, D)
    attended = low(low_back(attended))
    return low_back(jnp.dot(attended, merge_low, precision=highest))

def forward(features, norm_gains, norm_shifts, attention_bias, output_bias, project_weight, merge_weight, router_weight, expand_weight, expand_bias, contract_weight, contract_bias, router_noise, routes, slot_numbers):
    normed = low(layer_norm(features, norm_gains[0], norm_shifts[0]))
    project_low = low(project_weight)
    merge_low = low(merge_weight)

    def group_step(rows):
        return attend(rows, project_low, attention_bias[0], attention_bias[1], merge_low)
    projected = lax.map(jax.checkpoint(group_step), normed.reshape(N_EXPERT, TOK_DEV, D)).reshape(TOKENS, D)
    hidden = features + projected + output_bias
    second = low(layer_norm(hidden, norm_gains[1], norm_shifts[1]))
    logits = low_back(jnp.dot(second, low(router_weight), precision=highest)) + router_noise
    picked = jnp.take_along_axis(logits, routes, axis=1)
    gate_values = jax.nn.softmax(picked, axis=1)
    source_index = (jnp.arange(TOKENS, dtype=jnp.int32) // TOK_DEV)[:, None]
    slot_index = ((routes * N_EXPERT + source_index) * CAP + slot_numbers).reshape(-1).astype(jnp.int32)
    buffer = jnp.zeros((EXPERTS * N_EXPERT * CAP, D), jnp.float32).at[slot_index].set(jnp.repeat(second, TOP, axis=0))
    buffer = low_back(buffer).reshape(EXPERTS, N_EXPERT * CAP, D)

    def expert_step(items):
        block, first_weight, first_bias, second_weight, second_bias = items
        inner_value = low_back(jnp.dot(block, low(first_weight), precision=highest) + first_bias)
        active = low(jax.nn.gelu(inner_value, approximate=False))
        return low(low_back(jnp.dot(active, low(second_weight), precision=highest) + second_bias))
    returned = lax.map(jax.checkpoint(expert_step), (buffer, expand_weight, expand_bias, contract_weight, contract_bias)).reshape(-1, D)
    picked_rows = returned[slot_index].reshape(TOKENS, TOP, D)
    combined = lax.optimization_barrier(jnp.sum(gate_values[:, :, None] * picked_rows, axis=1))
    return hidden + combined

def reference(features, norm_gains, norm_shifts, attention_bias, output_bias, project_weight, merge_weight, router_weight, router_noise, routes, slot_numbers, expand_weight, expand_bias, contract_weight, contract_bias, cotangent):
    primals = (features.astype(jnp.float32), norm_gains, norm_shifts, attention_bias, output_bias, project_weight, merge_weight, router_weight, expand_weight, expand_bias, contract_weight, contract_bias)

    def wrapped(*params):
        return forward(*params, router_noise, routes, slot_numbers)
    output, pullback = jax.vjp(wrapped, *primals)
    grads = pullback(cotangent)
    return (output.astype(jnp.bfloat16), grads[0], grads[1], grads[2], grads[3], grads[4], grads[5], grads[6], grads[7], grads[8], grads[9], grads[10], grads[11])
```

```python
import functools

import jax
import jax.numpy as jnp
from jax import lax
from jax.experimental import pallas as pl
from jax.experimental.pallas import tpu as pltpu
from jax.sharding import PartitionSpec as P

HEAD = 64
SEQ = 197
MESH = pl.DeviceIdType.MESH
BF = jnp.bfloat16
F32 = jnp.float32
NARROW = 4
LIMIT = 62 * 1024 * 1024
eps_norm = 1e-06


def round_up(value, step):
    return -(-value // step) * step


def norm_parts(value):
    mean_value = jnp.mean(value, axis=-1, keepdims=True)
    centred = value - mean_value
    variance = jnp.mean(centred * centred, axis=-1, keepdims=True)
    inverse = lax.rsqrt(variance + eps_norm)
    return centred * inverse, inverse


def dot_nn(a, b):
    return jnp.dot(a, b, preferred_element_type=F32)


def dot_nt(a, b):
    return lax.dot_general(a, b, (((1,), (1,)), ((), ())), preferred_element_type=F32)


def dot_tn(a, b):
    return lax.dot_general(a, b, (((0,), (0,)), ((), ())), preferred_element_type=F32)


def places():
    e, m = lax.axis_index("expert"), lax.axis_index("mp")
    c, y = lax.rem(m, 2), lax.div(m, 2)
    return e, m, c, y, m + 1 - 2 * c, lax.rem(m + 2, NARROW)


def greet(n, e, m, narrow):
    barrier = pltpu.get_barrier_semaphore()

    def wide(i, carry):
        pl.semaphore_signal(
            barrier, inc=1, device_id={"expert": lax.rem(e + i, n), "mp": m}, device_id_type=MESH
        )
        return carry

    lax.fori_loop(1, n, wide, 0)
    for other in narrow:
        pl.semaphore_signal(
            barrier, inc=1, device_id={"expert": e, "mp": other}, device_id_type=MESH
        )
    pl.semaphore_wait(barrier, n - 1 + len(narrow))


def remote(src, dst, send, recv, e, m):
    return pltpu.make_async_remote_copy(
        src_ref=src,
        dst_ref=dst,
        send_sem=send,
        recv_sem=recv,
        device_id={"expert": e, "mp": m},
        device_id_type=MESH,
    )


def gather_kernel(
    n, mat_ref, vec_ref, mats_ref, tot_ref, first_ref, vmp, vsum, vex, ms, mr, ps, pr, vs, vr
):
    e, m, c, y, sib, far = places()
    greet(n, e, m, [lax.rem(m + j, NARROW) for j in range(1, NARROW)])

    def mat_copy(i, source):
        return remote(mat_ref, mats_ref.at[source], ms.at[i], mr.at[i], lax.rem(e + i, n), m)

    def start_mat(i, carry):
        mat_copy(i, e).start()
        return carry

    lax.fori_loop(1, n, start_mat, 0)
    mats_ref[e] = mat_ref[...]
    narrow = [
        remote(vec_ref, vmp.at[m], ps.at[j], pr.at[j], e, lax.rem(m + j, NARROW))
        for j in range(1, NARROW)
    ]
    for copy in narrow:
        copy.start()
    vmp[m] = vec_ref[...]
    for j in range(1, NARROW):
        remote(
            vec_ref, vmp.at[lax.rem(m + NARROW - j, NARROW)], ps.at[j], pr.at[j], e, m
        ).wait_recv()
    vsum[...] = vmp[0, 0:8] + vmp[1, 0:8] + vmp[2, 0:8] + vmp[3, 0:8]
    for j in range(NARROW):
        first_ref[j] = vmp[j, 8:16]

    def vec_copy(i, source):
        return remote(vsum, vex.at[source], vs.at[i], vr.at[i], lax.rem(e + i, n), m)

    def start_vec(i, carry):
        vec_copy(i, e).start()
        return carry

    lax.fori_loop(1, n, start_vec, 0)
    vex[e] = vsum[...]

    def finish_vec(i, carry):
        vec_copy(i, lax.rem(e + n - i, n)).wait_recv()
        return carry

    lax.fori_loop(1, n, finish_vec, 0)
    tot_ref[...] = vex[0]

    def add_vec(i, carry):
        tot_ref[...] += vex[i]
        return carry

    lax.fori_loop(1, n, add_vec, 0)

    def finish(i, carry):
        mat_copy(i, lax.rem(e + n - i, n)).wait_recv()
        mat_copy(i, e).wait_send()
        vec_copy(i, e).wait_send()
        return carry

    lax.fori_loop(1, n, finish, 0)
    for copy in narrow:
        copy.wait_send()


def gather_params(n, mat, vec):
    width = vec.shape[1]
    sem = pltpu.SemaphoreType.DMA
    return pl.pallas_call(
        functools.partial(gather_kernel, n),
        name="gather_params",
        out_shape=(
            jax.ShapeDtypeStruct((n, *mat.shape), BF),
            jax.ShapeDtypeStruct((8, width), F32),
            jax.ShapeDtypeStruct((NARROW, 8, width), F32),
        ),
        in_specs=[pl.BlockSpec(memory_space=pltpu.VMEM)] * 2,
        out_specs=(pl.BlockSpec(memory_space=pltpu.VMEM),) * 3,
        scratch_shapes=[
            pltpu.VMEM((NARROW, *vec.shape), F32),
            pltpu.VMEM((8, width), F32),
            pltpu.VMEM((n, 8, width), F32),
            sem((n,)),
            sem((n,)),
            sem((NARROW,)),
            sem((NARROW,)),
            sem((n,)),
            sem((n,)),
        ],
        compiler_params=pltpu.CompilerParams(
            collective_id=0, has_side_effects=True, vmem_limit_bytes=LIMIT
        ),
    )(mat, vec)


class Summed:
    def __init__(self, rows, part, sa, sb, tot, sems):
        self.rows, self.part, self.sa, self.sb, self.tot, self.sems = rows, part, sa, sb, tot, sems
        self.e, self.m, self.c, self.y, self.sib, self.far = places()

    def at(self, i):
        return pl.ds(pl.multiple_of(i * self.rows, 16), self.rows)

    def copy_a(self, i):
        at = self.at(i)
        return remote(
            self.part.at[1 - self.c, at],
            self.sa.at[at],
            self.sems.at[0, i],
            self.sems.at[1, i],
            self.e,
            self.sib,
        )

    def copy_b(self, i):
        at = self.at(i)
        return remote(
            self.part.at[self.c, at],
            self.sb.at[at],
            self.sems.at[2, i],
            self.sems.at[3, i],
            self.e,
            self.far,
        )

    def copy_c(self, i, half):
        at = self.at(i)
        return remote(
            self.tot.at[half, at],
            self.tot.at[half, at],
            self.sems.at[4, i],
            self.sems.at[5, i],
            self.e,
            self.sib,
        )

    def start_a(self, i):
        self.copy_a(i).start()

    def step_b(self, i):
        self.copy_a(i).wait_recv()
        at = self.at(i)
        self.part[self.c, at] = (
            self.part[self.c, at].astype(F32) + self.sa[at].astype(F32)
        ).astype(BF)
        self.copy_b(i).start()

    def step_c(self, i):
        self.copy_b(i).wait_recv()
        at = self.at(i)
        self.tot[self.c, at] = (self.part[self.c, at].astype(F32) + self.sb[at].astype(F32)).astype(
            BF
        )
        self.copy_c(i, self.c).start()

    def take(self, i):
        self.copy_c(i, 1 - self.c).wait_recv()
        at = self.at(i)
        return jnp.concatenate([self.tot[0, at].astype(F32), self.tot[1, at].astype(F32)], axis=1)

    def drain(self, images):
        def one(i, carry):
            self.copy_a(i).wait_send()
            self.copy_b(i).wait_send()
            self.copy_c(i, self.c).wait_send()
            return carry

        lax.fori_loop(0, images, one, 0)


def head_masks(width, heads, dtype, value=1.0):
    lane = lax.broadcasted_iota(jnp.int32, (1, width), 1)
    return [
        jnp.where((lane >= h * HEAD) & (lane < (h + 1) * HEAD), value, 0.0).astype(dtype)
        for h in range(heads)
    ]


def forward_kernel(
    n,
    images,
    rows,
    capq,
    x_ref,
    g_ref,
    mats_ref,
    rout_ref,
    vec_ref,
    ab_ref,
    keys_ref,
    routes_ref,
    noise_ref,
    q_ref,
    k_ref,
    v_ref,
    p_ref,
    o_ref,
    h_ref,
    a2_ref,
    gates_ref,
    xr_ref,
    gr_ref,
    gt_ref,
    gb,
    oh,
    xs,
    gs,
    gts,
    wt,
    part,
    sa,
    sb,
    tot,
    ar,
    xss,
    xsr,
    gss,
    gsr,
    tss,
    tsr,
):
    e, m, c, y, sib, far = places()
    count, width = x_ref.shape
    half = width // 2
    lanes = keys_ref.shape[1]
    heads = p_ref.shape[0]
    group = min(4, n)
    stride = NARROW * capq
    greet(n, e, m, [sib, far])
    key0, key1 = keys_ref[0:1, :], keys_ref[1:2, :]

    def dispatch(src, send_buf, recv_buf, ssem, rsem, gates):
        def step(g, carry):
            for j in range(group):
                i = g * group + j
                ex = lax.rem(e + i, n)
                want = lax.broadcasted_iota(jnp.int32, (capq, lanes), 0) + (ex * stride + m * capq)
                hit0, hit1 = key0 == want, key1 == want
                oh[j * capq : (j + 1) * capq, :] = jnp.where(hit0 | hit1, 1.0, 0.0).astype(BF)
                if gates is not None:
                    w = jnp.where(hit0, gates[0], 0.0) + jnp.where(hit1, gates[1], 0.0)
                    ws = w[:, 0:128]
                    for t in range(1, lanes // 128):
                        ws = ws + w[:, t * 128 : (t + 1) * 128]
                    wt[0:capq, :] = ws
                    row = jnp.sum(wt[...].T, axis=0, keepdims=True)
                    gts[i] = jnp.broadcast_to(row, (8, 128))
            block = dot_nn(oh[...], src[...]).astype(BF)
            for j in range(group):
                i = g * group + j
                send_buf[i] = block[j * capq : (j + 1) * capq]

                @pl.when(i == 0)
                def _():
                    recv_buf[e] = send_buf[0]
                    if gates is not None:
                        gt_ref[e] = gts[0]

                @pl.when(i > 0)
                def _():
                    ex = lax.rem(e + i, n)
                    remote(send_buf.at[i], recv_buf.at[e], ssem.at[i], rsem.at[i], ex, m).start()
                    if gates is not None:
                        remote(gts.at[i], gt_ref.at[e], tss.at[i], tsr.at[i], ex, m).start()

            return carry

        lax.fori_loop(0, n // group, step, 0)

    gb[0:count, :] = g_ref[...].astype(BF)
    if lanes > count:
        gb[count:lanes, :] = jnp.zeros((lanes - count, width), BF)
        a2_ref[count:lanes, :] = jnp.zeros((lanes - count, width), BF)
    wt[...] = jnp.zeros_like(wt)
    dispatch(gb, gs, gr_ref, gss, gsr, None)

    summed = Summed(rows, part, sa, sb, tot, ar)
    in_q = head_masks(256, heads, BF, HEAD ** (-0.5))
    in_o = head_masks(256, heads, F32)
    key_ok = lax.broadcasted_iota(jnp.int32, (rows, rows), 1) < SEQ
    gain0, gain1 = vec_ref[0:1, :], vec_ref[1:2, :]
    shift0, shift1 = vec_ref[2:3, :], vec_ref[3:4, :]
    out_shift = vec_ref[6:7, :]

    def attend(i):
        at = summed.at(i)
        normed = (norm_parts(x_ref[at, :].astype(F32))[0] * gain0 + shift0).astype(BF)
        q = (dot_nn(normed, mats_ref[:, 0:256]) + ab_ref[0:1, :]).astype(BF)
        k = dot_nn(normed, mats_ref[:, 256:512]).astype(BF)
        v = (dot_nn(normed, mats_ref[:, 512:768]) + ab_ref[1:2, :]).astype(BF)
        q_ref[at, :], k_ref[at, :], v_ref[at, :] = q, k, v
        o = jnp.zeros((rows, 256), F32)
        for h in range(heads):
            s = jnp.where(key_ok, dot_nt(q * in_q[h], k), -1e30)
            top = jnp.max(s, axis=-1, keepdims=True)
            ex = jnp.exp(s - top)
            p = (ex / jnp.sum(ex, axis=-1, keepdims=True)).astype(BF)
            p_ref[h, at, :] = p
            o = o + dot_nn(p, v) * in_o[h]
        o = o.astype(BF)
        o_ref[at, :] = o
        for hh in range(2):
            part[hh, at] = dot_nt(o, mats_ref[hh * half : (hh + 1) * half, 768:1024]).astype(BF)

    def second(i):
        at = summed.at(i)
        hidden = x_ref[at, :].astype(F32) + summed.take(i) + out_shift
        h_ref[0, at], h_ref[1, at] = hidden[:, :half], hidden[:, half:]
        a2_ref[at, :] = (norm_parts(hidden)[0] * gain1 + shift1).astype(BF)

    def tick(t, carry):
        @pl.when(t < images)
        def _():
            attend(t)
            summed.start_a(t)

        @pl.when((t >= 1) & (t <= images))
        def _():
            summed.step_b(t - 1)

        @pl.when((t >= 3) & (t <= images + 2))
        def _():
            summed.step_c(t - 3)

        @pl.when(t >= 4)
        def _():
            second(t - 4)

        return carry

    lax.fori_loop(0, images + 4, tick, 0)

    logits = dot_nt(rout_ref[...], a2_ref[...]) + noise_ref[...]
    who = lax.broadcasted_iota(jnp.int32, logits.shape, 0)
    picked = [
        jnp.sum(jnp.where(who == routes_ref[kk : kk + 1, :], logits, 0.0), axis=0, keepdims=True)
        for kk in range(2)
    ]
    top = jnp.maximum(picked[0], picked[1])
    ex0, ex1 = jnp.exp(picked[0] - top), jnp.exp(picked[1] - top)
    gate0, gate1 = ex0 / (ex0 + ex1), ex1 / (ex0 + ex1)
    gates_ref[...] = jnp.concatenate([gate0, gate1, jnp.zeros((6, lanes), F32)], axis=0)
    dispatch(a2_ref, xs, xr_ref, xss, xsr, (gate0, gate1))

    def finish(i, carry):
        ex, source = lax.rem(e + i, n), lax.rem(e + n - i, n)
        for send_buf, recv_buf, ssem, rsem in (
            (xs, xr_ref, xss, xsr),
            (gs, gr_ref, gss, gsr),
            (gts, gt_ref, tss, tsr),
        ):
            copy = remote(send_buf.at[i], recv_buf.at[source], ssem.at[i], rsem.at[i], ex, m)
            copy.wait_recv()
            copy.wait_send()
        return carry

    lax.fori_loop(1, n, finish, 0)
    summed.drain(images)


def forward(n, images, rows, capq, heads, x, g, mats, rout, vec, ab, keys, routes, noise):
    count, width = x.shape
    lanes = keys.shape[1]
    half = width // 2
    group = min(4, n)
    sem = pltpu.SemaphoreType.DMA
    struct = jax.ShapeDtypeStruct
    outs = (
        struct((count, 256), BF),
        struct((count, 256), BF),
        struct((count, 256), BF),
        struct((heads, count, rows), BF),
        struct((count, 256), BF),
        struct((2, count, half), F32),
        struct((lanes, width), BF),
        struct((8, lanes), F32),
        struct((n, capq, width), BF),
        struct((n, capq, width), BF),
        struct((n, 8, 128), F32),
    )
    return pl.pallas_call(
        functools.partial(forward_kernel, n, images, rows, capq),
        name="forward",
        out_shape=outs,
        in_specs=[pl.BlockSpec(memory_space=pltpu.VMEM)] * 9,
        out_specs=(pl.BlockSpec(memory_space=pltpu.VMEM),) * len(outs),
        scratch_shapes=[
            pltpu.VMEM((lanes, width), BF),
            pltpu.VMEM((group * capq, lanes), BF),
            pltpu.VMEM((n, capq, width), BF),
            pltpu.VMEM((n, capq, width), BF),
            pltpu.VMEM((n, 8, 128), F32),
            pltpu.VMEM((128, 128), F32),
            pltpu.VMEM((2, count, half), BF),
            pltpu.VMEM((count, half), BF),
            pltpu.VMEM((count, half), BF),
            pltpu.VMEM((2, count, half), BF),
            sem((6, images)),
        ]
        + [sem((n,))] * 6,
        compiler_params=pltpu.CompilerParams(
            collective_id=1, has_side_effects=True, vmem_limit_bytes=LIMIT
        ),
    )(x, g, mats, rout, vec, ab, keys, routes, noise)


def expert_kernel(
    x_ref,
    g_ref,
    gate_ref,
    w1_ref,
    w2_ref,
    b1_ref,
    b2_ref,
    dx_ref,
    gy_ref,
    dg_ref,
    dw1_ref,
    dw2_ref,
    db1_ref,
    db2_ref,
    dy,
    xt,
    yacc,
    dxacc,
):
    step = pl.program_id(0) * pl.num_programs(1) + pl.program_id(1)
    last = pl.num_programs(0) * pl.num_programs(1) - 1

    @pl.when(step == 0)
    def _():
        grad = (g_ref[...].astype(F32) * gate_ref[...]).astype(BF)
        dy[...] = grad
        db2_ref[...] = jnp.broadcast_to(
            jnp.sum(grad.astype(F32), axis=0, keepdims=True), db2_ref.shape
        )
        xt[...] = x_ref[...].T
        yacc[...] = jnp.zeros_like(yacc)
        dxacc[...] = jnp.zeros_like(dxacc)

    w1, w2 = w1_ref[0], w2_ref[0]
    z = dot_nn(x_ref[...], w1) + b1_ref[0, 0:1, :]
    cdf = 0.5 * (1.0 + lax.erf(z * (2.0**-0.5)))
    pdf = jnp.exp(-0.5 * z * z) * ((2.0 * jnp.pi) ** -0.5)
    u = (z * cdf).astype(BF)
    yacc[...] += dot_nn(u, w2)
    dz = dot_nt(dy[...], w2) * (cdf + z * pdf)
    db1_ref[0] = jnp.broadcast_to(
        jnp.sum(dz, axis=0, keepdims=True), (db1_ref.shape[1], dz.shape[1])
    )
    dz = dz.astype(BF)
    dxacc[...] += dot_nt(dz, w1)
    dw2_ref[0] = dot_tn(u, dy[...]).astype(BF)
    dw1_ref[0] = dot_nn(xt[...], dz).astype(BF)

    @pl.when(step == last)
    def _():
        yv = yacc[...] + b2_ref[0:1, :]
        gy_ref[...] = (yv * gate_ref[...]).astype(BF)
        dg_ref[...] = jnp.sum(yv * g_ref[...].astype(F32), axis=1, keepdims=True)
        dx_ref[...] = dxacc[...].astype(BF)


def experts(x, g, gate, w1, w2, b1, b2, chunk):
    slots, width = x.shape
    hidden = w1.shape[2]
    struct = jax.ShapeDtypeStruct
    whole = lambda q, j: (0, 0)
    return pl.pallas_call(
        expert_kernel,
        name="experts",
        grid=(NARROW, hidden // chunk),
        out_shape=(
            struct((slots, width), BF),
            struct((slots, width), BF),
            struct((slots, 1), F32),
            struct(w1.shape, BF),
            struct(w2.shape, BF),
            struct(b1.shape, F32),
            struct((8, width), F32),
        ),
        in_specs=[
            pl.BlockSpec((slots, width), whole),
            pl.BlockSpec((slots, width), whole),
            pl.BlockSpec((slots, 1), whole),
            pl.BlockSpec((1, width, chunk), lambda q, j: (q, 0, j)),
            pl.BlockSpec((1, chunk, width), lambda q, j: (q, j, 0)),
            pl.BlockSpec((1, 8, chunk), lambda q, j: (q, 0, j)),
            pl.BlockSpec((1, width), whole),
        ],
        out_specs=(
            pl.BlockSpec((slots, width), whole),
            pl.BlockSpec((slots, width), whole),
            pl.BlockSpec((slots, 1), whole),
            pl.BlockSpec((1, width, chunk), lambda q, j: (q, 0, j)),
            pl.BlockSpec((1, chunk, width), lambda q, j: (q, j, 0)),
            pl.BlockSpec((1, 8, chunk), lambda q, j: (q, 0, j)),
            pl.BlockSpec((8, width), whole),
        ),
        scratch_shapes=[
            pltpu.VMEM((slots, width), BF),
            pltpu.VMEM((width, slots), BF),
            pltpu.VMEM((slots, width), F32),
            pltpu.VMEM((slots, width), F32),
        ],
        compiler_params=pltpu.CompilerParams(vmem_limit_bytes=LIMIT),
    )(x, g, gate, w1, w2, b1, b2)


def backward_kernel(
    n,
    images,
    rows,
    capq,
    lanes_each,
    direct,
    dx_ref,
    gy_ref,
    dg_ref,
    x_ref,
    g_ref,
    h_ref,
    q_ref,
    k_ref,
    v_ref,
    p_ref,
    o_ref,
    a2_ref,
    gates_ref,
    keys_ref,
    routes_ref,
    mats_ref,
    rpad_ref,
    vec_ref,
    db_ref,
    fg_ref,
    po_ref,
    pg_ref,
    small_ref,
    dbo_ref,
    dxr,
    gyr,
    dgr,
    oht,
    dlog,
    part,
    sa,
    sb,
    tot,
    dh,
    part2,
    tot2,
    sa2,
    sb2,
    dq,
    dk,
    dv,
    dr,
    a1,
    acc,
    mine,
    mpv,
    exv,
    pgs,
    pgr,
    ar,
    ar2,
    pss,
    dxs,
    dxv,
    gys,
    gyv,
    dgs,
    dgv,
    pgss,
    pgsr,
    mss,
    msr,
    ess,
    esr,
):
    e, m, c, y, sib, far = places()
    count, width = x_ref.shape
    half = width // 2
    heads = p_ref.shape[0]
    stride = NARROW * capq
    slots = n * lanes_each
    span = lanes_each if lanes_each >= 128 else 128
    per = 128 // lanes_each if lanes_each < 128 else 1
    experts_pad = acc.shape[0] - 8
    here = pl.ds(0, capq)
    if lanes_each > capq:
        for buf in (dxr, gyr):
            buf[:, capq:lanes_each, :] = jnp.zeros((n, lanes_each - capq, width), BF)
    greet(n, e, m, [lax.rem(m + j, NARROW) for j in range(1, NARROW)])

    def dx_copy(i, to, source):
        return remote(dx_ref.at[to], dxr.at[source, here], dxs.at[i], dxv.at[i], to, m)

    def dg_copy(i, to, source):
        return remote(dg_ref.at[to], dgr.at[source], dgs.at[i], dgv.at[i], to, m)

    def gy_copy(i, to, source):
        return remote(gy_ref.at[to], gyr.at[source, here], gys.at[i], gyv.at[i], to, m)

    def start_dx(i, carry):
        to = lax.rem(e + i, n)
        dx_copy(i, to, e).start()
        dg_copy(i, to, e).start()
        return carry

    def start_gy(i, carry):
        gy_copy(i, lax.rem(e + i, n), e).start()
        return carry

    lax.fori_loop(1, n, start_dx, 0)
    lax.fori_loop(1, n, start_gy, 0)
    dxr[e, 0:capq, :] = dx_ref[e]
    gyr[e, 0:capq, :] = gy_ref[e]
    dgr[e] = dg_ref[e]

    gain0, gain1 = vec_ref[0:1, :], vec_ref[1:2, :]
    shift0 = vec_ref[2:3, :]

    lane = lax.broadcasted_iota(jnp.int32, (1, slots), 1)
    place = lane % lanes_each
    want = (lane // lanes_each) * stride + place + m * capq
    want = jnp.where(place < capq, want, -2)

    def fill(i, carry):
        at = pl.ds(pl.multiple_of(i * rows, 16), rows)
        hit = (keys_ref[at, 0:1] == want) | (keys_ref[at, 1:2] == want)
        oht[at, :] = jnp.where(hit, 1.0, 0.0).astype(BF)
        return carry

    lax.fori_loop(0, images, fill, 0)
    acc[...] = jnp.zeros_like(acc)

    def arrive_dx(i, carry):
        source = lax.rem(e + n - i, n)
        dx_copy(i, source, source).wait_recv()
        dg_copy(i, source, source).wait_recv()
        return carry

    lax.fori_loop(1, n, arrive_dx, 0)
    pieces = []
    for block in range(n // per):
        piece = dgr[block * per]
        for j in range(1, per):
            piece = piece + dgr[block * per + j]
        pieces.append(piece[0:1, :])
    dgrow = jnp.concatenate(pieces, axis=1)

    summed = Summed(rows, part, sa, sb, tot, ar)
    again = Summed(rows, part2, sa2, sb2, tot2, ar2)
    rlane = lax.broadcasted_iota(jnp.int32, (1, rpad_ref.shape[0]), 1)

    def returned(i):
        at = summed.at(i)
        dgate = [
            jnp.sum(jnp.where(keys_ref[at, kk : kk + 1] == want, dgrow, 0.0), axis=1, keepdims=True)
            for kk in range(2)
        ]
        gate0, gate1 = gates_ref[at, 0:1], gates_ref[at, 1:2]
        mean = gate0 * dgate[0] + gate1 * dgate[1]
        dl = jnp.where(routes_ref[at, 0:1] == rlane, gate0 * (dgate[0] - mean), 0.0)
        dl = dl + jnp.where(routes_ref[at, 1:2] == rlane, gate1 * (dgate[1] - mean), 0.0)
        dl = dl.astype(BF)
        dlog[at, :] = dl
        for hh in range(2):
            cols = slice(hh * half, (hh + 1) * half)
            rowsum = dot_nn(oht[at, :], dxr[:, :, cols].reshape(slots, half))
            part[hh, at] = (rowsum + dot_nn(dl, rpad_ref[:, cols])).astype(BF)

    in_b = head_masks(256, heads, BF)
    in_f = head_masks(256, heads, F32)
    scale = HEAD ** (-0.5)

    def attend(i):
        at = summed.at(i)
        da2 = summed.take(i)
        hidden = jnp.concatenate([h_ref[0, at], h_ref[1, at]], axis=1)
        normed, inverse = norm_parts(hidden)
        mixed = da2 * normed
        acc[1:2, :] += jnp.sum(mixed, axis=0, keepdims=True)
        acc[3:4, :] += jnp.sum(da2, axis=0, keepdims=True)
        mean_mixed = jnp.mean(mixed * gain1, axis=-1, keepdims=True)
        g2 = da2 * gain1
        mean_grad = jnp.mean(g2, axis=-1, keepdims=True)
        grad = g_ref[at, :] + inverse * (g2 - mean_grad - normed * mean_mixed)
        dh[at, :] = grad
        acc[6:7, :] += jnp.sum(grad, axis=0, keepdims=True)
        low = grad.astype(BF)
        dr[at, :] = low
        do = dot_nn(low, mats_ref[:, 768:1024]).astype(BF)
        q, k, v = q_ref[at, :], k_ref[at, :], v_ref[at, :]
        zero = jnp.zeros((rows, 256), F32)
        dqa, dka, dva = zero, zero, zero
        for h in range(heads):
            p = p_ref[h, at, :]
            dp = dot_nt(do * in_b[h], v)
            pf = p.astype(F32)
            t = pf * dp
            ds = (t - pf * jnp.sum(t, axis=-1, keepdims=True)).astype(BF)
            dqa = dqa + dot_nn(ds, k) * in_f[h]
            dka = dka + dot_tn(ds, q) * in_f[h]
            dva = dva + dot_tn(p, do) * in_f[h]
        dqb, dkb, dvb = (dqa * scale).astype(BF), (dka * scale).astype(BF), dva.astype(BF)
        dq[at, :], dk[at, :], dv[at, :] = dqb, dkb, dvb
        acc[4:5, 0:256] += jnp.sum(dqb.astype(F32), axis=0, keepdims=True)
        acc[5:6, 0:256] += jnp.sum(dvb.astype(F32), axis=0, keepdims=True)
        for hh in range(2):
            r = slice(hh * half, (hh + 1) * half)
            part2[hh, at] = (
                dot_nt(dqb, mats_ref[r, 0:256])
                + dot_nt(dkb, mats_ref[r, 256:512])
                + dot_nt(dvb, mats_ref[r, 512:768])
            ).astype(BF)

    def last(i):
        at = again.at(i)
        da1 = again.take(i)
        normed, inverse = norm_parts(x_ref[at, :].astype(F32))
        a1[at, :] = (normed * gain0 + shift0).astype(BF)
        mixed = da1 * normed
        acc[0:1, :] += jnp.sum(mixed, axis=0, keepdims=True)
        acc[2:3, :] += jnp.sum(da1, axis=0, keepdims=True)
        mean_mixed = jnp.mean(mixed * gain0, axis=-1, keepdims=True)
        g1 = da1 * gain0
        mean_grad = jnp.mean(g1, axis=-1, keepdims=True)
        fg_ref[at, :] = dh[at, :] + inverse * (g1 - mean_grad - normed * mean_mixed)

    def tick(t, carry):
        @pl.when(t < images)
        def _():
            returned(t)
            summed.start_a(t)

        @pl.when((t >= 1) & (t <= images))
        def _():
            summed.step_b(t - 1)

        @pl.when((t >= 3) & (t <= images + 2))
        def _():
            summed.step_c(t - 3)

        @pl.when((t >= 4) & (t <= images + 3))
        def _():
            attend(t - 4)
            again.start_a(t - 4)

        @pl.when((t >= 5) & (t <= images + 4))
        def _():
            again.step_b(t - 5)

        @pl.when((t >= 7) & (t <= images + 6))
        def _():
            again.step_c(t - 7)

        @pl.when(t >= 8)
        def _():
            last(t - 8)

        return carry

    lax.fori_loop(0, images + 8, tick, 0)
    summed.drain(images)
    again.drain(images)

    def arrive_gy(i, carry):
        source = lax.rem(e + n - i, n)
        gy_copy(i, source, source).wait_recv()
        return carry

    lax.fori_loop(1, n, arrive_gy, 0)

    def combine(i, carry):
        at = summed.at(i)
        for hh in range(2):
            cols = slice(hh * half, (hh + 1) * half)
            part[hh, at] = dot_nn(oht[at, :], gyr[:, :, cols].reshape(slots, half)).astype(BF)
        return carry

    lax.fori_loop(0, images, combine, 0)
    both = count // 2
    own = pl.ds(pl.multiple_of(c * both, 16), both)
    other = pl.ds(pl.multiple_of((1 - c) * both, 16), both)
    low_half, high_half = pl.ds(0, both), pl.ds(both, both)
    copy_pa = [
        remote(
            part.at[hh, other], sa.at[pl.ds(hh * both, both)], pss.at[hh], pss.at[2 + hh], e, sib
        )
        for hh in range(2)
    ]
    for copy in copy_pa:
        copy.start()
    for copy in copy_pa:
        copy.wait_recv()
    for hh in range(2):
        sb2[hh * both : (hh + 1) * both] = (
            part[hh, own].astype(F32) + sa[hh * both : (hh + 1) * both].astype(F32)
        ).astype(BF)
    send_to = pl.ds(pl.multiple_of((1 - y) * both, 16), both)
    keep_at = pl.ds(pl.multiple_of(y * both, 16), both)
    copy_pb = remote(sb2.at[send_to], sa2.at[low_half], pss.at[4], pss.at[5], e, far)
    copy_pb.start()

    pgs_full = [
        (a1, dq),
        (a1, dk),
        (a1, dv),
        (dr, o_ref),
    ]
    quarter = heads * HEAD
    for slot, (left, right) in enumerate(pgs_full):
        grad = dot_tn(left[...], right[...])[:, :quarter].astype(BF)
        cols = slice(slot * quarter, (slot + 1) * quarter)
        if direct:
            for i in range(n):
                pgs[i, :, cols] = grad[i * (width // n) : (i + 1) * (width // n)]
        else:
            pg_ref[:, cols] = grad.astype(F32)
    router_grad = dot_tn(dlog[...], a2_ref[0:count, :])
    acc[8 : 8 + experts_pad, :] = router_grad[0:experts_pad]

    if direct:

        def pg_copy(i, to, source):
            return remote(pgs.at[to], pgr.at[source], pgss.at[i], pgsr.at[i], to, m)

        def start_pg(i, carry):
            pg_copy(i, lax.rem(e + i, n), e).start()
            return carry

        lax.fori_loop(1, n, start_pg, 0)
        pgr[e] = pgs[e]

    wide = acc.shape[0]
    lane_w = lax.broadcasted_iota(jnp.int32, (1, width), 1)
    own_cols = (lane_w >= m * quarter) & (lane_w < (m + 1) * quarter)
    mine[0:8, :] = jnp.where(own_cols, acc[0:8, :], 0.0)
    mine[8:wide, :] = acc[8:wide, :]
    mine[wide:, :] = db_ref[...]
    bias = acc[4:6, 0:quarter]
    mine[4:6, :] = jnp.zeros((2, width), F32)
    for mm in range(NARROW):

        @pl.when(m == mm)
        def _():
            mine[4:6, mm * quarter : (mm + 1) * quarter] = bias

    narrow = [
        remote(mine, mpv.at[m], mss.at[j], msr.at[j], e, lax.rem(m + j, NARROW))
        for j in range(1, NARROW)
    ]
    for copy in narrow:
        copy.start()
    mpv[m] = mine[...]
    for j in range(1, NARROW):
        remote(
            mine, mpv.at[lax.rem(m + NARROW - j, NARROW)], mss.at[j], msr.at[j], e, m
        ).wait_recv()
    sums = mpv[0] + mpv[1] + mpv[2] + mpv[3]
    dbo_ref[...] = sums[wide:]
    small_ref[...] = sums[0:wide]
    acc[...] = sums[0:wide]

    top = pl.ds(0, exv.shape[1])

    def ex_copy(i, to, source):
        return remote(acc.at[top], exv.at[source], ess.at[i], esr.at[i], to, m)

    def start_ex(i, carry):
        ex_copy(i, lax.rem(e + i, n), e).start()
        return carry

    lax.fori_loop(1, n, start_ex, 0)

    copy_pb.wait_recv()
    yy = pl.ds(0, both)
    total = sb2[keep_at].astype(F32) + sa2[yy].astype(F32) + h_ref[y, own]
    po_ref[own, :] = total.astype(BF)
    copy_pc = remote(po_ref.at[own], po_ref.at[own], pss.at[6], pss.at[7], e, sib)
    copy_pc.start()
    wait_pc = remote(po_ref.at[other], po_ref.at[other], pss.at[6], pss.at[7], e, sib)

    def finish_ex(i, carry):
        source = lax.rem(e + n - i, n)
        ex_copy(i, source, source).wait_recv()
        small_ref[top, :] += exv[source]
        return carry

    lax.fori_loop(1, n, finish_ex, 0)
    wait_pc.wait_recv()

    if direct:

        def finish_pg(i, carry):
            source = lax.rem(e + n - i, n)
            pg_copy(i, source, source).wait_recv()
            return carry

        lax.fori_loop(1, n, finish_pg, 0)
        total = pgr[0].astype(F32)
        for i in range(1, n):
            total = total + pgr[i].astype(F32)
        pg_ref[...] = total

    def drain(i, carry):
        to = lax.rem(e + i, n)
        dx_copy(i, to, e).wait_send()
        dg_copy(i, to, e).wait_send()
        gy_copy(i, to, e).wait_send()
        ex_copy(i, to, e).wait_send()
        if direct:
            pg_copy(i, to, e).wait_send()
        return carry

    lax.fori_loop(1, n, drain, 0)
    for copy in copy_pa + [copy_pb, copy_pc] + narrow:
        copy.wait_send()


def backward(n, images, rows, capq, lanes_each, direct, extra, *args):
    dx, x, p = args[0], args[3], args[9]
    count, width = x.shape
    half = width // 2
    heads = p.shape[0]
    quarter = heads * HEAD
    slots = n * lanes_each
    each = width // n
    sem = pltpu.SemaphoreType.DMA
    struct = jax.ShapeDtypeStruct
    wide = 8 + extra
    tail = args[-1].shape[0]
    outs = (
        struct((count, width), F32),
        struct((count, half), BF),
        struct((each if direct else width, 4 * quarter), F32),
        struct((wide, width), F32),
        struct((tail, width), F32),
    )
    block = (n, each, 4 * quarter) if direct else (1, 16, 128)
    return pl.pallas_call(
        functools.partial(backward_kernel, n, images, rows, capq, lanes_each, direct),
        name="backward",
        out_shape=outs,
        in_specs=[pl.BlockSpec(memory_space=pltpu.VMEM)] * len(args),
        out_specs=(pl.BlockSpec(memory_space=pltpu.VMEM),) * len(outs),
        scratch_shapes=[
            pltpu.VMEM((n, lanes_each, width), BF),
            pltpu.VMEM((n, lanes_each, width), BF),
            pltpu.VMEM((n, 8, 128), F32),
            pltpu.VMEM((count, slots), BF),
            pltpu.VMEM((count, 128), BF),
            pltpu.VMEM((2, count, half), BF),
            pltpu.VMEM((count, half), BF),
            pltpu.VMEM((count, half), BF),
            pltpu.VMEM((2, count, half), BF),
            pltpu.VMEM((count, width), F32),
            pltpu.VMEM((2, count, half), BF),
            pltpu.VMEM((2, count, half), BF),
            pltpu.VMEM((count, half), BF),
            pltpu.VMEM((count, half), BF),
            pltpu.VMEM((count, 256), BF),
            pltpu.VMEM((count, 256), BF),
            pltpu.VMEM((count, 256), BF),
            pltpu.VMEM((count, width), BF),
            pltpu.VMEM((count, width), BF),
            pltpu.VMEM((wide, width), F32),
            pltpu.VMEM((wide + tail, width), F32),
            pltpu.VMEM((NARROW, wide + tail, width), F32),
            pltpu.VMEM((n, wide if direct else 8, width), F32),
            pltpu.VMEM(block, BF),
            pltpu.VMEM(block, BF),
            sem((6, images)),
            sem((6, images)),
            sem((8,)),
        ]
        + [sem((n,))] * 8
        + [sem((NARROW,))] * 2
        + [sem((n,))] * 2,
        compiler_params=pltpu.CompilerParams(
            collective_id=2, has_side_effects=True, vmem_limit_bytes=LIMIT
        ),
    )(*args)


def on_device(
    features,
    norm_gains,
    norm_shifts,
    attention_bias,
    output_bias,
    project_weight,
    merge_weight,
    router_weight,
    router_noise,
    routes,
    slot_numbers,
    expand_weight,
    expand_bias,
    contract_weight,
    contract_bias,
    cotangent,
):
    count, width = features.shape
    n = lax.axis_size("expert")
    e, m = lax.axis_index("expert"), lax.axis_index("mp")
    capacity = 3 * count // n
    quarter = project_weight.shape[2]
    heads = quarter // HEAD
    images = count // SEQ
    rows = round_up(SEQ, 16)
    padded = images * rows
    lanes = round_up(padded, 128)
    capq = round_up(-(-capacity // NARROW), 16)
    lanes_each = 16
    while lanes_each < capq:
        lanes_each *= 2
    each = width // n
    direct = each % 16 == 0
    owners = router_weight.shape[1]
    extra = round_up(owners, 8)

    low = project_weight.astype(BF)
    gap = jnp.zeros((each, 256 - quarter), BF)
    router_gap = jnp.zeros((each, 256 - quarter - owners), BF)
    mat = jnp.concatenate(
        [
            low[:, 0],
            router_weight.astype(BF),
            router_gap,
            low[:, 1],
            gap,
            low[:, 2],
            gap,
            merge_weight.T.astype(BF),
            gap,
        ],
        axis=1,
    )
    share = norm_gains.shape[1]
    packed = jnp.concatenate(
        [norm_gains, norm_shifts, attention_bias, output_bias[None], jnp.zeros((1, share), F32)]
    )
    vec = jnp.zeros((8, width), F32)
    vec = lax.dynamic_update_slice_in_dim(vec, packed, (e * NARROW + m) * share, 1)
    vec = jnp.concatenate([vec, jnp.broadcast_to(expand_bias, (8, width))])
    mats, vecs, first_bias = gather_params(n, mat, vec)
    mats = mats.reshape(width, 1024)
    router_t = mats[:, quarter : quarter + owners].T
    router_fwd = jnp.pad(router_t, ((0, extra - owners), (0, 0)))
    router_bwd = jnp.pad(router_t, ((0, 128 - owners), (0, 0)))
    ab = lax.dynamic_slice_in_dim(vecs[4:6], m * quarter, quarter, 1)
    ab = jnp.pad(ab, ((0, 6), (0, 256 - quarter)))

    def pad_rows(value, fill=0):
        value = value.reshape(images, SEQ, value.shape[1])
        return jnp.pad(value, ((0, 0), (0, rows - SEQ), (0, 0)), constant_values=fill).reshape(
            padded, -1
        )

    def along_lanes(value, top, fill=0):
        return jnp.pad(
            value.T,
            ((0, top - value.shape[1]), (0, lanes - padded)),
            constant_values=fill,
        )

    x = pad_rows(features)
    g = pad_rows(cotangent)
    keys = pad_rows(routes * (NARROW * capq) + slot_numbers, -1)
    routes_col = pad_rows(routes)
    noise = pad_rows(router_noise)
    w1 = lax.all_gather(expand_weight[0].astype(BF), "mp", axis=0)
    w2 = lax.all_gather(contract_weight[0].astype(BF), "mp", axis=0)
    q, k, v, p, o, h, a2, gates, xr, gr, gt = forward(
        n,
        images,
        rows,
        capq,
        heads,
        x,
        g,
        mats,
        router_fwd,
        vecs,
        ab,
        along_lanes(keys, 8, -1),
        along_lanes(routes_col, 8),
        along_lanes(noise, extra),
    )
    slots = n * capq
    gate_col = gt[:, 0, :capq].reshape(slots, 1)
    dx, gy, dg, dw1, dw2, db1, db2 = experts(
        xr.reshape(slots, width),
        gr.reshape(slots, width),
        gate_col,
        w1,
        w2,
        first_bias,
        contract_bias,
        256,
    )
    expand_grad = lax.psum_scatter(dw1, "mp", scatter_dimension=0)
    contract_grad = lax.psum_scatter(dw2, "mp", scatter_dimension=0)
    dg = jnp.pad(dg.reshape(n, capq), ((0, 0), (0, 128 - capq)))
    dg = jnp.roll(dg, (e * lanes_each) % 128, axis=1)
    dg = jnp.broadcast_to(dg[:, None, :], (n, 8, 128))
    db = jnp.concatenate([db1[:, 0], db2[0:1], jnp.zeros((3, width), F32)])
    fg, po, pg, small, dbo = backward(
        n,
        images,
        rows,
        capq,
        lanes_each,
        direct,
        extra,
        dx.reshape(n, capq, width),
        gy.reshape(n, capq, width),
        dg,
        x,
        g,
        h,
        q,
        k,
        v,
        p,
        o,
        a2,
        gates.T,
        keys,
        routes_col,
        mats,
        router_bwd,
        vecs,
        db,
    )

    def unpad(value):
        return value.reshape(images, rows, -1)[:, :SEQ].reshape(count, -1)

    block_output = lax.dynamic_slice_in_dim(unpad(po), lax.rem(m, 2) * quarter, quarter, 1)
    if not direct:
        pg = lax.psum_scatter(pg, "expert", scatter_dimension=0, tiled=True)
    project_share = pg[:, : 3 * quarter].reshape(each, 3, quarter)
    merge_share = pg[:, 3 * quarter :].T
    mine = lax.dynamic_slice_in_dim(small[0:8], (e * NARROW + m) * share, share, 1)
    router_rows = small[8 : 8 + owners]
    if not direct:
        router_rows = lax.psum(router_rows, "expert")
    router_share = lax.dynamic_slice_in_dim(router_rows, e * each, each, 1).T
    return (
        block_output,
        unpad(fg),
        mine[0:2],
        mine[2:4],
        mine[4:6],
        mine[6],
        project_share,
        merge_share,
        router_share,
        expand_grad[None].astype(F32),
        lax.dynamic_slice_in_dim(dbo, m, 1, 0),
        contract_grad[None].astype(F32),
        dbo[4:5],
    )


def solution(mesh):
    placed = (
        P("expert", None),
        P(None, ("expert", "mp")),
        P(None, ("expert", "mp")),
        P(None, ("expert", "mp")),
        P(("expert", "mp")),
        P("expert", None, "mp"),
        P("mp", "expert"),
        P("expert", None),
        P("expert", None),
        P("expert", None),
        P("expert", None),
        P("expert", None, "mp"),
        P("expert", "mp"),
        P("expert", "mp", None),
        P("expert", None),
        P("expert", None),
    )
    return jax.shard_map(
        on_device,
        mesh=mesh,
        in_specs=placed,
        out_specs=(
            P("expert", "mp"),
            P("expert", None),
            P(None, ("expert", "mp")),
            P(None, ("expert", "mp")),
            P(None, ("expert", "mp")),
            P(("expert", "mp")),
            P("expert", None, "mp"),
            P("mp", "expert"),
            P("expert", None),
            P("expert", None, "mp"),
            P("expert", "mp"),
            P("expert", "mp", None),
            P("expert", None),
        ),
        check_vma=False,
    )
```

```python
import functools

import jax
import jax.numpy as jnp
from jax import lax
from jax.experimental import pallas as pl
from jax.experimental.pallas import tpu as pltpu
from jax.sharding import PartitionSpec as P

HEAD = 64
SEQ = 197
MESH = pl.DeviceIdType.MESH
BF = jnp.bfloat16
F32 = jnp.float32
NARROW = 4
LIMIT = 62 * 1024 * 1024
eps_norm = 1e-06


def round_up(value, step):
    return -(-value // step) * step


def norm_parts(value):
    mean_value = jnp.mean(value, axis=-1, keepdims=True)
    centred = value - mean_value
    variance = jnp.mean(centred * centred, axis=-1, keepdims=True)
    inverse = lax.rsqrt(variance + eps_norm)
    return centred * inverse, inverse


def dot_nn(a, b):
    return jnp.dot(a, b, preferred_element_type=F32)


def dot_nt(a, b):
    return lax.dot_general(a, b, (((1,), (1,)), ((), ())), preferred_element_type=F32)


def dot_tn(a, b):
    return lax.dot_general(a, b, (((0,), (0,)), ((), ())), preferred_element_type=F32)


def places():
    e, m = lax.axis_index("expert"), lax.axis_index("mp")
    c, y = lax.rem(m, 2), lax.div(m, 2)
    return e, m, c, y, m + 1 - 2 * c, lax.rem(m + 2, NARROW)


def greet(n, e, m, narrow):
    barrier = pltpu.get_barrier_semaphore()

    def wide(i, carry):
        pl.semaphore_signal(
            barrier, inc=1, device_id={"expert": lax.rem(e + i, n), "mp": m}, device_id_type=MESH
        )
        return carry

    lax.fori_loop(1, n, wide, 0)
    for other in narrow:
        pl.semaphore_signal(
            barrier, inc=1, device_id={"expert": e, "mp": other}, device_id_type=MESH
        )
    pl.semaphore_wait(barrier, n - 1 + len(narrow))


def remote(src, dst, send, recv, e, m):
    return pltpu.make_async_remote_copy(
        src_ref=src,
        dst_ref=dst,
        send_sem=send,
        recv_sem=recv,
        device_id={"expert": e, "mp": m},
        device_id_type=MESH,
    )


class Summed:
    def __init__(self, rows, part, sa, sb, tot, sems):
        self.rows, self.part, self.sa, self.sb, self.tot, self.sems = rows, part, sa, sb, tot, sems
        self.e, self.m, self.c, self.y, self.sib, self.far = places()

    def at(self, i):
        return pl.ds(pl.multiple_of(i * self.rows, 16), self.rows)

    def copy_a(self, i):
        at = self.at(i)
        return remote(
            self.part.at[1 - self.c, at],
            self.sa.at[at],
            self.sems.at[0, i],
            self.sems.at[1, i],
            self.e,
            self.sib,
        )

    def copy_b(self, i):
        at = self.at(i)
        return remote(
            self.part.at[self.c, at],
            self.sb.at[at],
            self.sems.at[2, i],
            self.sems.at[3, i],
            self.e,
            self.far,
        )

    def copy_c(self, i, half):
        at = self.at(i)
        return remote(
            self.tot.at[half, at],
            self.tot.at[half, at],
            self.sems.at[4, i],
            self.sems.at[5, i],
            self.e,
            self.sib,
        )

    def start_a(self, i):
        self.copy_a(i).start()

    def step_b(self, i):
        self.copy_a(i).wait_recv()
        at = self.at(i)
        self.part[self.c, at] = (
            self.part[self.c, at].astype(F32) + self.sa[at].astype(F32)
        ).astype(BF)
        self.copy_b(i).start()

    def step_c(self, i):
        self.copy_b(i).wait_recv()
        at = self.at(i)
        self.tot[self.c, at] = (self.part[self.c, at].astype(F32) + self.sb[at].astype(F32)).astype(
            BF
        )
        self.copy_c(i, self.c).start()

    def take(self, i):
        self.copy_c(i, 1 - self.c).wait_recv()
        at = self.at(i)
        return jnp.concatenate([self.tot[0, at].astype(F32), self.tot[1, at].astype(F32)], axis=1)

    def drain(self, images):
        def one(i, carry):
            self.copy_a(i).wait_send()
            self.copy_b(i).wait_send()
            self.copy_c(i, self.c).wait_send()
            return carry

        lax.fori_loop(0, images, one, 0)


def head_masks(width, heads, dtype, value=1.0):
    lane = lax.broadcasted_iota(jnp.int32, (1, width), 1)
    return [
        jnp.where((lane >= h * HEAD) & (lane < (h + 1) * HEAD), value, 0.0).astype(dtype)
        for h in range(heads)
    ]


def forward_kernel(
    n,
    images,
    rows,
    capq,
    direct,
    share,
    x_ref,
    g_ref,
    mat_ref,
    small_ref,
    rout_ref,
    first_ref,
    keys_ref,
    noise_ref,
    xp_ref,
    a1_ref,
    q_ref,
    k_ref,
    v_ref,
    p_ref,
    o_ref,
    h_ref,
    a2_ref,
    cols_ref,
    mats_ref,
    rpad_ref,
    vec_ref,
    b1_ref,
    xr_ref,
    gr_ref,
    gt_ref,
    raw,
    packed,
    rpad,
    ab,
    smp,
    sex,
    gb,
    oh,
    xs,
    gs,
    gts,
    wt,
    part,
    sa,
    sb,
    tot,
    ar,
    zrs,
    zls,
    zv,
    nbs,
    nbv,
    pss,
    psv,
    vss,
    vsv,
    xss,
    xsr,
    gss,
    gsr,
    tss,
    tsr,
):
    e, m, c, y, sib, far = places()
    count, width = xp_ref.shape
    half = width // 2
    lanes = keys_ref.shape[1]
    heads = p_ref.shape[0]
    quarter = heads * HEAD
    group = min(4, n)
    stride = NARROW * capq
    each = width // n
    nodes = n // 2
    node, side = lax.div(e, 2), lax.rem(e, 2)
    beside = e + 1 - 2 * side
    greet(n, e, m, [lax.rem(m + j, NARROW) for j in range(1, NARROW)])
    key0, key1 = keys_ref[0:1, :], keys_ref[1:2, :]

    def block_of(where):
        return where * 2 + side

    def right_copy(where):
        at = packed.at[block_of(where)]
        return remote(at, at, zrs.at[where], zv.at[where], jnp.minimum(e + 2, n - 1), m)

    def left_copy(where):
        at = packed.at[block_of(where)]
        return remote(at, at, zls.at[where], zv.at[where], jnp.maximum(e - 2, 0), m)

    def pair_copy(where, which):
        at = packed.at[where * 2 + which]
        return remote(at, at, nbs.at[where], nbv.at[where], beside, m)

    def small_copy(j, source):
        return remote(
            small_ref, smp.at[source], pss.at[j], psv.at[j], e, lax.rem(m + j, NARROW)
        )

    def wide_copy(i, source):
        return remote(
            sex.at[source], sex.at[source], vss.at[i], vsv.at[i], lax.rem(e + i, n), m
        )

    def forward_block(where):
        @pl.when((where <= node) & (node < nodes - 1))
        def _():
            right_copy(where).start()

        @pl.when((where >= node) & (node > 0))
        def _():
            left_copy(where).start()

        pair_copy(where, side).start()

    def forward_from(d):
        for where in (node - d, node + d):

            @pl.when((where >= 0) & (where < nodes))
            def _():
                right_copy(where).wait_recv()
                forward_block(where)

    if direct:
        packed[e] = mat_ref[...]
        forward_block(node)
        for j in range(1, NARROW):
            small_copy(j, m).start()
        smp[m] = small_ref[...]

    def pad_into(to_ref, source, cast):
        for i in range(images):
            to_ref[i * rows : i * rows + SEQ, :] = source[i * SEQ : (i + 1) * SEQ, :].astype(cast)
            to_ref[i * rows + SEQ : (i + 1) * rows, :] = jnp.zeros((rows - SEQ, width), cast)

    def build(g, src, send_buf, gates):
        for j in range(group):
            i = g * group + j
            ex = lax.rem(e + i, n)
            want = lax.broadcasted_iota(jnp.int32, (capq, lanes), 0) + (ex * stride + m * capq)
            hit0, hit1 = key0 == want, key1 == want
            oh[j * capq : (j + 1) * capq, :] = jnp.where(hit0 | hit1, 1.0, 0.0).astype(BF)
            if gates is not None:
                w = jnp.where(hit0, gates[0], 0.0) + jnp.where(hit1, gates[1], 0.0)
                ws = w[:, 0:128]
                for t in range(1, lanes // 128):
                    ws = ws + w[:, t * 128 : (t + 1) * 128]
                wt[0:capq, :] = ws
                row = jnp.sum(wt[...].T, axis=0, keepdims=True)
                gts[i] = jnp.broadcast_to(row, (8, 128))
        block = dot_nn(oh[...], src[...]).astype(BF)
        for j in range(group):
            send_buf[g * group + j] = block[j * capq : (j + 1) * capq]

    def g_copy(i, source):
        return remote(gs.at[i], gr_ref.at[source], gss.at[i], gsr.at[i], lax.rem(e + i, n), m)

    def x_copy(i, source):
        return remote(xs.at[i], xr_ref.at[source], xss.at[i], xsr.at[i], lax.rem(e + i, n), m)

    def t_copy(i, source):
        return remote(gts.at[i], gt_ref.at[source], tss.at[i], tsr.at[i], lax.rem(e + i, n), m)

    pad_into(gb, g_ref, BF)
    if lanes > count:
        gb[count:lanes, :] = jnp.zeros((lanes - count, width), BF)
        a2_ref[count:lanes, :] = jnp.zeros((lanes - count, width), BF)
    wt[...] = jnp.zeros_like(wt)

    if direct:
        for j in range(1, NARROW):
            small_copy(j, lax.rem(m + NARROW - j, NARROW)).wait_recv()
        for j in range(NARROW):
            sex[e, j] = smp[j, 0:8]
            for t in range(width // 128):
                b1_ref[j, :, t * 128 : (t + 1) * 128] = jnp.broadcast_to(
                    smp[j, 8 + t : 9 + t], (8, 128)
                )
        sex[e, NARROW] = small_ref[16:24, :]

        def start_wide(i, carry):
            wide_copy(i, e).start()
            return carry

        lax.fori_loop(1, n, start_wide, 0)

    def build_g(g, carry):
        build(g, gb, gs, None)
        return carry

    lax.fori_loop(0, n // group, build_g, 0)
    gr_ref[e] = gs[0]
    if direct:
        for d in range(1, nodes // 2):
            forward_from(d)

    raw[...] = x_ref[...].astype(F32)
    for i in range(images):
        xp_ref[i * rows : (i + 1) * rows, :] = jnp.concatenate(
            [raw[i * SEQ : (i + 1) * SEQ, :], jnp.zeros((rows - SEQ, width), F32)], axis=0
        ).astype(BF)

    if direct:
        for d in range(max(1, nodes // 2), nodes):
            forward_from(d)

        def finish_wide(i, carry):
            wide_copy(i, lax.rem(e + n - i, n)).wait_recv()
            return carry

        lax.fori_loop(1, n, finish_wide, 0)
        vec_ref[...] = jnp.zeros_like(vec_ref)
        rpad[...] = jnp.zeros_like(rpad)
        for i in range(n):
            for j in range(NARROW):
                at = (i * NARROW + j) * share
                vec_ref[:, at : at + share] = sex[i, j, :, 0:share]
            rpad[0:8, i * each : (i + 1) * each] = sex[i, NARROW, :, 0:each]
        rpad_ref[...] = rpad[...].astype(BF)
        for where in range(nodes):
            pair_copy(where, 1 - side).wait_recv()
        weights = packed[...].reshape(width, 4 * quarter)
    else:
        vec_ref[...] = small_ref[...]
        rpad_ref[...] = rout_ref[...]
        b1_ref[...] = first_ref[...]
        weights = mat_ref[...]
    for j in range(4):
        mats_ref[:, j * 256 : j * 256 + quarter] = weights[:, j * quarter : (j + 1) * quarter]
        mats_ref[:, j * 256 + quarter : (j + 1) * 256] = jnp.zeros((width, 256 - quarter), BF)
    ab[...] = jnp.zeros_like(ab)
    for mm in range(NARROW):

        @pl.when(m == mm)
        def _():
            ab[0:2, 0:quarter] = vec_ref[4:6, mm * quarter : (mm + 1) * quarter]

    def start_g(i, carry):
        g_copy(i, e).start()
        return carry

    lax.fori_loop(1, n, start_g, 0)

    summed = Summed(rows, part, sa, sb, tot, ar)
    in_q = head_masks(256, heads, BF, HEAD ** (-0.5))
    in_o = head_masks(256, heads, F32)
    key_ok = lax.broadcasted_iota(jnp.int32, (rows, rows), 1) < SEQ
    gain0, gain1 = vec_ref[0:1, :], vec_ref[1:2, :]
    shift0, shift1 = vec_ref[2:3, :], vec_ref[3:4, :]
    out_shift = vec_ref[6:7, :]

    def attend(i):
        at = summed.at(i)
        normed = (norm_parts(xp_ref[at, :].astype(F32))[0] * gain0 + shift0).astype(BF)
        a1_ref[at, :] = normed
        q = (dot_nn(normed, mats_ref[:, 0:256]) + ab[0:1, :]).astype(BF)
        k = dot_nn(normed, mats_ref[:, 256:512]).astype(BF)
        v = (dot_nn(normed, mats_ref[:, 512:768]) + ab[1:2, :]).astype(BF)
        q_ref[at, :], k_ref[at, :], v_ref[at, :] = q, k, v
        o = jnp.zeros((rows, 256), F32)
        for h in range(heads):
            s = jnp.where(key_ok, dot_nt(q * in_q[h], k), -1e30)
            top = jnp.max(s, axis=-1, keepdims=True)
            ex = jnp.exp(s - top)
            p = (ex / jnp.sum(ex, axis=-1, keepdims=True)).astype(BF)
            p_ref[h, at, :] = p
            o = o + dot_nn(p, v) * in_o[h]
        o = o.astype(BF)
        o_ref[at, :] = o
        for hh in range(2):
            part[hh, at] = dot_nt(o, mats_ref[hh * half : (hh + 1) * half, 768:1024]).astype(BF)

    def second(i):
        at = summed.at(i)
        hidden = xp_ref[at, :].astype(F32) + summed.take(i) + out_shift
        h_ref[0, at], h_ref[1, at] = hidden[:, :half], hidden[:, half:]
        a2_ref[at, :] = (norm_parts(hidden)[0] * gain1 + shift1).astype(BF)

    def tick(t, carry):
        @pl.when(t < images)
        def _():
            attend(t)
            summed.start_a(t)

        @pl.when((t >= 1) & (t <= images))
        def _():
            summed.step_b(t - 1)

        @pl.when((t >= 3) & (t <= images + 2))
        def _():
            summed.step_c(t - 3)

        @pl.when(t >= 4)
        def _():
            second(t - 4)

        return carry

    lax.fori_loop(0, images + 4, tick, 0)

    tops = noise_ref.shape[0]
    logits = dot_nt(rpad_ref[0:tops, :], a2_ref[...]) + noise_ref[...]
    floor = lax.broadcasted_iota(jnp.int32, logits.shape, 0) * stride
    picked = [
        jnp.sum(
            jnp.where((key >= floor) & (key < floor + stride), logits, 0.0), axis=0, keepdims=True
        )
        for key in (key0, key1)
    ]
    top = jnp.maximum(picked[0], picked[1])
    ex0, ex1 = jnp.exp(picked[0] - top), jnp.exp(picked[1] - top)
    gate0, gate1 = ex0 / (ex0 + ex1), ex1 / (ex0 + ex1)

    def build_x(g, carry):
        build(g, a2_ref, xs, (gate0, gate1))
        for j in range(group):
            i = g * group + j

            @pl.when(i == 0)
            def _():
                xr_ref[e] = xs[0]
                gt_ref[e] = gts[0]

            @pl.when(i > 0)
            def _():
                x_copy(i, e).start()
                t_copy(i, e).start()

        return carry

    lax.fori_loop(0, n // group, build_x, 0)
    cols_ref[...] = jnp.concatenate(
        [key0.astype(F32), key1.astype(F32), gate0, gate1, jnp.zeros((124, lanes), F32)], axis=0
    ).T

    def finish(i, carry):
        source = lax.rem(e + n - i, n)
        for copy in (g_copy, x_copy, t_copy):
            copy(i, source).wait_recv()
            copy(i, source).wait_send()
        if direct:
            wide_copy(i, e).wait_send()
        return carry

    lax.fori_loop(1, n, finish, 0)
    summed.drain(images)
    if direct:
        for j in range(1, NARROW):
            small_copy(j, m).wait_send()
        for where in range(nodes):
            pair_copy(where, side).wait_send()

            @pl.when((where <= node) & (node < nodes - 1))
            def _():
                right_copy(where).wait_send()

            @pl.when((where >= node) & (node > 0))
            def _():
                left_copy(where).wait_send()


def forward(n, images, rows, capq, heads, direct, share, x, g, mat, small, rout, first, keys, noise):
    width = x.shape[1]
    count, lanes = images * rows, keys.shape[1]
    half = width // 2
    group = min(4, n)
    sem = pltpu.SemaphoreType.DMA
    struct = jax.ShapeDtypeStruct
    outs = (
        struct((count, width), BF),
        struct((count, width), BF),
        struct((count, 256), BF),
        struct((count, 256), BF),
        struct((count, 256), BF),
        struct((heads, count, rows), BF),
        struct((count, 256), BF),
        struct((2, count, half), F32),
        struct((lanes, width), BF),
        struct((lanes, 128), F32),
        struct((width, 1024), BF),
        struct((128, width), BF),
        struct((8, width), F32),
        struct((NARROW, 8, width), F32),
        struct((n, capq, width), BF),
        struct((n, capq, width), BF),
        struct((n, 8, 128), F32),
    )
    args = (x, g, mat, small, rout, first, keys, noise)
    return pl.pallas_call(
        functools.partial(forward_kernel, n, images, rows, capq, direct, share),
        name="forward",
        out_shape=outs,
        in_specs=[pl.BlockSpec(memory_space=pltpu.VMEM)] * len(args),
        out_specs=(pl.BlockSpec(memory_space=pltpu.VMEM),) * len(outs),
        scratch_shapes=[
            pltpu.VMEM(x.shape, F32),
            pltpu.VMEM((n, *mat.shape) if direct else (1, 16, 128), BF),
            pltpu.VMEM((128, width), F32),
            pltpu.VMEM((8, 256), F32),
            pltpu.VMEM((NARROW, 24, 128), F32),
            pltpu.VMEM((n, NARROW + 1, 8, 128), F32),
            pltpu.VMEM((lanes, width), BF),
            pltpu.VMEM((group * capq, lanes), BF),
            pltpu.VMEM((n, capq, width), BF),
            pltpu.VMEM((n, capq, width), BF),
            pltpu.VMEM((n, 8, 128), F32),
            pltpu.VMEM((128, 128), F32),
            pltpu.VMEM((2, count, half), BF),
            pltpu.VMEM((count, half), BF),
            pltpu.VMEM((count, half), BF),
            pltpu.VMEM((2, count, half), BF),
            sem((6, images)),
        ]
        + [sem((n // 2,))] * 5
        + [sem((NARROW,))] * 2
        + [sem((n,))] * 8,
        compiler_params=pltpu.CompilerParams(
            collective_id=1, has_side_effects=True, vmem_limit_bytes=LIMIT
        ),
    )(*args)


def expert_kernel(
    n,
    capq,
    lanes_each,
    chunk,
    x_ref,
    g_ref,
    gt_ref,
    w1_ref,
    w2_ref,
    b1_ref,
    b2_ref,
    dxr_ref,
    dgr_ref,
    gy_ref,
    d1_ref,
    d2_ref,
    db_ref,
    gcol,
    dy,
    xt,
    yacc,
    dxacc,
    dxs,
    dgs,
    wt,
    s1,
    s2,
    r1,
    r2,
    ws,
    wv,
    dxss,
    dxsv,
    dgss,
    dgsv,
):
    e, m, c, y, sib, far = places()
    slots, width = x_ref.shape
    hidden = w1_ref.shape[2]
    greet(n, e, m, [sib, far])

    def gate_col(i, carry):
        row = jnp.broadcast_to(gt_ref[i, 0:1, :], (128, 128))
        gcol[pl.ds(pl.multiple_of(i * capq, 16), capq), :] = row.T[0:capq]
        return carry

    lax.fori_loop(0, n, gate_col, 0)
    gate = gcol[:, 0:1]
    grad = (g_ref[...].astype(F32) * gate).astype(BF)
    dy[...] = grad
    db_ref[NARROW] = jnp.broadcast_to(jnp.sum(grad.astype(F32), axis=0, keepdims=True), (8, width))
    xt[...] = x_ref[...].T
    yacc[...] = jnp.zeros_like(yacc)
    dxacc[...] = jnp.zeros_like(dxacc)
    if lanes_each > capq:
        dxr_ref[:, capq:lanes_each, :] = jnp.zeros((n, lanes_each - capq, width), BF)

    def w_copies(t, to):
        return [
            remote(s1.at[t], r1.at[t], ws.at[0, t], wv.at[0, t], e, to),
            remote(s2.at[t], r2.at[t], ws.at[1, t], wv.at[1, t], e, to),
        ]

    route = [(3 - m, sib), (far, far), (sib, sib), (m, None)]
    for t, (q, to) in enumerate(route):

        def step(j, carry):
            at = pl.ds(pl.multiple_of(j * chunk, chunk), chunk)
            w1, w2 = w1_ref[q, :, at], w2_ref[q, at, :]
            z = dot_nn(x_ref[...], w1) + b1_ref[q, 0:1, at]
            cdf = 0.5 * (1.0 + lax.erf(z * (2.0**-0.5)))
            pdf = jnp.exp(-0.5 * z * z) * ((2.0 * jnp.pi) ** -0.5)
            u = (z * cdf).astype(BF)
            yacc[...] += dot_nn(u, w2)
            dz = dot_nt(dy[...], w2) * (cdf + z * pdf)
            db_ref[q, :, at] = jnp.broadcast_to(jnp.sum(dz, axis=0, keepdims=True), (8, chunk))
            dz = dz.astype(BF)
            dxacc[...] += dot_nt(dz, w1)
            dw2 = dot_tn(u, dy[...])
            dw1 = dot_nn(xt[...], dz)
            if to is None:
                d2_ref[at, :] = dw2
                d1_ref[:, at] = dw1
            else:
                s2[t, at, :] = dw2.astype(BF)
                s1[t, :, at] = dw1.astype(BF)
            return carry

        lax.fori_loop(0, hidden // chunk, step, 0)
        if t == 1:
            for copy in w_copies(0, sib):
                copy.wait_recv()
            s1[1] = (s1[1].astype(F32) + r1[0].astype(F32)).astype(BF)
            s2[1] = (s2[1].astype(F32) + r2[0].astype(F32)).astype(BF)
        if to is not None:
            for copy in w_copies(t, to):
                copy.start()

    def dx_copy(i, to, source):
        return remote(
            dxs.at[to], dxr_ref.at[source, pl.ds(0, capq)], dxss.at[i], dxsv.at[i], to, m
        )

    def dg_copy(i, to, source):
        return remote(dgs.at[to], dgr_ref.at[source], dgss.at[i], dgsv.at[i], to, m)

    def start_dx(i, carry):
        to = lax.rem(e + i, n)
        at = pl.ds(pl.multiple_of(to * capq, 16), capq)
        dxs[to] = dxacc[at, :].astype(BF)
        dx_copy(i, to, e).start()
        return carry

    lax.fori_loop(1, n, start_dx, 0)
    own = pl.ds(pl.multiple_of(e * capq, 16), capq)
    dxr_ref[e, 0:capq, :] = dxacc[own, :].astype(BF)
    yv = yacc[...] + b2_ref[0:1, :]
    gy_ref[...] = (yv * gate).astype(BF)
    gcol[...] = jnp.broadcast_to(
        jnp.sum(yv * g_ref[...].astype(F32), axis=1, keepdims=True), gcol.shape
    )
    wt[...] = jnp.zeros_like(wt)
    dgs[...] = jnp.zeros_like(dgs)
    per = max(1, 128 // lanes_each)

    def gate_row(i, carry):
        wt[0:capq, :] = gcol[pl.ds(pl.multiple_of(i * capq, 16), capq), :]
        row = wt[...].T[0:8, :]
        for k in range(per):

            @pl.when(lax.rem(e, per) == k)
            def _():
                dgs[i, :, k * lanes_each : (k + 1) * lanes_each] = row[:, 0:lanes_each]

        return carry

    lax.fori_loop(0, n, gate_row, 0)

    def start_dg(i, carry):
        dg_copy(i, lax.rem(e + i, n), e).start()
        return carry

    lax.fori_loop(1, n, start_dg, 0)
    dgr_ref[e] = dgs[e]

    for copy in w_copies(2, sib):
        copy.wait_recv()
    d1_ref[...] += r1[2].astype(F32)
    d2_ref[...] += r2[2].astype(F32)
    for copy in w_copies(1, far):
        copy.wait_recv()
    d1_ref[...] += r1[1].astype(F32)
    d2_ref[...] += r2[1].astype(F32)

    def finish(i, carry):
        source = lax.rem(e + n - i, n)
        dx_copy(i, source, source).wait_recv()
        dg_copy(i, source, source).wait_recv()
        dx_copy(i, lax.rem(e + i, n), e).wait_send()
        dg_copy(i, lax.rem(e + i, n), e).wait_send()
        return carry

    lax.fori_loop(1, n, finish, 0)
    for t, to in ((0, sib), (1, far), (2, sib)):
        for copy in w_copies(t, to):
            copy.wait_send()


def experts(n, capq, lanes_each, x, g, gt, w1, w2, b1, b2, chunk):
    slots, width = x.shape
    hidden = w1.shape[2]
    struct = jax.ShapeDtypeStruct
    sem = pltpu.SemaphoreType.DMA
    outs = (
        struct((n, lanes_each, width), BF),
        struct((n, 8, 128), F32),
        struct((slots, width), BF),
        struct(w1.shape[1:], F32),
        struct(w2.shape[1:], F32),
        struct((NARROW + 1, 8, width), F32),
    )
    args = (x, g, gt, w1, w2, b1, b2)
    return pl.pallas_call(
        functools.partial(expert_kernel, n, capq, lanes_each, chunk),
        name="experts",
        out_shape=outs,
        in_specs=[pl.BlockSpec(memory_space=pltpu.VMEM)] * len(args),
        out_specs=(pl.BlockSpec(memory_space=pltpu.VMEM),) * len(outs),
        scratch_shapes=[
            pltpu.VMEM((slots, 128), F32),
            pltpu.VMEM((slots, width), BF),
            pltpu.VMEM((width, slots), BF),
            pltpu.VMEM((slots, width), F32),
            pltpu.VMEM((slots, width), F32),
            pltpu.VMEM((n, capq, width), BF),
            pltpu.VMEM((n, 8, 128), F32),
            pltpu.VMEM((128, 128), F32),
            pltpu.VMEM((3, width, hidden), BF),
            pltpu.VMEM((3, hidden, width), BF),
            pltpu.VMEM((3, width, hidden), BF),
            pltpu.VMEM((3, hidden, width), BF),
            sem((2, 3)),
            sem((2, 3)),
        ]
        + [sem((n,))] * 4,
        compiler_params=pltpu.CompilerParams(
            collective_id=3, has_side_effects=True, vmem_limit_bytes=LIMIT
        ),
    )(*args)


def backward_kernel(
    n,
    images,
    rows,
    capq,
    lanes_each,
    direct,
    share,
    owners,
    dxr_ref,
    dgr_ref,
    gy_ref,
    x_ref,
    g_ref,
    h_ref,
    a1_ref,
    q_ref,
    k_ref,
    v_ref,
    p_ref,
    o_ref,
    a2_ref,
    cols_ref,
    mats_ref,
    rpad_ref,
    vec_ref,
    db_ref,
    fg_ref,
    po_ref,
    pg_ref,
    small_ref,
    router_ref,
    dbo_ref,
    gyr,
    oht,
    dlog,
    part,
    sa,
    sb,
    tot,
    dh,
    part2,
    tot2,
    sa2,
    sb2,
    dq,
    dk,
    dv,
    dr,
    acc,
    mine,
    mpv,
    exv,
    pgs,
    pgr,
    ar,
    ar2,
    pss,
    gys,
    gyv,
    pgss,
    pgsr,
    mss,
    msr,
    ess,
    esr,
):
    e, m, c, y, sib, far = places()
    count, width = x_ref.shape
    half = width // 2
    heads = p_ref.shape[0]
    quarter = heads * HEAD
    each = width // n
    stride = NARROW * capq
    slots = n * lanes_each
    per = max(1, 128 // lanes_each)
    wide = acc.shape[0]
    here = pl.ds(0, capq)
    if lanes_each > capq:
        gyr[:, capq:lanes_each, :] = jnp.zeros((n, lanes_each - capq, width), BF)
    greet(n, e, m, [lax.rem(m + j, NARROW) for j in range(1, NARROW)])

    def gy_copy(i, to, source):
        return remote(gy_ref.at[to], gyr.at[source, here], gys.at[i], gyv.at[i], to, m)

    def start_gy(i, carry):
        gy_copy(i, lax.rem(e + i, n), e).start()
        return carry

    lax.fori_loop(1, n, start_gy, 0)
    gyr[e, 0:capq, :] = gy_ref[e]

    gain0, gain1 = vec_ref[0:1, :], vec_ref[1:2, :]

    lane = lax.broadcasted_iota(jnp.int32, (1, slots), 1)
    place = lane % lanes_each
    want = (lane // lanes_each) * stride + place + m * capq
    want = jnp.where(place < capq, want, -2).astype(F32)
    pieces = []
    for block in range(n // per):
        piece = dgr_ref[block * per]
        for j in range(1, per):
            piece = piece + dgr_ref[block * per + j]
        pieces.append(piece[0:1, :])
    dgrow = jnp.concatenate(pieces, axis=1)
    acc[...] = jnp.zeros_like(acc)
    dh[...] = jnp.zeros_like(dh)
    for i in range(images):
        dh[i * rows : i * rows + SEQ, :] = g_ref[i * SEQ : (i + 1) * SEQ, :]

    summed = Summed(rows, part, sa, sb, tot, ar)
    again = Summed(rows, part2, sa2, sb2, tot2, ar2)
    rfloor = lax.broadcasted_iota(jnp.int32, (1, 128), 1).astype(F32) * stride

    def returned(i):
        at = summed.at(i)
        key = [cols_ref[at, 0:1], cols_ref[at, 1:2]]
        gate = [cols_ref[at, 2:3], cols_ref[at, 3:4]]
        hits = [key[0] == want, key[1] == want]
        oht[at, :] = jnp.where(hits[0] | hits[1], 1.0, 0.0).astype(BF)
        dgate = [jnp.sum(jnp.where(hit, dgrow, 0.0), axis=1, keepdims=True) for hit in hits]
        mean = gate[0] * dgate[0] + gate[1] * dgate[1]
        dl = [
            jnp.where(
                (key[kk] >= rfloor) & (key[kk] < rfloor + stride), gate[kk] * (dgate[kk] - mean), 0.0
            )
            for kk in range(2)
        ]
        dl = (dl[0] + dl[1]).astype(BF)
        dlog[at, :] = dl
        for hh in range(2):
            cut = slice(hh * half, (hh + 1) * half)
            rowsum = dot_nn(oht[at, :], dxr_ref[:, :, cut].reshape(slots, half))
            part[hh, at] = (rowsum + dot_nn(dl, rpad_ref[:, cut])).astype(BF)

    in_b = head_masks(256, heads, BF)
    in_f = head_masks(256, heads, F32)
    scale = HEAD ** (-0.5)

    def attend(i):
        at = summed.at(i)
        da2 = summed.take(i)
        hidden = jnp.concatenate([h_ref[0, at], h_ref[1, at]], axis=1)
        normed, inverse = norm_parts(hidden)
        mixed = da2 * normed
        acc[1:2, :] += jnp.sum(mixed, axis=0, keepdims=True)
        acc[3:4, :] += jnp.sum(da2, axis=0, keepdims=True)
        mean_mixed = jnp.mean(mixed * gain1, axis=-1, keepdims=True)
        g2 = da2 * gain1
        mean_grad = jnp.mean(g2, axis=-1, keepdims=True)
        grad = dh[at, :] + inverse * (g2 - mean_grad - normed * mean_mixed)
        dh[at, :] = grad
        acc[6:7, :] += jnp.sum(grad, axis=0, keepdims=True)
        low = grad.astype(BF)
        dr[at, :] = low
        do = dot_nn(low, mats_ref[:, 768:1024]).astype(BF)
        q, k, v = q_ref[at, :], k_ref[at, :], v_ref[at, :]
        zero = jnp.zeros((rows, 256), F32)
        dqa, dka, dva = zero, zero, zero
        for h in range(heads):
            p = p_ref[h, at, :]
            dp = dot_nt(do * in_b[h], v)
            pf = p.astype(F32)
            t = pf * dp
            ds = (t - pf * jnp.sum(t, axis=-1, keepdims=True)).astype(BF)
            dqa = dqa + dot_nn(ds, k) * in_f[h]
            dka = dka + dot_tn(ds, q) * in_f[h]
            dva = dva + dot_tn(p, do) * in_f[h]
        dqb, dkb, dvb = (dqa * scale).astype(BF), (dka * scale).astype(BF), dva.astype(BF)
        dq[at, :], dk[at, :], dv[at, :] = dqb, dkb, dvb
        acc[4:5, 0:256] += jnp.sum(dqb.astype(F32), axis=0, keepdims=True)
        acc[5:6, 0:256] += jnp.sum(dvb.astype(F32), axis=0, keepdims=True)
        for hh in range(2):
            r = slice(hh * half, (hh + 1) * half)
            part2[hh, at] = (
                dot_nt(dqb, mats_ref[r, 0:256])
                + dot_nt(dkb, mats_ref[r, 256:512])
                + dot_nt(dvb, mats_ref[r, 512:768])
            ).astype(BF)

    def last(i):
        at = again.at(i)
        da1 = again.take(i)
        normed, inverse = norm_parts(x_ref[at, :].astype(F32))
        mixed = da1 * normed
        acc[0:1, :] += jnp.sum(mixed, axis=0, keepdims=True)
        acc[2:3, :] += jnp.sum(da1, axis=0, keepdims=True)
        mean_mixed = jnp.mean(mixed * gain0, axis=-1, keepdims=True)
        g1 = da1 * gain0
        mean_grad = jnp.mean(g1, axis=-1, keepdims=True)
        dh[at, :] += inverse * (g1 - mean_grad - normed * mean_mixed)

    def tick(t, carry):
        @pl.when(t < images)
        def _():
            returned(t)
            summed.start_a(t)

        @pl.when((t >= 1) & (t <= images))
        def _():
            summed.step_b(t - 1)

        @pl.when((t >= 3) & (t <= images + 2))
        def _():
            summed.step_c(t - 3)

        @pl.when((t >= 4) & (t <= images + 3))
        def _():
            attend(t - 4)
            again.start_a(t - 4)

        @pl.when((t >= 5) & (t <= images + 4))
        def _():
            again.step_b(t - 5)

        @pl.when((t >= 7) & (t <= images + 6))
        def _():
            again.step_c(t - 7)

        @pl.when(t >= 8)
        def _():
            last(t - 8)

        return carry

    lax.fori_loop(0, images + 5, tick, 0)

    def pg_copy(b, i, to, source):
        return remote(
            pgs.at[b, to], pgr.at[b, source], pgss.at[b, i], pgsr.at[b, i], to, m
        )

    pairs = [(dr, o_ref), (a1_ref, dq), (a1_ref, dk), (a1_ref, dv)]
    for b in range(2):
        for s in range(2):
            left, right = pairs[2 * b + s]
            grad = dot_tn(left[...], right[...])[:, :quarter]
            if direct:
                grad = grad.astype(BF)
                for i in range(n):
                    pgs[b, i, :, s * quarter : (s + 1) * quarter] = grad[i * each : (i + 1) * each]
            else:
                slot = 2 * b + s
                pg_ref[:, slot * quarter : (slot + 1) * quarter] = grad
        if direct:

            def start_pg(i, carry):
                pg_copy(b, i, lax.rem(e + i, n), e).start()
                return carry

            lax.fori_loop(1, n, start_pg, 0)
            pgr[b, e] = pgs[b, e]

    lax.fori_loop(images + 5, images + 8, tick, 0)
    summed.drain(images)
    again.drain(images)
    for i in range(images):
        fg_ref[i * SEQ : (i + 1) * SEQ, :] = dh[i * rows : i * rows + SEQ, :]

    acc[8:wide, :] = dot_tn(dlog[...], a2_ref[0:count, :])[0 : wide - 8]
    lane_w = lax.broadcasted_iota(jnp.int32, (1, width), 1)
    own_cols = (lane_w >= m * quarter) & (lane_w < (m + 1) * quarter)
    mine[0:8, :] = jnp.where(own_cols, acc[0:8, :], 0.0)
    mine[8:wide, :] = acc[8:wide, :]
    bias = acc[4:6, 0:quarter]
    mine[4:6, :] = jnp.zeros((2, width), F32)
    for mm in range(NARROW):

        @pl.when(m == mm)
        def _():
            mine[4:6, mm * quarter : (mm + 1) * quarter] = bias

    for j in range(NARROW + 1):
        mine[wide + j : wide + j + 1, :] = db_ref[j, 0:1, :]
    mine[wide + NARROW + 1 :, :] = jnp.zeros((8 - NARROW - 1, width), F32)

    def narrow(j, source):
        return remote(mine, mpv.at[source], mss.at[j], msr.at[j], e, lax.rem(m + j, NARROW))

    for j in range(1, NARROW):
        narrow(j, m).start()
    mpv[m] = mine[...]

    def arrive_gy(i, carry):
        source = lax.rem(e + n - i, n)
        gy_copy(i, source, source).wait_recv()
        return carry

    lax.fori_loop(1, n, arrive_gy, 0)

    def combine(i, carry):
        at = summed.at(i)
        for hh in range(2):
            cut = slice(hh * half, (hh + 1) * half)
            part[hh, at] = dot_nn(oht[at, :], gyr[:, :, cut].reshape(slots, half)).astype(BF)
        return carry

    lax.fori_loop(0, images, combine, 0)
    both = count // 2
    own = pl.ds(pl.multiple_of(c * both, 16), both)
    other = pl.ds(pl.multiple_of((1 - c) * both, 16), both)
    low_half = pl.ds(0, both)
    copy_pa = [
        remote(
            part.at[hh, other], sa.at[pl.ds(hh * both, both)], pss.at[hh], pss.at[2 + hh], e, sib
        )
        for hh in range(2)
    ]
    for copy in copy_pa:
        copy.start()

    for j in range(1, NARROW):
        narrow(j, lax.rem(m + NARROW - j, NARROW)).wait_recv()
    sums = mpv[0] + mpv[1] + mpv[2] + mpv[3]
    for mm in range(NARROW):

        @pl.when(m == mm)
        def _():
            dbo_ref[0:1, :] = sums[wide + mm : wide + mm + 1]

    dbo_ref[1:2, :] = sums[wide + NARROW : wide + NARROW + 1]
    acc[...] = sums[0:wide]
    top = pl.ds(0, exv.shape[1])

    def ex_copy(i, to, source):
        return remote(acc.at[top], exv.at[source], ess.at[i], esr.at[i], to, m)

    def start_ex(i, carry):
        ex_copy(i, lax.rem(e + i, n), e).start()
        return carry

    lax.fori_loop(1, n, start_ex, 0)
    exv[e] = acc[top, :]

    for copy in copy_pa:
        copy.wait_recv()
    for hh in range(2):
        sb2[hh * both : (hh + 1) * both] = (
            part[hh, own].astype(F32) + sa[hh * both : (hh + 1) * both].astype(F32)
        ).astype(BF)
    send_to = pl.ds(pl.multiple_of((1 - y) * both, 16), both)
    keep_at = pl.ds(pl.multiple_of(y * both, 16), both)
    copy_pb = remote(sb2.at[send_to], sa2.at[low_half], pss.at[4], pss.at[5], e, far)
    copy_pb.start()

    def finish_ex(i, carry):
        source = lax.rem(e + n - i, n)
        ex_copy(i, source, source).wait_recv()
        return carry

    lax.fori_loop(1, n, finish_ex, 0)
    total = exv[0]
    for i in range(1, n):
        total = total + exv[i]
    pick = lax.broadcasted_iota(jnp.int32, (width, 128), 0) - lax.broadcasted_iota(
        jnp.int32, (width, 128), 1
    )

    def picked(values, offset):
        return jnp.dot(
            values,
            jnp.where(pick == offset, 1.0, 0.0),
            precision=lax.Precision.HIGHEST,
            preferred_element_type=F32,
        )

    small_ref[...] = picked(total[0:8], (e * NARROW + m) * share)[:, 0:share]
    if direct:
        mixed = picked(total[8:wide], e * each)
        router_ref[...] = jnp.concatenate(
            [mixed, jnp.zeros((128 - mixed.shape[0], 128), F32)], axis=0
        ).T[0:each, 0:owners]
    else:
        router_ref[...] = acc[8:wide, :]

    copy_pb.wait_recv()
    total = sb2[keep_at].astype(F32) + sa2[low_half].astype(F32) + h_ref[y, own]
    po_ref[own, :] = total.astype(BF)
    copy_pc = remote(po_ref.at[own], po_ref.at[own], pss.at[6], pss.at[7], e, sib)
    copy_pc.start()
    wait_pc = remote(po_ref.at[other], po_ref.at[other], pss.at[6], pss.at[7], e, sib)

    if direct:
        for b in range(2):

            def finish_pg(i, carry):
                source = lax.rem(e + n - i, n)
                pg_copy(b, i, source, source).wait_recv()
                return carry

            lax.fori_loop(1, n, finish_pg, 0)
            total = pgr[b, 0].astype(F32)
            for i in range(1, n):
                total = total + pgr[b, i].astype(F32)
            pg_ref[:, b * 2 * quarter : (b + 1) * 2 * quarter] = total
    wait_pc.wait_recv()

    def drain(i, carry):
        to = lax.rem(e + i, n)
        gy_copy(i, to, e).wait_send()
        ex_copy(i, to, e).wait_send()
        if direct:
            pg_copy(0, i, to, e).wait_send()
            pg_copy(1, i, to, e).wait_send()
        return carry

    lax.fori_loop(1, n, drain, 0)
    for copy in copy_pa + [copy_pb, copy_pc] + [narrow(j, m) for j in range(1, NARROW)]:
        copy.wait_send()


def backward(n, images, rows, capq, lanes_each, direct, share, owners, *args):
    g, x, p = args[4], args[3], args[10]
    count, width = x.shape
    half = width // 2
    heads = p.shape[0]
    quarter = heads * HEAD
    slots = n * lanes_each
    each = width // n
    sem = pltpu.SemaphoreType.DMA
    struct = jax.ShapeDtypeStruct
    extra = round_up(owners, 8)
    wide = 8 + extra
    outs = (
        struct(g.shape, F32),
        struct((count, half), BF),
        struct((each if direct else width, 4 * quarter), F32),
        struct((8, share), F32),
        struct((each, owners) if direct else (extra, width), F32),
        struct((2, width), F32),
    )
    block = (2, n, each, 2 * quarter) if direct else (1, 1, 16, 128)
    return pl.pallas_call(
        functools.partial(
            backward_kernel, n, images, rows, capq, lanes_each, direct, share, owners
        ),
        name="backward",
        out_shape=outs,
        in_specs=[pl.BlockSpec(memory_space=pltpu.VMEM)] * len(args),
        out_specs=(pl.BlockSpec(memory_space=pltpu.VMEM),) * len(outs),
        scratch_shapes=[
            pltpu.VMEM((n, lanes_each, width), BF),
            pltpu.VMEM((count, slots), BF),
            pltpu.VMEM((count, 128), BF),
            pltpu.VMEM((2, count, half), BF),
            pltpu.VMEM((count, half), BF),
            pltpu.VMEM((count, half), BF),
            pltpu.VMEM((2, count, half), BF),
            pltpu.VMEM((count, width), F32),
            pltpu.VMEM((2, count, half), BF),
            pltpu.VMEM((2, count, half), BF),
            pltpu.VMEM((count, half), BF),
            pltpu.VMEM((count, half), BF),
            pltpu.VMEM((count, 256), BF),
            pltpu.VMEM((count, 256), BF),
            pltpu.VMEM((count, 256), BF),
            pltpu.VMEM((count, width), BF),
            pltpu.VMEM((wide, width), F32),
            pltpu.VMEM((wide + 8, width), F32),
            pltpu.VMEM((NARROW, wide + 8, width), F32),
            pltpu.VMEM((n, wide if direct else 8, width), F32),
            pltpu.VMEM(block, BF),
            pltpu.VMEM(block, BF),
            sem((6, images)),
            sem((6, images)),
            sem((8,)),
        ]
        + [sem((n,))] * 2
        + [sem((2, n))] * 2
        + [sem((NARROW,))] * 2
        + [sem((n,))] * 2,
        compiler_params=pltpu.CompilerParams(
            collective_id=2, has_side_effects=True, vmem_limit_bytes=LIMIT
        ),
    )(*args)


def on_device(
    features,
    norm_gains,
    norm_shifts,
    attention_bias,
    output_bias,
    project_weight,
    merge_weight,
    router_weight,
    router_noise,
    routes,
    slot_numbers,
    expand_weight,
    expand_bias,
    contract_weight,
    contract_bias,
    cotangent,
):
    count, width = features.shape
    n = lax.axis_size("expert")
    e, m = lax.axis_index("expert"), lax.axis_index("mp")
    capacity = 3 * count // n
    quarter = project_weight.shape[2]
    heads = quarter // HEAD
    images = count // SEQ
    rows = round_up(SEQ, 16)
    padded = images * rows
    lanes = round_up(padded, 128)
    capq = round_up(-(-capacity // NARROW), 16)
    lanes_each = 16
    while lanes_each < capq:
        lanes_each *= 2
    each = width // n
    direct = each % 16 == 0
    owners = router_weight.shape[1]
    extra = round_up(owners, 8)

    low = project_weight.astype(BF)
    mat = jnp.concatenate([low[:, 0], low[:, 1], low[:, 2], merge_weight.T.astype(BF)], axis=1)
    share = norm_gains.shape[1]
    packed = jnp.concatenate(
        [norm_gains, norm_shifts, attention_bias, output_bias[None], jnp.zeros((1, share), F32)]
    )
    router_low = router_weight.astype(BF)
    if direct:
        small = jnp.concatenate(
            [
                jnp.pad(packed, ((0, 0), (0, 128 - share))),
                jnp.pad(
                    expand_bias.reshape(-1, 128), ((0, 8 - expand_bias.shape[1] // 128), (0, 0))
                ),
                jnp.pad(
                    router_low.T.astype(F32), ((0, 8 - owners), (0, 128 - each))
                ),
            ]
        )
        rout = jnp.zeros((8, 128), BF)
        first = jnp.zeros((NARROW, 8, 128), F32)
    else:
        mat = lax.all_gather(mat, "expert", axis=0, tiled=True)
        small = lax.all_gather(packed, ("expert", "mp"), axis=1, tiled=True)
        rout = lax.all_gather(router_low, "expert", axis=0, tiled=True).T
        rout = jnp.pad(rout, ((0, 128 - owners), (0, 0)))
        first = lax.all_gather(expand_bias, "mp", axis=0)
        first = jnp.broadcast_to(first, (NARROW, 8, width))

    def along_lanes(value, top, fill):
        value = value.T.reshape(-1, images, SEQ)
        value = jnp.pad(
            value,
            ((0, top - value.shape[0]), (0, 0), (0, rows - SEQ)),
            constant_values=fill,
        )
        return jnp.pad(
            value.reshape(top, padded), ((0, 0), (0, lanes - padded)), constant_values=fill
        )

    keys = along_lanes(routes * (NARROW * capq) + slot_numbers, 8, -1)
    noise = along_lanes(router_noise, extra, 0)
    w1 = lax.all_gather(expand_weight[0].astype(BF), "mp", axis=0)
    w2 = lax.all_gather(contract_weight[0].astype(BF), "mp", axis=0)
    x, a1, q, k, v, p, o, h, a2, cols, mats, rpad, vecs, b1, xr, gr, gt = forward(
        n,
        images,
        rows,
        capq,
        heads,
        direct,
        share,
        features,
        cotangent,
        mat,
        small,
        rout,
        first,
        keys,
        noise,
    )
    slots = n * capq
    dxr, dgr, gy, d1, d2, db = experts(
        n,
        capq,
        lanes_each,
        xr.reshape(slots, width),
        gr.reshape(slots, width),
        gt,
        w1,
        w2,
        b1,
        contract_bias,
        256,
    )
    fg, po, pg, small, router_share, dbo = backward(
        n,
        images,
        rows,
        capq,
        lanes_each,
        direct,
        share,
        owners,
        dxr,
        dgr,
        gy.reshape(n, capq, width),
        x,
        cotangent,
        h,
        a1,
        q,
        k,
        v,
        p,
        o,
        a2,
        cols,
        mats,
        rpad,
        vecs,
        db,
    )
    po = po.reshape(images, rows, -1)[:, :SEQ].reshape(count, -1)
    block_output = lax.dynamic_slice_in_dim(po, lax.rem(m, 2) * quarter, quarter, 1)
    if not direct:
        pg = lax.psum_scatter(pg, "expert", scatter_dimension=0, tiled=True)
        router_share = lax.psum_scatter(
            router_share[:owners].T, "expert", scatter_dimension=0, tiled=True
        )
    return (
        block_output,
        fg,
        small[0:2],
        small[2:4],
        small[4:6],
        small[6],
        pg[:, quarter:].reshape(each, 3, quarter),
        pg[:, :quarter].T,
        router_share,
        d1[None],
        dbo[0:1],
        d2[None],
        dbo[1:2],
    )


def solution(mesh):
    placed = (
        P("expert", None),
        P(None, ("expert", "mp")),
        P(None, ("expert", "mp")),
        P(None, ("expert", "mp")),
        P(("expert", "mp")),
        P("expert", None, "mp"),
        P("mp", "expert"),
        P("expert", None),
        P("expert", None),
        P("expert", None),
        P("expert", None),
        P("expert", None, "mp"),
        P("expert", "mp"),
        P("expert", "mp", None),
        P("expert", None),
        P("expert", None),
    )
    return jax.shard_map(
        on_device,
        mesh=mesh,
        in_specs=placed,
        out_specs=(
            P("expert", "mp"),
            P("expert", None),
            P(None, ("expert", "mp")),
            P(None, ("expert", "mp")),
            P(None, ("expert", "mp")),
            P(("expert", "mp")),
            P("expert", None, "mp"),
            P("mp", "expert"),
            P("expert", None),
            P("expert", None, "mp"),
            P("expert", "mp"),
            P("expert", "mp", None),
            P("expert", None),
        ),
        check_vma=False,
    )
```

```python
import functools

import jax
import jax.numpy as jnp
from jax import lax
from jax.experimental import pallas as pl
from jax.experimental.pallas import tpu as pltpu
from jax.sharding import PartitionSpec as P

HEAD = 64
SEQ = 197
MESH = pl.DeviceIdType.MESH
BF = jnp.bfloat16
F32 = jnp.float32
NARROW = 4
LIMIT = 62 * 1024 * 1024
eps_norm = 1e-06


def round_up(value, step):
    return -(-value // step) * step


def norm_parts(value):
    mean_value = jnp.mean(value, axis=-1, keepdims=True)
    centred = value - mean_value
    variance = jnp.mean(centred * centred, axis=-1, keepdims=True)
    inverse = lax.rsqrt(variance + eps_norm)
    return centred * inverse, inverse


def dot_nn(a, b):
    return jnp.dot(a, b, preferred_element_type=F32)


def dot_nt(a, b):
    return lax.dot_general(a, b, (((1,), (1,)), ((), ())), preferred_element_type=F32)


def dot_tn(a, b):
    return lax.dot_general(a, b, (((0,), (0,)), ((), ())), preferred_element_type=F32)


def places():
    e, m = lax.axis_index("expert"), lax.axis_index("mp")
    c, y = lax.rem(m, 2), lax.div(m, 2)
    return e, m, c, y, m + 1 - 2 * c, lax.rem(m + 2, NARROW)


def greet(n, e, m, narrow):
    barrier = pltpu.get_barrier_semaphore()

    def wide(i, carry):
        pl.semaphore_signal(
            barrier, inc=1, device_id={"expert": lax.rem(e + i, n), "mp": m}, device_id_type=MESH
        )
        return carry

    lax.fori_loop(1, n, wide, 0)
    for other in narrow:
        pl.semaphore_signal(
            barrier, inc=1, device_id={"expert": e, "mp": other}, device_id_type=MESH
        )
    pl.semaphore_wait(barrier, n - 1 + len(narrow))


def remote(src, dst, send, recv, e, m):
    return pltpu.make_async_remote_copy(
        src_ref=src,
        dst_ref=dst,
        send_sem=send,
        recv_sem=recv,
        device_id={"expert": e, "mp": m},
        device_id_type=MESH,
    )


def partner(e, i, n):
    to, bit = e, 1
    while bit < n:
        to = to + lax.rem(lax.div(i, bit), 2) * (bit - 2 * bit * lax.rem(lax.div(e, bit), 2))
        bit *= 2
    return to


def offset_of(s, n):
    rest = lax.rem(s, n // 2)
    return lax.div(rest, 2) * 4 + lax.div(s, n // 2) * 2 + lax.rem(rest, 2)


def mate(e, s, n):
    s = jnp.asarray(s, jnp.int32)
    return partner(e, offset_of(s, n), n)


def move(pairs, sems):
    return [pltpu.make_async_copy(src, dst, sems.at[i]) for i, (src, dst) in enumerate(pairs)]


class Summed:
    def __init__(self, rows, part, sa, sb, tot, sems):
        self.rows, self.part, self.sa, self.sb, self.tot, self.sems = rows, part, sa, sb, tot, sems
        self.e, self.m, self.c, self.y, self.sib, self.far = places()

    def at(self, i):
        return pl.ds(pl.multiple_of(i * self.rows, 16), self.rows)

    def copy_a(self, i):
        at = self.at(i)
        return remote(
            self.part.at[1 - self.c, at],
            self.sa.at[at],
            self.sems.at[0, i],
            self.sems.at[1, i],
            self.e,
            self.sib,
        )

    def copy_b(self, i):
        at = self.at(i)
        return remote(
            self.part.at[self.c, at],
            self.sb.at[at],
            self.sems.at[2, i],
            self.sems.at[3, i],
            self.e,
            self.far,
        )

    def copy_c(self, i, half):
        at = self.at(i)
        return remote(
            self.tot.at[half, at],
            self.tot.at[half, at],
            self.sems.at[4, i],
            self.sems.at[5, i],
            self.e,
            self.sib,
        )

    def start_a(self, i):
        self.copy_a(i).start()

    def step_b(self, i):
        self.copy_a(i).wait_recv()
        at = self.at(i)
        self.part[self.c, at] = (
            self.part[self.c, at].astype(F32) + self.sa[at].astype(F32)
        ).astype(BF)
        self.copy_b(i).start()

    def step_c(self, i):
        self.copy_b(i).wait_recv()
        at = self.at(i)
        self.tot[self.c, at] = (self.part[self.c, at].astype(F32) + self.sb[at].astype(F32)).astype(
            BF
        )
        self.copy_c(i, self.c).start()

    def take(self, i):
        self.copy_c(i, 1 - self.c).wait_recv()
        at = self.at(i)
        return jnp.concatenate([self.tot[0, at].astype(F32), self.tot[1, at].astype(F32)], axis=1)

    def drain(self, images):
        def one(i, carry):
            self.copy_a(i).wait_send()
            self.copy_b(i).wait_send()
            self.copy_c(i, self.c).wait_send()
            return carry

        lax.fori_loop(0, images, one, 0)


def head_masks(width, heads, dtype, value=1.0):
    lane = lax.broadcasted_iota(jnp.int32, (1, width), 1)
    return [
        jnp.where((lane >= h * HEAD) & (lane < (h + 1) * HEAD), value, 0.0).astype(dtype)
        for h in range(heads)
    ]


def forward_kernel(n, images, rows, capq, direct, share, *refs):
    params, rest = refs[: 8 if direct else 4], refs[8 if direct else 4 :]
    forward_body(n, images, rows, capq, direct, share, params, *rest)


def forward_body(
    n,
    images,
    rows,
    capq,
    direct,
    share,
    params,
    x_ref,
    g_ref,
    routes_ref,
    slots_ref,
    noise_in,
    w_ref,
    gb_out,
    xp_out,
    a1_out,
    q_out,
    k_out,
    v_out,
    p_out,
    o_out,
    h_out,
    a2_out,
    mats_out,
    w_out,
    gr_out,
    cols_ref,
    rpad_ref,
    vec_ref,
    b1_ref,
    xs,
    gts,
    gb,
    xp_ref,
    a1_ref,
    q_ref,
    k_ref,
    v_ref,
    p_ref,
    o_ref,
    h_ref,
    a2_ref,
    mats_ref,
    wg,
    gr_ref,
    outs,
    raw,
    packed,
    rpad,
    ab,
    smp,
    sex,
    turn,
    keys_ref,
    noise_ref,
    oh,
    gs,
    wt,
    part,
    sa,
    sb,
    tot,
    ar,
    zs,
    zv,
    nbs,
    nbv,
    pss,
    psv,
    vss,
    vsv,
    gss,
    gsr,
    wss,
    wsv,
):
    e, m, c, y, sib, far = places()
    count, width = xp_ref.shape
    half = width // 2
    lanes = cols_ref.shape[0]
    heads = p_ref.shape[0]
    quarter = heads * HEAD
    group = min(4, n)
    stride = NARROW * capq
    each = width // n
    nodes = n // 2
    beside = e + 1 - 2 * lax.rem(e, 2)
    owners = noise_in.shape[0]

    if direct:
        pw_ref, mw_ref, rw_ref, ng_ref, ns_ref, ab_ref, ob_ref, eb_ref = params
        for j in range(3):
            packed[e, :, (j + 1) * quarter : (j + 2) * quarter] = pw_ref[j].astype(BF)
        turn[0:quarter, 0:each] = mw_ref[...]
        packed[e, :, 0:quarter] = turn[...].T[0:each, 0:quarter].astype(BF)
        smp[m] = jnp.zeros(smp.shape[1:], F32)
        smp[m, 0:2, 0:share] = ng_ref[...]
        smp[m, 2:4, 0:share] = ns_ref[...]
        smp[m, 4:6, 0:share] = ab_ref[...]
        smp[m, 6:7, 0:share] = ob_ref[...]
        for t in range(width // 128):
            smp[m, 8 + t : 9 + t, :] = eb_ref[:, t * 128 : (t + 1) * 128]
        sex[e, NARROW] = jnp.zeros((8, 128), F32)
        sex[e, NARROW, 0:owners, 0:each] = rw_ref[...].astype(BF).astype(F32)
    greet(n, e, m, [lax.rem(m + j, NARROW) for j in range(1, NARROW)])

    def line_copy(d, source):
        to = lax.rem(e + 2 * d, n)
        return remote(packed.at[source], packed.at[source], zs.at[d], zv.at[d], to, m)

    def pair_copy(d, source):
        at = packed.at[source]
        return remote(at, at, nbs.at[d], nbv.at[d], beside, m)

    def small_copy(j, source):
        return remote(
            smp.at[source], smp.at[source], pss.at[j], psv.at[j], e, lax.rem(m + j, NARROW)
        )

    def wide_copy(i, source):
        return remote(
            sex.at[source], sex.at[source], vss.at[i], vsv.at[i], lax.rem(e + i, n), m
        )

    def w_copy(j, source, to):
        return remote(wg.at[source], wg.at[source], wss.at[j], wsv.at[j], e, to)

    if direct:
        for d in range(1, nodes):
            line_copy(d, e).start()
        pair_copy(0, e).start()
        for j in range(1, NARROW):
            small_copy(j, m).start()
    wg[m] = w_ref[0].astype(BF)
    w_copy(0, m, far).start()
    w_copy(1, m, sib).start()

    def pad_into(to_ref, source, cast):
        for i in range(images):
            to_ref[i * rows : i * rows + SEQ, :] = source[i * SEQ : (i + 1) * SEQ, :].astype(cast)
            to_ref[i * rows + SEQ : (i + 1) * rows, :] = jnp.zeros((rows - SEQ, width), cast)

    def build(g, src, send_buf, gates):
        for j in range(group):
            i = g * group + j
            ex = mate(e, i, n)
            want = lax.broadcasted_iota(jnp.int32, (capq, lanes), 0) + (ex * stride + m * capq)
            hit0, hit1 = key0 == want, key1 == want
            oh[j * capq : (j + 1) * capq, :] = jnp.where(hit0 | hit1, 1.0, 0.0).astype(BF)
            if gates is not None:
                w = jnp.where(hit0, gates[0], 0.0) + jnp.where(hit1, gates[1], 0.0)
                ws = w[:, 0:128]
                for t in range(1, lanes // 128):
                    ws = ws + w[:, t * 128 : (t + 1) * 128]
                wt[0:capq, :] = ws
                row = jnp.sum(wt[...].T, axis=0, keepdims=True)
                gts[i] = jnp.broadcast_to(row, (8, 128))
        block = dot_nn(oh[...], src[...]).astype(BF)
        for j in range(group):
            send_buf[g * group + j] = block[j * capq : (j + 1) * capq]

    def g_copy(i):
        return remote(gs.at[i], gr_ref.at[i], gss.at[i], gsr.at[i], mate(e, i, n), m)

    keys_ref[...] = jnp.full(keys_ref.shape, -1, jnp.int32)
    noise_ref[...] = jnp.zeros_like(noise_ref)
    for i in range(images):
        at = slice(i * SEQ, (i + 1) * SEQ)
        to = slice(i * rows, i * rows + SEQ)
        keys_ref[0:2, to] = routes_ref[:, at] * stride + slots_ref[:, at]
        noise_ref[0:owners, to] = noise_in[:, at]
    key0, key1 = keys_ref[0:1, :], keys_ref[1:2, :]

    pad_into(gb, g_ref, BF)
    if lanes > count:
        gb[count:lanes, :] = jnp.zeros((lanes - count, width), BF)
        a2_ref[count:lanes, :] = jnp.zeros((lanes - count, width), BF)
    wt[...] = jnp.zeros_like(wt)

    if direct:
        for j in range(1, NARROW):
            small_copy(j, lax.rem(m + NARROW - j, NARROW)).wait_recv()
        for j in range(NARROW):
            sex[e, j] = smp[j, 0:8]
            for t in range(width // 128):
                b1_ref[j, :, t * 128 : (t + 1) * 128] = jnp.broadcast_to(
                    smp[j, 8 + t : 9 + t], (8, 128)
                )

        def start_wide(i, carry):
            wide_copy(i, e).start()
            return carry

        lax.fori_loop(1, n, start_wide, 0)

    raw[...] = x_ref[...].astype(F32)
    for i in range(images):
        xp_ref[i * rows : (i + 1) * rows, :] = jnp.concatenate(
            [raw[i * SEQ : (i + 1) * SEQ, :], jnp.zeros((rows - SEQ, width), F32)], axis=0
        ).astype(BF)

    def build_g(g, carry):
        build(g, gb, gs, None)
        return carry

    lax.fori_loop(0, n // group // 2, build_g, 0)

    if direct:

        def finish_wide(i, carry):
            wide_copy(i, lax.rem(e + n - i, n)).wait_recv()
            return carry

        lax.fori_loop(1, n, finish_wide, 0)
        vec_ref[...] = jnp.zeros_like(vec_ref)
        rpad[...] = jnp.zeros_like(rpad)
        for i in range(n):
            for j in range(NARROW):
                at = (i * NARROW + j) * share
                vec_ref[:, at : at + share] = sex[i, j, :, 0:share]
            rpad[0:8, i * each : (i + 1) * each] = sex[i, NARROW, :, 0:each]
        rpad_ref[...] = rpad[...].astype(BF)
    else:
        mat_ref, small_ref, rout_ref, first_ref = params
        vec_ref[...] = small_ref[...]
        rpad_ref[...] = rout_ref[...]
        b1_ref[...] = first_ref[...]
    gain0, gain1 = vec_ref[0:1, :], vec_ref[1:2, :]
    shift0, shift1 = vec_ref[2:3, :], vec_ref[3:4, :]
    out_shift = vec_ref[6:7, :]
    ab[...] = jnp.zeros_like(ab)
    for mm in range(NARROW):

        @pl.when(m == mm)
        def _():
            ab[0:2, 0:quarter] = vec_ref[4:6, mm * quarter : (mm + 1) * quarter]

    def first_norm(i, carry):
        at = pl.ds(pl.multiple_of(i * rows, 16), rows)
        normed = norm_parts(xp_ref[at, :].astype(F32))[0]
        a1_ref[at, :] = (normed * gain0 + shift0).astype(BF)
        return carry

    lax.fori_loop(0, images, first_norm, 0)

    if direct:
        for d in range(1, nodes):
            source = lax.rem(e + n - 2 * d, n)
            line_copy(d, source).wait_recv()
            pair_copy(d, source).start()

    lax.fori_loop(n // group // 2, n // group, build_g, 0)
    gr_ref[0] = gs[0]

    if direct:
        for d in range(nodes):
            pair_copy(d, lax.rem(beside + n - 2 * d, n)).wait_recv()
        weights = packed[...].reshape(width, 4 * quarter)
    else:
        weights = mat_ref[...]
    for j in range(4):
        at = ((j + 1) % 4) * quarter
        mats_ref[:, j * 256 : j * 256 + quarter] = weights[:, at : at + quarter]
        mats_ref[:, j * 256 + quarter : (j + 1) * 256] = jnp.zeros((width, 256 - quarter), BF)

    summed = Summed(rows, part, sa, sb, tot, ar)
    in_q = head_masks(256, heads, BF, HEAD ** (-0.5))
    in_o = head_masks(256, heads, F32)
    key_ok = lax.broadcasted_iota(jnp.int32, (rows, rows), 1) < SEQ

    def attend(i):
        at = summed.at(i)
        normed = a1_ref[at, :]
        q = (dot_nn(normed, mats_ref[:, 0:256]) + ab[0:1, :]).astype(BF)
        k = dot_nn(normed, mats_ref[:, 256:512]).astype(BF)
        v = (dot_nn(normed, mats_ref[:, 512:768]) + ab[1:2, :]).astype(BF)
        q_ref[at, :], k_ref[at, :], v_ref[at, :] = q, k, v
        o = jnp.zeros((rows, 256), F32)
        for h in range(heads):
            s = jnp.where(key_ok, dot_nt(q * in_q[h], k), -1e30)
            top = jnp.max(s, axis=-1, keepdims=True)
            ex = jnp.exp(s - top)
            p = (ex / jnp.sum(ex, axis=-1, keepdims=True)).astype(BF)
            p_ref[h, at, :] = p
            o = o + dot_nn(p, v) * in_o[h]
        o = o.astype(BF)
        o_ref[at, :] = o
        for hh in range(2):
            part[hh, at] = dot_nt(o, mats_ref[hh * half : (hh + 1) * half, 768:1024]).astype(BF)

    def second(i):
        at = summed.at(i)
        hidden = xp_ref[at, :].astype(F32) + summed.take(i) + out_shift
        h_ref[0, at], h_ref[1, at] = hidden[:, :half], hidden[:, half:]
        a2_ref[at, :] = (norm_parts(hidden)[0] * gain1 + shift1).astype(BF)

    each_tick = -(-(n - 1) // (images + 1))

    def tick(t, carry):
        for j in range(each_tick):
            i = 1 + t * each_tick + j

            @pl.when(i < n)
            def _():
                g_copy(i).start()

        @pl.when(t < images)
        def _():
            attend(t)
            summed.start_a(t)

        @pl.when((t >= 1) & (t <= images))
        def _():
            summed.step_b(t - 1)

        @pl.when((t >= 3) & (t <= images + 2))
        def _():
            summed.step_c(t - 3)

        @pl.when(t >= 4)
        def _():
            second(t - 4)

        return carry

    lax.fori_loop(0, images + 4, tick, 0)
    kept = move(
        [
            (xp_ref, xp_out),
            (a1_ref, a1_out),
            (q_ref, q_out),
            (k_ref, k_out),
            (v_ref, v_out),
            (p_ref, p_out),
            (o_ref, o_out),
            (h_ref, h_out),
            (a2_ref, a2_out),
            (mats_ref, mats_out),
        ],
        outs,
    )
    kept.append(pltpu.make_async_copy(gb, gb_out, outs.at[12]))
    for copy in kept:
        copy.start()
    w_copy(0, far, far).wait_recv()
    w_copy(2, far, sib).start()

    tops = noise_ref.shape[0]
    logits = dot_nt(rpad_ref[0:tops, :], a2_ref[...]) + noise_ref[...]
    floor = lax.broadcasted_iota(jnp.int32, logits.shape, 0) * stride
    picked = [
        jnp.sum(
            jnp.where((key >= floor) & (key < floor + stride), logits, 0.0), axis=0, keepdims=True
        )
        for key in (key0, key1)
    ]
    top = jnp.maximum(picked[0], picked[1])
    ex0, ex1 = jnp.exp(picked[0] - top), jnp.exp(picked[1] - top)
    gate0, gate1 = ex0 / (ex0 + ex1), ex1 / (ex0 + ex1)

    def build_x(g, carry):
        build(g, a2_ref, xs, (gate0, gate1))
        return carry

    lax.fori_loop(0, n // group, build_x, 0)
    cols_ref[...] = jnp.concatenate(
        [key0.astype(F32), key1.astype(F32), gate0, gate1, jnp.zeros((124, lanes), F32)], axis=0
    ).T

    def finish(i, carry):
        g_copy(i).wait_recv()
        g_copy(i).wait_send()
        if direct:
            wide_copy(i, e).wait_send()
        return carry

    lax.fori_loop(1, n, finish, 0)
    w_copy(1, sib, sib).wait_recv()
    w_copy(2, 3 - m, sib).wait_recv()
    late = [
        pltpu.make_async_copy(gr_ref, gr_out, outs.at[10]),
        pltpu.make_async_copy(wg, w_out, outs.at[11]),
    ]
    for copy in late:
        copy.start()
    summed.drain(images)
    w_copy(0, m, far).wait_send()
    w_copy(1, m, sib).wait_send()
    w_copy(2, far, sib).wait_send()
    if direct:
        for j in range(1, NARROW):
            small_copy(j, m).wait_send()
        for d in range(nodes):
            pair_copy(d, e).wait_send()
            if d > 0:
                line_copy(d, e).wait_send()
    for copy in kept + late:
        copy.wait()


def forward(n, images, rows, capq, heads, direct, share, extra, params, x, g, routes, slots, noise, w):
    width = x.shape[1]
    count = images * rows
    lanes = round_up(count, 128)
    each = width // n
    half = width // 2
    group = min(4, n)
    sem = pltpu.SemaphoreType.DMA
    struct = jax.ShapeDtypeStruct
    moved = [
        ((lanes, width), BF),
        ((count, width), BF),
        ((count, width), BF),
        ((count, 256), BF),
        ((count, 256), BF),
        ((count, 256), BF),
        ((heads, count, rows), BF),
        ((count, 256), BF),
        ((2, count, half), F32),
        ((lanes, width), BF),
        ((width, 1024), BF),
        ((NARROW, *w.shape[1:]), BF),
        ((n, capq, width), BF),
    ]
    held = [
        ((lanes, 128), F32),
        ((128, width), BF),
        ((8, width), F32),
        ((NARROW, 8, width), F32),
        ((n, capq, width), BF),
        ((n, 8, 128), F32),
    ]
    args = (*params, x, g, routes, slots, noise, w)
    return pl.pallas_call(
        functools.partial(forward_kernel, n, images, rows, capq, direct, share),
        name="forward",
        out_shape=tuple(struct(*shape) for shape in moved + held),
        in_specs=[pl.BlockSpec(memory_space=pltpu.VMEM)] * len(args),
        out_specs=(pl.BlockSpec(memory_space=pl.ANY),) * len(moved)
        + (pl.BlockSpec(memory_space=pltpu.VMEM),) * len(held),
        scratch_shapes=[pltpu.VMEM(*shape) for shape in moved]
        + [
            sem((len(moved),)),
            pltpu.VMEM(x.shape, F32),
            pltpu.VMEM((n, each, width) if direct else (1, 16, 128), BF),
            pltpu.VMEM((128, width), F32),
            pltpu.VMEM((8, 256), F32),
            pltpu.VMEM((NARROW, 16, 128), F32),
            pltpu.VMEM((n, NARROW + 1, 8, 128), F32),
            pltpu.VMEM((256, 128), F32),
            pltpu.VMEM((8, lanes), jnp.int32),
            pltpu.VMEM((extra, lanes), F32),
            pltpu.VMEM((group * capq, lanes), BF),
            pltpu.VMEM((n, capq, width), BF),
            pltpu.VMEM((128, 128), F32),
            pltpu.VMEM((2, count, half), BF),
            pltpu.VMEM((count, half), BF),
            pltpu.VMEM((count, half), BF),
            pltpu.VMEM((2, count, half), BF),
            sem((6, images)),
        ]
        + [sem((n // 2,))] * 4
        + [sem((NARROW,))] * 2
        + [sem((n,))] * 4
        + [sem((3,))] * 2,
        compiler_params=pltpu.CompilerParams(
            collective_id=1, has_side_effects=True, vmem_limit_bytes=LIMIT
        ),
    )(*args)


def expert_kernel(
    n,
    capq,
    lanes_each,
    xs_ref,
    gts_ref,
    w2_ref,
    b1_ref,
    b2_ref,
    g_in,
    w1_in,
    dxr_ref,
    dgr_ref,
    gy_out,
    db_ref,
    mine1_out,
    mine2_out,
    sum1_out,
    far2,
    far1,
    g_ref,
    w1_ref,
    gy_ref,
    io,
    wg,
    xr,
    gt,
    gcol,
    dy,
    xt,
    yacc,
    dxacc,
    dxs,
    dgs,
    wt,
    s1,
    s2,
    r1,
    r2,
    wss,
    wsv,
    xss,
    xsv,
    tss,
    tsv,
    ws,
    wv,
    dxss,
    dxsv,
    dgss,
    dgsv,
):
    e, m, c, y, sib, far = places()
    slots, width = g_ref.shape
    part = slots // 2
    load_g, load_w = move([(g_in, g_ref), (w1_in, w1_ref)], io)
    load_g.start()
    load_w.start()
    greet(n, e, m, [sib, far])

    def x_copy(i):
        return remote(xs_ref.at[i], xr.at[i], xss.at[i], xsv.at[i], mate(e, i, n), m)

    def t_copy(i):
        return remote(gts_ref.at[i], gt.at[i], tss.at[i], tsv.at[i], mate(e, i, n), m)

    def start_t(i, carry):
        t_copy(i).start()
        return carry

    def start_x(i, carry):
        x_copy(i).start()
        return carry

    def arrive_x(i, carry):
        x_copy(i).wait_recv()
        return carry

    lax.fori_loop(1, n, start_t, 0)
    lax.fori_loop(1, n // 2, start_x, 0)

    def w_copy(j, source, to):
        return remote(wg.at[source], wg.at[source], wss.at[j], wsv.at[j], e, to)

    wg[m] = w2_ref[0].astype(BF)
    w_copy(0, m, far).start()
    w_copy(1, m, sib).start()
    xr[0] = xs_ref[0]
    gt[0] = gts_ref[0]

    def gate_col(i, carry):
        @pl.when(i > 0)
        def _():
            t_copy(i).wait_recv()

        row = jnp.broadcast_to(gt[i, 0:1, :], (128, 128))
        gcol[pl.ds(pl.multiple_of(i * capq, 16), capq), :] = row.T[0:capq]
        return carry

    lax.fori_loop(0, n, gate_col, 0)
    gate = gcol[:, 0:1]
    load_g.wait()
    grad = (g_ref[...].astype(F32) * gate).astype(BF)
    dy[...] = grad
    db_ref[NARROW] = jnp.broadcast_to(jnp.sum(grad.astype(F32), axis=0, keepdims=True), (8, width))
    if lanes_each > capq:
        dxr_ref[:, capq:lanes_each, :] = jnp.zeros((n, lanes_each - capq, width), BF)

    cut = pl.ds(0, far1.shape[0])

    def d_copies(t, to):
        if t == 1:
            return [
                remote(s2.at[1], far2, ws.at[1, 1], wv.at[1, 1], e, to),
                remote(s1.at[1, cut], far1, ws.at[0, 1], wv.at[0, 1], e, to),
            ]
        return [
            remote(s1.at[t], r1.at[t], ws.at[0, t], wv.at[0, t], e, to),
            remote(s2.at[t], r2.at[t], ws.at[1, t], wv.at[1, t], e, to),
        ]

    def step(piece, t, q, fresh):
        at = pl.ds(piece * part, part)
        x = xr[piece * (n // 2) : (piece + 1) * (n // 2)].reshape(part, width)
        w1, w2 = w1_ref[q], wg[q]
        z = dot_nn(x, w1) + b1_ref[q, 0:1, :]
        cdf = 0.5 * (1.0 + lax.erf(z * (2.0**-0.5)))
        pdf = jnp.exp(-0.5 * z * z) * ((2.0 * jnp.pi) ** -0.5)
        u = (z * cdf).astype(BF)
        dz = dot_nt(dy[at, :], w2) * (cdf + z * pdf)
        db = jnp.broadcast_to(jnp.sum(dz, axis=0, keepdims=True), (8, dz.shape[1]))
        dz = dz.astype(BF)
        ypart, dxpart = dot_nn(u, w2), dot_nt(dz, w1)
        dw2, dw1 = dot_tn(u, dy[at, :]), dot_nn(xt[piece], dz)
        if fresh:
            yacc[at, :] = ypart
            dxacc[at, :] = dxpart
        else:
            yacc[at, :] += ypart
            dxacc[at, :] += dxpart
        if piece == 0:
            db_ref[q] = db
            s2[t] = dw2.astype(BF)
            s1[t] = dw1.astype(BF)
        else:
            db_ref[q] += db
            s2[t] = (s2[t].astype(F32) + dw2).astype(BF)
            s1[t] = (s1[t].astype(F32) + dw1).astype(BF)

    def dx_copy(i):
        return remote(
            dxs.at[i], dxr_ref.at[e, pl.ds(0, capq)], dxss.at[i], dxsv.at[i], mate(e, i, n), m
        )

    def dx_arrival(i):
        to = mate(e, i, n)
        return remote(dxs.at[i], dxr_ref.at[to, pl.ds(0, capq)], dxss.at[i], dxsv.at[i], to, m)

    def dg_copy(i, source):
        to = mate(e, i, n)
        return remote(dgs.at[i], dgr_ref.at[source], dgss.at[i], dgsv.at[i], to, m)

    def start_dx(i, carry):
        at = pl.ds(pl.multiple_of(i * capq, 16), capq)
        dxs[i] = dxacc[at, :].astype(BF)

        @pl.when(i > 0)
        def _():
            dx_copy(i).start()

        return carry

    lax.fori_loop(1, n // 2, arrive_x, 0)
    lax.fori_loop(n // 2, n, start_x, 0)
    xt[0] = xr[0 : n // 2].reshape(part, width).T
    load_w.wait()
    step(0, 3, m, True)
    w_copy(1, sib, sib).wait_recv()
    step(0, 2, sib, False)
    w_copy(0, far, far).wait_recv()
    w_copy(2, far, sib).start()
    step(0, 1, far, False)
    w_copy(2, 3 - m, sib).wait_recv()
    step(0, 0, 3 - m, False)
    lax.fori_loop(0, n // 2, start_dx, 0)

    lax.fori_loop(n // 2, n, arrive_x, 0)
    xt[1] = xr[n // 2 : n].reshape(part, width).T
    step(1, 0, 3 - m, True)
    for copy in d_copies(0, sib):
        copy.start()
    step(1, 1, far, False)
    for copy in d_copies(0, sib):
        copy.wait_recv()
    s2[1] = (s2[1].astype(F32) + r2[0].astype(F32)).astype(BF)
    across = d_copies(1, far)
    across[0].start()
    s1[1] = (s1[1].astype(F32) + r1[0].astype(F32)).astype(BF)
    across[1].start()
    keep = move([(s1.at[1], sum1_out), (s1.at[3], mine1_out), (s2.at[3], mine2_out), (gy_ref, gy_out)], io)
    keep[0].start()
    step(1, 2, sib, False)
    for copy in d_copies(2, sib):
        copy.start()
    step(1, 3, m, False)
    lax.fori_loop(n // 2, n, start_dx, 0)
    dxr_ref[e, 0:capq, :] = dxs[0]

    yv = yacc[...] + b2_ref[0:1, :]
    gy_ref[...] = (yv * gate).astype(BF)
    keep[3].start()
    gcol[...] = jnp.broadcast_to(
        jnp.sum(yv * g_ref[...].astype(F32), axis=1, keepdims=True), gcol.shape
    )
    wt[...] = jnp.zeros_like(wt)
    dgs[...] = jnp.zeros_like(dgs)
    per = max(1, 128 // lanes_each)

    def gate_row(i, carry):
        wt[0:capq, :] = gcol[pl.ds(pl.multiple_of(i * capq, 16), capq), :]
        row = wt[...].T[0:8, :]
        for k in range(per):

            @pl.when(lax.rem(e, per) == k)
            def _():
                dgs[i, :, k * lanes_each : (k + 1) * lanes_each] = row[:, 0:lanes_each]

        @pl.when(i > 0)
        def _():
            dg_copy(i, e).start()

        return carry

    lax.fori_loop(0, n, gate_row, 0)
    dgr_ref[e] = dgs[0]

    for copy in d_copies(2, sib):
        copy.wait_recv()
    s1[3] = (s1[3].astype(F32) + r1[2].astype(F32)).astype(BF)
    s2[3] = (s2[3].astype(F32) + r2[2].astype(F32)).astype(BF)
    keep[1].start()
    keep[2].start()

    def finish(i, carry):
        dx_arrival(i).wait_recv()
        dg_copy(i, mate(e, i, n)).wait_recv()
        dx_copy(i).wait_send()
        dg_copy(i, e).wait_send()
        x_copy(i).wait_send()
        t_copy(i).wait_send()
        return carry

    lax.fori_loop(1, n, finish, 0)
    for copy in across:
        copy.wait_recv()
    for copy in keep:
        copy.wait()
    for t, to in ((0, sib), (1, far), (2, sib)):
        for copy in d_copies(t, to):
            copy.wait_send()
    w_copy(0, m, far).wait_send()
    w_copy(1, m, sib).wait_send()
    w_copy(2, far, sib).wait_send()


def experts(n, capq, lanes_each, xs, gts, g, w1, w2, b1, b2):
    slots, width = g.shape
    hidden = w1.shape[2]
    struct = jax.ShapeDtypeStruct
    sem = pltpu.SemaphoreType.DMA
    one, two = (width, hidden), (hidden, width)
    outs = (
        struct((n, lanes_each, width), BF),
        struct((n, 8, 128), F32),
        struct((slots, width), BF),
        struct((NARROW + 1, 8, width), F32),
        struct(one, BF),
        struct(two, BF),
        struct(one, BF),
        struct(two, BF),
        struct((width // 2, hidden), BF),
    )
    args = (xs, gts, w2, b1, b2, g, w1)
    here, away = pl.BlockSpec(memory_space=pltpu.VMEM), pl.BlockSpec(memory_space=pl.ANY)
    return pl.pallas_call(
        functools.partial(expert_kernel, n, capq, lanes_each),
        name="experts",
        out_shape=outs,
        in_specs=[here] * 5 + [away] * 2,
        out_specs=(here, here, away, here, away, away, away, here, here),
        scratch_shapes=[
            pltpu.VMEM(g.shape, BF),
            pltpu.VMEM(w1.shape, BF),
            pltpu.VMEM((slots, width), BF),
            sem((4,)),
            pltpu.VMEM((NARROW, *two), BF),
            pltpu.VMEM((n, capq, width), BF),
            pltpu.VMEM((n, 8, 128), F32),
            pltpu.VMEM((slots, 128), F32),
            pltpu.VMEM((slots, width), BF),
            pltpu.VMEM((2, width, slots // 2), BF),
            pltpu.VMEM((slots, width), F32),
            pltpu.VMEM((slots, width), F32),
            pltpu.VMEM((n, capq, width), BF),
            pltpu.VMEM((n, 8, 128), F32),
            pltpu.VMEM((128, 128), F32),
            pltpu.VMEM((4, *one), BF),
            pltpu.VMEM((4, *two), BF),
            pltpu.VMEM((3, *one), BF),
            pltpu.VMEM((3, *two), BF),
            sem((3,)),
            sem((3,)),
        ]
        + [sem((n,))] * 4
        + [sem((2, 3))] * 2
        + [sem((n,))] * 4,
        compiler_params=pltpu.CompilerParams(
            collective_id=3, has_side_effects=True, vmem_limit_bytes=LIMIT
        ),
    )(*args)


def backward_kernel(
    n,
    images,
    rows,
    capq,
    lanes_each,
    direct,
    share,
    owners,
    dxr_ref,
    dgr_ref,
    gy_ref,
    cols_ref,
    rpad_ref,
    vec_ref,
    db_ref,
    g_in,
    h_in,
    mats_in,
    q_in,
    k_in,
    v_in,
    p_in,
    x_in,
    o_in,
    a1_in,
    a2_in,
    sum1_in,
    fg_ref,
    po_ref,
    pgr,
    small_ref,
    router_ref,
    dbo_ref,
    far1,
    g_ref,
    h_ref,
    mats_ref,
    q_ref,
    k_ref,
    v_ref,
    p_ref,
    x_ref,
    o_ref,
    a1_ref,
    a2_ref,
    ins,
    gyr,
    oht,
    dlog,
    part,
    sa,
    sb,
    tot,
    dh,
    part2,
    tot2,
    sa2,
    sb2,
    dq,
    dk,
    dv,
    dr,
    acc,
    mine,
    mpv,
    exv,
    pgs,
    ar,
    ar2,
    ppart,
    pin,
    pfar,
    fars,
    pss,
    gys,
    gyv,
    pgss,
    pgsr,
    mss,
    msr,
    ess,
    esr,
):
    e, m, c, y, sib, far = places()
    count, width = x_ref.shape
    half = width // 2
    heads = p_ref.shape[0]
    quarter = heads * HEAD
    each = width // n
    stride = NARROW * capq
    slots = n * lanes_each
    per = max(1, 128 // lanes_each)
    wide = acc.shape[0]
    here = pl.ds(0, capq)
    if lanes_each > capq:
        gyr[:, capq:lanes_each, :] = jnp.zeros((n, lanes_each - capq, width), BF)
    greet(n, e, m, [lax.rem(m + j, NARROW) for j in range(1, NARROW)])

    loads = move(
        [
            (g_in, g_ref),
            (h_in, h_ref),
            (mats_in, mats_ref),
            (q_in, q_ref),
            (k_in, k_ref),
            (v_in, v_ref),
            (p_in, p_ref),
            (x_in, x_ref),
            (o_in, o_ref),
            (a1_in, a1_ref),
            (a2_in, a2_ref),
        ],
        ins,
    )
    for copy in loads:
        copy.start()

    def gy_copy(i, source):
        to = mate(e, i, n)
        return remote(gy_ref.at[i], gyr.at[source, here], gys.at[i], gyv.at[i], to, m)

    def start_gy(i, carry):
        gy_copy(i, e).start()
        return carry

    lax.fori_loop(1, n, start_gy, 0)
    gyr[e, 0:capq, :] = gy_ref[0]
    rest = pl.ds(far1.shape[0], far1.shape[0])
    far_copy = remote(sum1_in.at[rest], far1, fars.at[0], fars.at[1], e, far)

    gain0, gain1 = vec_ref[0:1, :], vec_ref[1:2, :]

    lane = lax.broadcasted_iota(jnp.int32, (1, slots), 1)
    place = lane % lanes_each
    want = (lane // lanes_each) * stride + place + m * capq
    want = jnp.where(place < capq, want, -2).astype(F32)
    pieces = []
    for block in range(n // per):
        piece = dgr_ref[block * per]
        for j in range(1, per):
            piece = piece + dgr_ref[block * per + j]
        pieces.append(piece[0:1, :])
    dgrow = jnp.concatenate(pieces, axis=1)
    acc[...] = jnp.zeros_like(acc)
    summed = Summed(rows, part, sa, sb, tot, ar)
    again = Summed(rows, part2, sa2, sb2, tot2, ar2)
    rfloor = lax.broadcasted_iota(jnp.int32, (1, 128), 1).astype(F32) * stride

    def returned(i):
        at = summed.at(i)
        key = [cols_ref[at, 0:1], cols_ref[at, 1:2]]
        gate = [cols_ref[at, 2:3], cols_ref[at, 3:4]]
        hits = [key[0] == want, key[1] == want]
        oht[at, :] = jnp.where(hits[0] | hits[1], 1.0, 0.0).astype(BF)
        dgate = [jnp.sum(jnp.where(hit, dgrow, 0.0), axis=1, keepdims=True) for hit in hits]
        mean = gate[0] * dgate[0] + gate[1] * dgate[1]
        dl = [
            jnp.where(
                (key[kk] >= rfloor) & (key[kk] < rfloor + stride), gate[kk] * (dgate[kk] - mean), 0.0
            )
            for kk in range(2)
        ]
        dl = (dl[0] + dl[1]).astype(BF)
        dlog[at, :] = dl
        for hh in range(2):
            cut = slice(hh * half, (hh + 1) * half)
            rowsum = dot_nn(oht[at, :], dxr_ref[:, :, cut].reshape(slots, half))
            part[hh, at] = (rowsum + dot_nn(dl, rpad_ref[:, cut])).astype(BF)

    in_b = head_masks(256, heads, BF)
    in_f = head_masks(256, heads, F32)
    scale = HEAD ** (-0.5)

    def attend(i):
        at = summed.at(i)
        da2 = summed.take(i)
        hidden = jnp.concatenate([h_ref[0, at], h_ref[1, at]], axis=1)
        normed, inverse = norm_parts(hidden)
        mixed = da2 * normed
        acc[1:2, :] += jnp.sum(mixed, axis=0, keepdims=True)
        acc[3:4, :] += jnp.sum(da2, axis=0, keepdims=True)
        mean_mixed = jnp.mean(mixed * gain1, axis=-1, keepdims=True)
        g2 = da2 * gain1
        mean_grad = jnp.mean(g2, axis=-1, keepdims=True)
        grad = g_ref[at, :].astype(F32) + inverse * (g2 - mean_grad - normed * mean_mixed)
        dh[at, :] = grad
        acc[6:7, :] += jnp.sum(grad, axis=0, keepdims=True)
        low = grad.astype(BF)
        dr[at, :] = low
        do = dot_nn(low, mats_ref[:, 768:1024]).astype(BF)
        q, k, v = q_ref[at, :], k_ref[at, :], v_ref[at, :]
        zero = jnp.zeros((rows, 256), F32)
        dqa, dka, dva = zero, zero, zero
        for h in range(heads):
            p = p_ref[h, at, :]
            dp = dot_nt(do * in_b[h], v)
            pf = p.astype(F32)
            t = pf * dp
            ds = (t - pf * jnp.sum(t, axis=-1, keepdims=True)).astype(BF)
            dqa = dqa + dot_nn(ds, k) * in_f[h]
            dka = dka + dot_tn(ds, q) * in_f[h]
            dva = dva + dot_tn(p, do) * in_f[h]
        dqb, dkb, dvb = (dqa * scale).astype(BF), (dka * scale).astype(BF), dva.astype(BF)
        dq[at, :], dk[at, :], dv[at, :] = dqb, dkb, dvb
        acc[4:5, 0:256] += jnp.sum(dqb.astype(F32), axis=0, keepdims=True)
        acc[5:6, 0:256] += jnp.sum(dvb.astype(F32), axis=0, keepdims=True)
        for hh in range(2):
            r = slice(hh * half, (hh + 1) * half)
            part2[hh, at] = (
                dot_nt(dqb, mats_ref[r, 0:256])
                + dot_nt(dkb, mats_ref[r, 256:512])
                + dot_nt(dvb, mats_ref[r, 512:768])
            ).astype(BF)

    def last(i):
        at = again.at(i)
        da1 = again.take(i)
        normed, inverse = norm_parts(x_ref[at, :].astype(F32))
        mixed = da1 * normed
        acc[0:1, :] += jnp.sum(mixed, axis=0, keepdims=True)
        acc[2:3, :] += jnp.sum(da1, axis=0, keepdims=True)
        mean_mixed = jnp.mean(mixed * gain0, axis=-1, keepdims=True)
        g1 = da1 * gain0
        mean_grad = jnp.mean(g1, axis=-1, keepdims=True)
        dh[at, :] += inverse * (g1 - mean_grad - normed * mean_mixed)

    def tick(t, carry):
        @pl.when(t < images)
        def _():
            returned(t)
            summed.start_a(t)

        @pl.when((t >= 1) & (t <= images))
        def _():
            summed.step_b(t - 1)

        @pl.when((t >= 3) & (t <= images + 2))
        def _():
            summed.step_c(t - 3)

        @pl.when((t >= 4) & (t <= images + 3))
        def _():
            attend(t - 4)
            again.start_a(t - 4)

        @pl.when((t >= 5) & (t <= images + 4))
        def _():
            again.step_b(t - 5)

        @pl.when((t >= 7) & (t <= images + 6))
        def _():
            again.step_c(t - 7)

        @pl.when(t >= 8)
        def _():
            last(t - 8)

        return carry

    lax.fori_loop(0, 4, tick, 0)
    for copy in loads[0:7]:
        copy.wait()
    lax.fori_loop(4, images + 2, tick, 0)
    for copy in loads[7:]:
        copy.wait()
    lax.fori_loop(images + 2, images + 5, tick, 0)
    far_copy.start()

    def arrive_gy(i, carry):
        gy_copy(i, mate(e, i, n)).wait_recv()
        return carry

    lax.fori_loop(1, n, arrive_gy, 0)

    def combine(i, carry):
        at = summed.at(i)
        for hh in range(2):
            cut = slice(hh * half, (hh + 1) * half)
            ppart[hh, at] = dot_nn(oht[at, :], gyr[:, :, cut].reshape(slots, half)).astype(BF)
        return carry

    lax.fori_loop(0, images, combine, 0)
    both = count // 2
    own = pl.ds(pl.multiple_of(c * both, 16), both)
    other = pl.ds(pl.multiple_of((1 - c) * both, 16), both)
    copy_pa = [
        remote(
            ppart.at[hh, other], pin.at[pl.ds(hh * both, both)], pss.at[hh], pss.at[2 + hh], e, sib
        )
        for hh in range(2)
    ]
    for copy in copy_pa:
        copy.start()

    def pg_copy(b, i):
        to = mate(e, i, n)
        return remote(pgs.at[b, to], pgr.at[b, i], pgss.at[b, i], pgsr.at[b, i], to, m)

    pairs = [(dr, o_ref), (a1_ref, dq), (a1_ref, dk), (a1_ref, dv)]
    for b in range(2):
        for s in range(2):
            left, right = pairs[2 * b + s]
            grad = dot_tn(left[...], right[...])[:, :quarter]
            if direct:
                grad = grad.astype(BF)
                for i in range(n):
                    pgs[b, i, :, s * quarter : (s + 1) * quarter] = grad[i * each : (i + 1) * each]
            else:
                slot = 2 * b + s
                pgr[:, slot * quarter : (slot + 1) * quarter] = grad
        if direct:

            def start_pg(i, carry):
                pg_copy(b, i).start()
                return carry

            lax.fori_loop(1, n, start_pg, 0)
            pgr[b, 0] = pgs[b, e]

    lax.fori_loop(images + 5, images + 6, tick, 0)
    for copy in copy_pa:
        copy.wait_recv()
    for hh in range(2):
        pin[hh * both : (hh + 1) * both] = (
            ppart[hh, own].astype(F32) + pin[hh * both : (hh + 1) * both].astype(F32)
        ).astype(BF)
    send_to = pl.ds(pl.multiple_of((1 - y) * both, 16), both)
    keep_at = pl.ds(pl.multiple_of(y * both, 16), both)
    copy_pb = remote(pin.at[send_to], pfar, pss.at[4], pss.at[5], e, far)
    copy_pb.start()

    lax.fori_loop(images + 6, images + 8, tick, 0)
    summed.drain(images)
    again.drain(images)
    for i in range(images):
        fg_ref[i * SEQ : (i + 1) * SEQ, :] = dh[i * rows : i * rows + SEQ, :]

    acc[8:wide, :] = dot_tn(dlog[...], a2_ref[0:count, :])[0 : wide - 8]
    lane_w = lax.broadcasted_iota(jnp.int32, (1, width), 1)
    own_cols = (lane_w >= m * quarter) & (lane_w < (m + 1) * quarter)
    mine[0:8, :] = jnp.where(own_cols, acc[0:8, :], 0.0)
    mine[8:wide, :] = acc[8:wide, :]
    bias = acc[4:6, 0:quarter]
    mine[4:6, :] = jnp.zeros((2, width), F32)
    for mm in range(NARROW):

        @pl.when(m == mm)
        def _():
            mine[4:6, mm * quarter : (mm + 1) * quarter] = bias

    for j in range(NARROW + 1):
        mine[wide + j : wide + j + 1, :] = db_ref[j, 0:1, :]
    mine[wide + NARROW + 1 :, :] = jnp.zeros((8 - NARROW - 1, width), F32)

    def narrow(j, source):
        return remote(mine, mpv.at[source], mss.at[j], msr.at[j], e, lax.rem(m + j, NARROW))

    for j in range(1, NARROW):
        narrow(j, m).start()
    mpv[m] = mine[...]

    for j in range(1, NARROW):
        narrow(j, lax.rem(m + NARROW - j, NARROW)).wait_recv()
    sums = mpv[0] + mpv[1] + mpv[2] + mpv[3]
    for mm in range(NARROW):

        @pl.when(m == mm)
        def _():
            dbo_ref[0:1, :] = sums[wide + mm : wide + mm + 1]

    dbo_ref[1:2, :] = sums[wide + NARROW : wide + NARROW + 1]
    acc[...] = sums[0:wide]
    def ex_copy(i, to, source):
        return remote(acc, exv.at[source], ess.at[i], esr.at[i], to, m)

    def start_ex(i, carry):
        ex_copy(i, lax.rem(e + i, n), e).start()
        return carry

    def finish_ex(i, carry):
        source = lax.rem(e + n - i, n)
        ex_copy(i, source, source).wait_recv()
        return carry

    if direct:
        lax.fori_loop(1, n, start_ex, 0)
        exv[e] = acc[...]
        lax.fori_loop(1, n, finish_ex, 0)
        total = exv[0]
        for i in range(1, n):
            total = total + exv[i]
        pick = lax.broadcasted_iota(jnp.int32, (width, 128), 0) - lax.broadcasted_iota(
            jnp.int32, (width, 128), 1
        )

        def picked(values, offset):
            return jnp.dot(
                values,
                jnp.where(pick == offset, 1.0, 0.0),
                precision=lax.Precision.HIGHEST,
                preferred_element_type=F32,
            )

        small_ref[...] = picked(total[0:8], (e * NARROW + m) * share)[:, 0:share]
        router_ref[...] = picked(total[8:wide], e * each)[0:owners, 0:each]
    else:
        small_ref[...] = acc[0:8, :]
        router_ref[...] = acc[8:wide, :]

    copy_pb.wait_recv()
    total = pin[keep_at].astype(F32) + pfar[...].astype(F32) + h_ref[y, own]
    po_ref[own, :] = total.astype(BF)
    copy_pc = remote(po_ref.at[own], po_ref.at[own], pss.at[6], pss.at[7], e, sib)
    copy_pc.start()
    wait_pc = remote(po_ref.at[other], po_ref.at[other], pss.at[6], pss.at[7], e, sib)

    if direct:
        for b in range(2):

            def finish_pg(i, carry):
                pg_copy(b, i).wait_recv()
                return carry

            lax.fori_loop(1, n, finish_pg, 0)
    wait_pc.wait_recv()

    def drain(i, carry):
        gy_copy(i, e).wait_send()
        if direct:
            ex_copy(i, lax.rem(e + i, n), e).wait_send()
            pg_copy(0, i).wait_send()
            pg_copy(1, i).wait_send()
        return carry

    lax.fori_loop(1, n, drain, 0)
    for copy in copy_pa + [copy_pb, copy_pc, far_copy] + [narrow(j, m) for j in range(1, NARROW)]:
        copy.wait_send()
    far_copy.wait_recv()


def backward(n, images, rows, capq, lanes_each, direct, share, owners, first, moved, sum1):
    x, p = moved[7], moved[6]
    count, width = x.shape
    half = width // 2
    heads = p.shape[0]
    quarter = heads * HEAD
    slots = n * lanes_each
    each = width // n
    sem = pltpu.SemaphoreType.DMA
    struct = jax.ShapeDtypeStruct
    extra = round_up(owners, 8)
    wide = 8 + extra
    block = (2, n, each, 2 * quarter)
    outs = (
        struct((images * SEQ, width), F32),
        struct((count, half), BF),
        struct(block, BF) if direct else struct((width, 4 * quarter), F32),
        struct((8, share if direct else width), F32),
        struct((owners, each) if direct else (extra, width), F32),
        struct((2, width), F32),
        struct((sum1.shape[0] // 2, sum1.shape[1]), BF),
    )
    args = (*first, *moved, sum1)
    here, away = pl.BlockSpec(memory_space=pltpu.VMEM), pl.BlockSpec(memory_space=pl.ANY)
    return pl.pallas_call(
        functools.partial(
            backward_kernel, n, images, rows, capq, lanes_each, direct, share, owners
        ),
        name="backward",
        out_shape=outs,
        in_specs=[here] * len(first) + [away] * len(moved) + [here],
        out_specs=(here,) * 7,
        scratch_shapes=[pltpu.VMEM(a.shape, a.dtype) for a in moved]
        + [
            sem((len(moved),)),
            pltpu.VMEM((n, lanes_each, width), BF),
            pltpu.VMEM((count, slots), BF),
            pltpu.VMEM((count, 128), BF),
            pltpu.VMEM((2, count, half), BF),
            pltpu.VMEM((count, half), BF),
            pltpu.VMEM((count, half), BF),
            pltpu.VMEM((2, count, half), BF),
            pltpu.VMEM((count, width), F32),
            pltpu.VMEM((2, count, half), BF),
            pltpu.VMEM((2, count, half), BF),
            pltpu.VMEM((count, half), BF),
            pltpu.VMEM((count, half), BF),
            pltpu.VMEM((count, 256), BF),
            pltpu.VMEM((count, 256), BF),
            pltpu.VMEM((count, 256), BF),
            pltpu.VMEM((count, width), BF),
            pltpu.VMEM((wide, width), F32),
            pltpu.VMEM((wide + 8, width), F32),
            pltpu.VMEM((NARROW, wide + 8, width), F32),
            pltpu.VMEM((n, wide, width) if direct else (1, 8, 128), F32),
            pltpu.VMEM(block if direct else (1, 1, 16, 128), BF),
            sem((6, images)),
            sem((6, images)),
            pltpu.VMEM((2, count, half), BF),
            pltpu.VMEM((count, half), BF),
            pltpu.VMEM((count // 2, half), BF),
            sem((2,)),
            sem((8,)),
        ]
        + [sem((n,))] * 2
        + [sem((2, n))] * 2
        + [sem((NARROW,))] * 2
        + [sem((n,))] * 2,
        compiler_params=pltpu.CompilerParams(
            collective_id=2, has_side_effects=True, vmem_limit_bytes=LIMIT
        ),
    )(*args)


def finish_kernel(
    images,
    rows,
    fg_in,
    po_ref,
    pgr_ref,
    small_ref,
    router_in,
    dbo_ref,
    mine1,
    far1a,
    far1b,
    mine2,
    far2,
    out_ref,
    fg_ref,
    gain_ref,
    shift_ref,
    bias_ref,
    oshift_ref,
    pg_ref,
    mg_ref,
    router_ref,
    d1_ref,
    e1_ref,
    d2_ref,
    e2_ref,
    flat,
    tall,
    turn,
    sem,
):
    copy = pltpu.make_async_copy(fg_in, fg_ref, sem)
    copy.start()
    c = lax.rem(lax.axis_index("mp"), 2)
    quarter = out_ref.shape[0]
    for half in range(2):

        @pl.when(c == half)
        def _():
            flat[...] = po_ref[:, half * quarter : (half + 1) * quarter].astype(F32)

    for i in range(images):
        tall[i * SEQ : (i + 1) * SEQ, 0:quarter] = flat[i * rows : i * rows + SEQ, :]
    out_ref[...] = tall[...].T[0:quarter, 0 : images * SEQ].astype(BF)
    gain_ref[...] = small_ref[0:2]
    shift_ref[...] = small_ref[2:4]
    bias_ref[...] = small_ref[4:6]
    oshift_ref[...] = small_ref[6:7]
    router_ref[...] = router_in[...]
    e1_ref[...] = dbo_ref[0:1]
    e2_ref[...] = dbo_ref[1:2]
    totals = []
    for b in range(2):
        total = pgr_ref[b, 0].astype(F32)
        for i in range(1, pgr_ref.shape[1]):
            total = total + pgr_ref[b, i].astype(F32)
        totals.append(total)
    each = totals[0].shape[0]
    turn[0:each, 0:quarter] = totals[0][:, 0:quarter]
    mg_ref[...] = turn[...].T[0:quarter, 0:each]
    pg_ref[0] = totals[0][:, quarter:]
    pg_ref[1] = totals[1][:, 0:quarter]
    pg_ref[2] = totals[1][:, quarter:]
    cut = far1a.shape[0]
    d1_ref[0, 0:cut] = mine1[0:cut].astype(F32) + far1a[...].astype(F32)
    d1_ref[0, cut:] = mine1[cut:].astype(F32) + far1b[...].astype(F32)
    d2_ref[0] = mine2[...].astype(F32) + far2[...].astype(F32)
    copy.wait()


def finish(images, rows, quarter, args):
    fg, po, pgr, small, router, dbo, mine1 = args[:7]
    count, width = fg.shape
    each, share = pgr.shape[2], small.shape[1]
    struct = jax.ShapeDtypeStruct
    outs = (
        struct((quarter, count), BF),
        struct(fg.shape, F32),
        struct((2, share), F32),
        struct((2, share), F32),
        struct((2, share), F32),
        struct((1, share), F32),
        struct((3, each, quarter), F32),
        struct((quarter, each), F32),
        struct(router.shape, F32),
        struct((1, *mine1.shape), F32),
        struct((1, width), F32),
        struct((1, *args[9].shape), F32),
        struct((1, width), F32),
    )
    here, away = pl.BlockSpec(memory_space=pltpu.VMEM), pl.BlockSpec(memory_space=pl.ANY)
    return pl.pallas_call(
        functools.partial(finish_kernel, images, rows),
        name="finish",
        out_shape=outs,
        in_specs=[here] * len(args),
        out_specs=(here, away) + (here,) * (len(outs) - 2),
        scratch_shapes=[
            pltpu.VMEM((po.shape[0], quarter), F32),
            pltpu.VMEM((round_up(count, 128), 256), F32),
            pltpu.VMEM((128, 256), F32),
            pltpu.SemaphoreType.DMA,
        ],
        compiler_params=pltpu.CompilerParams(vmem_limit_bytes=LIMIT),
    )(*args)


def on_device(
    features,
    norm_gains,
    norm_shifts,
    attention_bias,
    output_bias,
    project_weight,
    merge_weight,
    router_weight,
    router_noise,
    routes,
    slot_numbers,
    expand_weight,
    expand_bias,
    contract_weight,
    contract_bias,
    cotangent,
):
    count, width = features.shape
    n = lax.axis_size("expert")
    e, m = lax.axis_index("expert"), lax.axis_index("mp")
    capacity = 3 * count // n
    quarter = project_weight.shape[2]
    heads = quarter // HEAD
    images = count // SEQ
    rows = round_up(SEQ, 16)
    capq = round_up(-(-capacity // NARROW), 16)
    lanes_each = 16
    while lanes_each < capq:
        lanes_each *= 2
    each = width // n
    direct = each % 16 == 0
    owners = router_weight.shape[1]
    extra = round_up(owners, 8)

    share = norm_gains.shape[1]
    if direct:
        params = (
            project_weight.transpose(1, 0, 2),
            merge_weight,
            router_weight.T,
            norm_gains,
            norm_shifts,
            attention_bias,
            output_bias[None],
            expand_bias,
        )
    else:
        low = project_weight.astype(BF)
        mat = jnp.concatenate([merge_weight.T.astype(BF), low[:, 0], low[:, 1], low[:, 2]], axis=1)
        packed = jnp.concatenate(
            [norm_gains, norm_shifts, attention_bias, output_bias[None], jnp.zeros((1, share), F32)]
        )
        rout = lax.all_gather(router_weight.astype(BF), "expert", axis=0, tiled=True).T
        first = lax.all_gather(expand_bias, "mp", axis=0)
        params = (
            lax.all_gather(mat, "expert", axis=0, tiled=True),
            lax.all_gather(packed, ("expert", "mp"), axis=1, tiled=True),
            jnp.pad(rout, ((0, 128 - owners), (0, 0))),
            jnp.broadcast_to(first, (NARROW, 8, width)),
        )
    g, x, a1, q, k, v, p, o, h, a2, mats, w1, gr, cols, rpad, vecs, b1, xs, gts = forward(
        n,
        images,
        rows,
        capq,
        heads,
        direct,
        share,
        extra,
        params,
        features,
        cotangent,
        routes.T,
        slot_numbers.T,
        router_noise.T,
        expand_weight,
    )
    slots = n * capq
    dxr, dgr, gy, db, mine1, mine2, sum1, far2, far1a = experts(
        n, capq, lanes_each, xs, gts, gr.reshape(slots, width), w1, contract_weight, b1, contract_bias
    )
    fg, po, pgr, small, router_share, dbo, far1b = backward(
        n,
        images,
        rows,
        capq,
        lanes_each,
        direct,
        share,
        owners,
        (dxr, dgr, gy.reshape(n, capq, width), cols, rpad, vecs, db),
        (g, h, mats, q, k, v, p, x, o, a1, a2),
        sum1,
    )
    if not direct:
        small = lax.psum_scatter(small, "expert", scatter_dimension=1, tiled=True)
        small = lax.dynamic_slice_in_dim(small, m * share, share, 1)
        pg = lax.psum_scatter(pgr, "expert", scatter_dimension=0, tiled=True)
        pgr = jnp.stack([pg[:, : 2 * quarter], pg[:, 2 * quarter :]])[:, None]
        router_share = lax.psum_scatter(
            router_share[:owners].T, "expert", scatter_dimension=0, tiled=True
        ).T
    done = finish(
        images,
        rows,
        quarter,
        (fg, po, pgr, small, router_share, dbo, mine1, far1a, far1b, mine2, far2),
    )
    out, fg, gain, shift, bias, oshift, pg, mg, router_share, d1, e1, d2, e2 = done
    return (
        out.T,
        fg,
        gain,
        shift,
        bias,
        oshift[0],
        pg.transpose(1, 0, 2),
        mg,
        router_share.T,
        d1,
        e1,
        d2,
        e2,
    )


def solution(mesh):
    placed = (
        P("expert", None),
        P(None, ("expert", "mp")),
        P(None, ("expert", "mp")),
        P(None, ("expert", "mp")),
        P(("expert", "mp")),
        P("expert", None, "mp"),
        P("mp", "expert"),
        P("expert", None),
        P("expert", None),
        P("expert", None),
        P("expert", None),
        P("expert", None, "mp"),
        P("expert", "mp"),
        P("expert", "mp", None),
        P("expert", None),
        P("expert", None),
    )
    return jax.shard_map(
        on_device,
        mesh=mesh,
        in_specs=placed,
        out_specs=(
            P("expert", "mp"),
            P("expert", None),
            P(None, ("expert", "mp")),
            P(None, ("expert", "mp")),
            P(None, ("expert", "mp")),
            P(("expert", "mp")),
            P("expert", None, "mp"),
            P("mp", "expert"),
            P("expert", None),
            P("expert", None, "mp"),
            P("expert", "mp"),
            P("expert", "mp", None),
            P("expert", None),
        ),
        check_vma=False,
    )
```

```python
import functools

import jax
import jax.numpy as jnp
from jax import lax
from jax.experimental import pallas as pl
from jax.experimental.pallas import tpu as pltpu
from jax.sharding import PartitionSpec as P

HEAD = 64
SEQ = 197
MESH = pl.DeviceIdType.MESH
BF = jnp.bfloat16
F32 = jnp.float32
NARROW = 4
EARLY = 1
LIMIT = 62 * 1024 * 1024
eps_norm = 1e-06


def round_up(value, step):
    return -(-value // step) * step


def norm_parts(value):
    mean_value = jnp.mean(value, axis=-1, keepdims=True)
    centred = value - mean_value
    variance = jnp.mean(centred * centred, axis=-1, keepdims=True)
    inverse = lax.rsqrt(variance + eps_norm)
    return centred * inverse, inverse


def dot_nn(a, b):
    return jnp.dot(a, b, preferred_element_type=F32)


def dot_nt(a, b):
    return lax.dot_general(a, b, (((1,), (1,)), ((), ())), preferred_element_type=F32)


def dot_tn(a, b):
    return lax.dot_general(a, b, (((0,), (0,)), ((), ())), preferred_element_type=F32)


def places():
    e, m = lax.axis_index("expert"), lax.axis_index("mp")
    c, y = lax.rem(m, 2), lax.div(m, 2)
    return e, m, c, y, m + 1 - 2 * c, lax.rem(m + 2, NARROW)


def greet(n, e, m, narrow):
    barrier = pltpu.get_barrier_semaphore()

    def wide(i, carry):
        pl.semaphore_signal(
            barrier, inc=1, device_id={"expert": lax.rem(e + i, n), "mp": m}, device_id_type=MESH
        )
        return carry

    lax.fori_loop(1, n, wide, 0)
    for other in narrow:
        pl.semaphore_signal(
            barrier, inc=1, device_id={"expert": e, "mp": other}, device_id_type=MESH
        )
    pl.semaphore_wait(barrier, n - 1 + len(narrow))


def remote(src, dst, send, recv, e, m):
    return pltpu.make_async_remote_copy(
        src_ref=src,
        dst_ref=dst,
        send_sem=send,
        recv_sem=recv,
        device_id={"expert": e, "mp": m},
        device_id_type=MESH,
    )


def partner(e, i, n):
    to, bit = e, 1
    while bit < n:
        to = to + lax.rem(lax.div(i, bit), 2) * (bit - 2 * bit * lax.rem(lax.div(e, bit), 2))
        bit *= 2
    return to


def offset_of(s, n):
    rest = lax.rem(s, n // 2)
    return lax.div(rest, 2) * 4 + lax.div(s, n // 2) * 2 + lax.rem(rest, 2)


def mate(e, s, n):
    s = jnp.asarray(s, jnp.int32)
    return partner(e, offset_of(s, n), n)


def move(pairs, sems):
    return [pltpu.make_async_copy(src, dst, sems.at[i]) for i, (src, dst) in enumerate(pairs)]


class Summed:
    def __init__(self, rows, part, sa, sb, tot, sems):
        self.rows, self.part, self.sa, self.sb, self.tot, self.sems = rows, part, sa, sb, tot, sems
        self.e, self.m, self.c, self.y, self.sib, self.far = places()

    def at(self, i):
        return pl.ds(pl.multiple_of(i * self.rows, 16), self.rows)

    def copy_a(self, i):
        at = self.at(i)
        return remote(
            self.part.at[1 - self.c, at],
            self.sa.at[at],
            self.sems.at[0, i],
            self.sems.at[1, i],
            self.e,
            self.sib,
        )

    def copy_b(self, i):
        at = self.at(i)
        return remote(
            self.part.at[self.c, at],
            self.sb.at[at],
            self.sems.at[2, i],
            self.sems.at[3, i],
            self.e,
            self.far,
        )

    def copy_c(self, i, half):
        at = self.at(i)
        return remote(
            self.tot.at[half, at],
            self.tot.at[half, at],
            self.sems.at[4, i],
            self.sems.at[5, i],
            self.e,
            self.sib,
        )

    def start_a(self, i):
        self.copy_a(i).start()

    def step_b(self, i):
        self.copy_a(i).wait_recv()
        at = self.at(i)
        self.part[self.c, at] = (
            self.part[self.c, at].astype(F32) + self.sa[at].astype(F32)
        ).astype(BF)
        self.copy_b(i).start()

    def step_c(self, i):
        self.copy_b(i).wait_recv()
        at = self.at(i)
        self.tot[self.c, at] = (self.part[self.c, at].astype(F32) + self.sb[at].astype(F32)).astype(
            BF
        )
        self.copy_c(i, self.c).start()

    def take(self, i):
        self.copy_c(i, 1 - self.c).wait_recv()
        at = self.at(i)
        return jnp.concatenate([self.tot[0, at].astype(F32), self.tot[1, at].astype(F32)], axis=1)

    def drain(self, images):
        def one(i, carry):
            self.copy_a(i).wait_send()
            self.copy_b(i).wait_send()
            self.copy_c(i, self.c).wait_send()
            return carry

        lax.fori_loop(0, images, one, 0)


def head_masks(width, heads, dtype, value=1.0):
    lane = lax.broadcasted_iota(jnp.int32, (1, width), 1)
    return [
        jnp.where((lane >= h * HEAD) & (lane < (h + 1) * HEAD), value, 0.0).astype(dtype)
        for h in range(heads)
    ]


def forward_kernel(n, images, rows, capq, direct, share, *refs):
    params, rest = refs[: 8 if direct else 4], refs[8 if direct else 4 :]
    forward_body(n, images, rows, capq, direct, share, params, *rest)


def forward_body(
    n,
    images,
    rows,
    capq,
    direct,
    share,
    params,
    x_in,
    g_in,
    routes_ref,
    slots_ref,
    noise_in,
    w_in,
    w2_in,
    gb_out,
    xp_out,
    a1_out,
    q_out,
    k_out,
    v_out,
    p_out,
    o_out,
    h_out,
    a2_out,
    mats_out,
    w_out,
    gr_out,
    w2_out,
    cols_ref,
    rpad_ref,
    vec_ref,
    b1_ref,
    xs_late,
    xr_ref,
    gt_ref,
    gb,
    xp_ref,
    a1_ref,
    q_ref,
    k_ref,
    v_ref,
    p_ref,
    o_ref,
    h_ref,
    a2_ref,
    mats_ref,
    wg,
    gr_ref,
    wg2,
    outs,
    x_ref,
    g_ref,
    w_ref,
    ins,
    raw,
    packed,
    rpad,
    ab,
    smp,
    sex,
    turn,
    keys_ref,
    noise_ref,
    oh,
    gs,
    xs,
    gts,
    wt,
    part,
    sa,
    sb,
    tot,
    ar,
    zs,
    zv,
    nbs,
    nbv,
    pss,
    psv,
    vss,
    vsv,
    gss,
    gsr,
    xss,
    xsr,
    tss,
    tsr,
    wss,
    wsv,
):
    e, m, c, y, sib, far = places()
    count, width = xp_ref.shape
    half = width // 2
    lanes = cols_ref.shape[0]
    heads = p_ref.shape[0]
    quarter = heads * HEAD
    group = min(4, n)
    stride = NARROW * capq
    each = width // n
    nodes = n // 2
    beside = e + 1 - 2 * lax.rem(e, 2)
    owners = noise_in.shape[0]
    load_w, load_g, load_x = move([(w_in, w_ref), (g_in, g_ref), (x_in, x_ref)], ins)
    load_w2 = pltpu.make_async_copy(w2_in, w_ref, ins.at[3])
    for copy in (load_w, load_g, load_x):
        copy.start()

    if direct:
        pw_ref, mw_ref, rw_ref, ng_ref, ns_ref, ab_ref, ob_ref, eb_ref = params
        for j in range(3):
            packed[e, :, (j + 1) * quarter : (j + 2) * quarter] = pw_ref[j].astype(BF)
        turn[0:quarter, 0:each] = mw_ref[...]
        packed[e, :, 0:quarter] = turn[...].T[0:each, 0:quarter].astype(BF)
        smp[m] = jnp.zeros(smp.shape[1:], F32)
        smp[m, 0:2, 0:share] = ng_ref[...]
        smp[m, 2:4, 0:share] = ns_ref[...]
        smp[m, 4:6, 0:share] = ab_ref[...]
        smp[m, 6:7, 0:share] = ob_ref[...]
        for t in range(width // 128):
            smp[m, 8 + t : 9 + t, :] = eb_ref[:, t * 128 : (t + 1) * 128]
        sex[e, NARROW] = jnp.zeros((8, 128), F32)
        sex[e, NARROW, 0:owners, 0:each] = rw_ref[...].astype(BF).astype(F32)
    greet(n, e, m, [lax.rem(m + j, NARROW) for j in range(1, NARROW)])

    def line_copy(d, source):
        to = lax.rem(e + 2 * d, n)
        return remote(packed.at[source], packed.at[source], zs.at[d], zv.at[d], to, m)

    def pair_copy(d, source):
        at = packed.at[source]
        return remote(at, at, nbs.at[d], nbv.at[d], beside, m)

    def small_copy(j, source):
        return remote(
            smp.at[source], smp.at[source], pss.at[j], psv.at[j], e, lax.rem(m + j, NARROW)
        )

    def wide_copy(i, source):
        return remote(
            sex.at[source], sex.at[source], vss.at[i], vsv.at[i], lax.rem(e + i, n), m
        )

    def w_copy(j, source, to):
        return remote(wg.at[source], wg.at[source], wss.at[j], wsv.at[j], e, to)

    def w2_copy(j, source, to):
        return remote(wg2.at[source], wg2.at[source], wss.at[3 + j], wsv.at[3 + j], e, to)

    if direct:
        for d in range(1, nodes):
            line_copy(d, e).start()
        pair_copy(0, e).start()
        for j in range(1, NARROW):
            small_copy(j, m).start()
    load_w.wait()
    wg[m] = w_ref[0].astype(BF)
    load_w2.start()
    w_copy(0, m, far).start()
    w_copy(1, m, sib).start()

    def pad_into(to_ref, source, cast):
        for i in range(images):
            to_ref[i * rows : i * rows + SEQ, :] = source[i * SEQ : (i + 1) * SEQ, :].astype(cast)
            to_ref[i * rows + SEQ : (i + 1) * rows, :] = jnp.zeros((rows - SEQ, width), cast)

    def build(g, src, send_buf, gates):
        for j in range(group):
            i = g * group + j
            ex = mate(e, i, n)
            want = lax.broadcasted_iota(jnp.int32, (capq, lanes), 0) + (ex * stride + m * capq)
            hit0, hit1 = key0 == want, key1 == want
            oh[j * capq : (j + 1) * capq, :] = jnp.where(hit0 | hit1, 1.0, 0.0).astype(BF)
            if gates is not None:
                w = jnp.where(hit0, gates[0], 0.0) + jnp.where(hit1, gates[1], 0.0)
                ws = w[:, 0:128]
                for t in range(1, lanes // 128):
                    ws = ws + w[:, t * 128 : (t + 1) * 128]
                wt[0:capq, :] = ws
                row = jnp.sum(wt[...].T, axis=0, keepdims=True)
                gts[i] = jnp.broadcast_to(row, (8, 128))
        block = dot_nn(oh[...], src[...]).astype(BF)
        for j in range(group):
            send_buf[g * group + j] = block[j * capq : (j + 1) * capq]

    early = n // 2

    def x_copy(i):
        return remote(xs.at[i], xr_ref.at[i], xss.at[i], xsr.at[i], mate(e, i, n), m)

    def t_copy(i):
        return remote(gts.at[i], gt_ref.at[i], tss.at[i], tsr.at[i], mate(e, i, n), m)

    def g_copy(i):
        return remote(gs.at[i], gr_ref.at[i], gss.at[i], gsr.at[i], mate(e, i, n), m)

    keys_ref[...] = jnp.full(keys_ref.shape, -1, jnp.int32)
    noise_ref[...] = jnp.zeros_like(noise_ref)
    for i in range(images):
        at = slice(i * SEQ, (i + 1) * SEQ)
        to = slice(i * rows, i * rows + SEQ)
        keys_ref[0:2, to] = routes_ref[:, at] * stride + slots_ref[:, at]
        noise_ref[0:owners, to] = noise_in[:, at]
    key0, key1 = keys_ref[0:1, :], keys_ref[1:2, :]

    load_g.wait()
    pad_into(gb, g_ref, BF)
    if lanes > count:
        gb[count:lanes, :] = jnp.zeros((lanes - count, width), BF)
        a2_ref[count:lanes, :] = jnp.zeros((lanes - count, width), BF)
    wt[...] = jnp.zeros_like(wt)

    if direct:
        for j in range(1, NARROW):
            small_copy(j, lax.rem(m + NARROW - j, NARROW)).wait_recv()
        for j in range(NARROW):
            sex[e, j] = smp[j, 0:8]
            for t in range(width // 128):
                b1_ref[j, :, t * 128 : (t + 1) * 128] = jnp.broadcast_to(
                    smp[j, 8 + t : 9 + t], (8, 128)
                )

        def start_wide(i, carry):
            wide_copy(i, e).start()
            return carry

        lax.fori_loop(1, n, start_wide, 0)

    load_x.wait()
    raw[...] = x_ref[...].astype(F32)
    for i in range(images):
        xp_ref[i * rows : (i + 1) * rows, :] = jnp.concatenate(
            [raw[i * SEQ : (i + 1) * SEQ, :], jnp.zeros((rows - SEQ, width), F32)], axis=0
        ).astype(BF)

    def build_g(g, carry):
        build(g, gb, gs, None)
        return carry

    lax.fori_loop(0, n // group // 2, build_g, 0)

    if direct:

        def finish_wide(i, carry):
            wide_copy(i, lax.rem(e + n - i, n)).wait_recv()
            return carry

        lax.fori_loop(1, n, finish_wide, 0)
        vec_ref[...] = jnp.zeros_like(vec_ref)
        rpad[...] = jnp.zeros_like(rpad)
        for i in range(n):
            for j in range(NARROW):
                at = (i * NARROW + j) * share
                vec_ref[:, at : at + share] = sex[i, j, :, 0:share]
            rpad[0:8, i * each : (i + 1) * each] = sex[i, NARROW, :, 0:each]
        rpad_ref[...] = rpad[...].astype(BF)
    else:
        mat_ref, small_ref, rout_ref, first_ref = params
        vec_ref[...] = small_ref[...]
        rpad_ref[...] = rout_ref[...]
        b1_ref[...] = first_ref[...]
    gain0, gain1 = vec_ref[0:1, :], vec_ref[1:2, :]
    shift0, shift1 = vec_ref[2:3, :], vec_ref[3:4, :]
    out_shift = vec_ref[6:7, :]
    ab[...] = jnp.zeros_like(ab)
    for mm in range(NARROW):

        @pl.when(m == mm)
        def _():
            ab[0:2, 0:quarter] = vec_ref[4:6, mm * quarter : (mm + 1) * quarter]

    def first_norm(i, carry):
        at = pl.ds(pl.multiple_of(i * rows, 16), rows)
        normed = norm_parts(xp_ref[at, :].astype(F32))[0]
        a1_ref[at, :] = (normed * gain0 + shift0).astype(BF)
        return carry

    lax.fori_loop(0, images, first_norm, 0)

    if direct:
        for d in range(1, nodes):
            source = lax.rem(e + n - 2 * d, n)
            line_copy(d, source).wait_recv()
            pair_copy(d, source).start()

    lax.fori_loop(n // group // 2, n // group, build_g, 0)
    gr_ref[0] = gs[0]

    if direct:
        for d in range(nodes):
            pair_copy(d, lax.rem(beside + n - 2 * d, n)).wait_recv()
        weights = packed[...].reshape(width, 4 * quarter)
    else:
        weights = mat_ref[...]
    for j in range(4):
        at = ((j + 1) % 4) * quarter
        mats_ref[:, j * 256 : j * 256 + quarter] = weights[:, at : at + quarter]
        mats_ref[:, j * 256 + quarter : (j + 1) * 256] = jnp.zeros((width, 256 - quarter), BF)

    summed = Summed(rows, part, sa, sb, tot, ar)
    in_q = head_masks(256, heads, BF, HEAD ** (-0.5))
    in_o = head_masks(256, heads, F32)
    key_ok = lax.broadcasted_iota(jnp.int32, (rows, rows), 1) < SEQ

    def attend(i):
        at = summed.at(i)
        normed = a1_ref[at, :]
        q = (dot_nn(normed, mats_ref[:, 0:256]) + ab[0:1, :]).astype(BF)
        k = dot_nn(normed, mats_ref[:, 256:512]).astype(BF)
        v = (dot_nn(normed, mats_ref[:, 512:768]) + ab[1:2, :]).astype(BF)
        q_ref[at, :], k_ref[at, :], v_ref[at, :] = q, k, v
        o = jnp.zeros((rows, 256), F32)
        for h in range(heads):
            s = jnp.where(key_ok, dot_nt(q * in_q[h], k), -1e30)
            top = jnp.max(s, axis=-1, keepdims=True)
            ex = jnp.exp(s - top)
            p = (ex / jnp.sum(ex, axis=-1, keepdims=True)).astype(BF)
            p_ref[h, at, :] = p
            o = o + dot_nn(p, v) * in_o[h]
        o = o.astype(BF)
        o_ref[at, :] = o
        for hh in range(2):
            part[hh, at] = dot_nt(o, mats_ref[hh * half : (hh + 1) * half, 768:1024]).astype(BF)

    def second(i):
        at = summed.at(i)
        hidden = xp_ref[at, :].astype(F32) + summed.take(i) + out_shift
        h_ref[0, at], h_ref[1, at] = hidden[:, :half], hidden[:, half:]
        a2_ref[at, :] = (norm_parts(hidden)[0] * gain1 + shift1).astype(BF)

    each_tick = -(-(n - 1) // (images + 1))

    def tick(t, carry):
        for j in range(each_tick):
            i = 1 + t * each_tick + j

            @pl.when(i < n)
            def _():
                g_copy(i).start()

        @pl.when(t < images)
        def _():
            attend(t)
            summed.start_a(t)

        @pl.when((t >= 1) & (t <= images))
        def _():
            summed.step_b(t - 1)

        @pl.when(t == images)
        def _():
            w2_copy(0, m, far).start()
            w2_copy(1, m, sib).start()

        @pl.when((t >= 3) & (t <= images + 2))
        def _():
            summed.step_c(t - 3)

        @pl.when(t >= 4)
        def _():
            second(t - 4)

        return carry

    load_w2.wait()
    wg2[m] = w_ref[0].astype(BF)
    lax.fori_loop(0, images + 4, tick, 0)
    kept = move(
        [
            (xp_ref, xp_out),
            (a1_ref, a1_out),
            (q_ref, q_out),
            (k_ref, k_out),
            (v_ref, v_out),
            (p_ref, p_out),
            (o_ref, o_out),
            (h_ref, h_out),
            (a2_ref, a2_out),
            (mats_ref, mats_out),
        ],
        outs,
    )
    kept.append(pltpu.make_async_copy(gb, gb_out, outs.at[12]))
    for copy in kept:
        copy.start()
    w_copy(0, far, far).wait_recv()
    w_copy(2, far, sib).start()

    tops = noise_ref.shape[0]
    logits = dot_nt(rpad_ref[0:tops, :], a2_ref[...]) + noise_ref[...]
    floor = lax.broadcasted_iota(jnp.int32, logits.shape, 0) * stride
    picked = [
        jnp.sum(
            jnp.where((key >= floor) & (key < floor + stride), logits, 0.0), axis=0, keepdims=True
        )
        for key in (key0, key1)
    ]
    top = jnp.maximum(picked[0], picked[1])
    ex0, ex1 = jnp.exp(picked[0] - top), jnp.exp(picked[1] - top)
    gate0, gate1 = ex0 / (ex0 + ex1), ex1 / (ex0 + ex1)

    def build_x(g, carry):
        build(g, a2_ref, xs, (gate0, gate1))
        return carry

    def start_x(i, carry):
        x_copy(i).start()
        return carry

    def start_t(i, carry):
        t_copy(i).start()
        return carry

    lax.fori_loop(0, early // group, build_x, 0)
    lax.fori_loop(1, early, start_x, 0)
    lax.fori_loop(early // group, n // group, build_x, 0)
    lax.fori_loop(1, n, start_t, 0)
    xr_ref[0] = xs[0]
    gt_ref[0] = gts[0]
    xs_late[...] = xs[early:n]
    cols_ref[...] = jnp.concatenate(
        [key0.astype(F32), key1.astype(F32), gate0, gate1, jnp.zeros((124, lanes), F32)], axis=0
    ).T
    w_copy(1, sib, sib).wait_recv()
    w_copy(2, 3 - m, sib).wait_recv()
    w2_copy(1, sib, sib).wait_recv()
    late = [
        pltpu.make_async_copy(wg, w_out, outs.at[11]),
        pltpu.make_async_copy(wg2.at[m], w2_out.at[m], outs.at[13]),
        pltpu.make_async_copy(wg2.at[sib], w2_out.at[sib], outs.at[14]),
    ]
    for copy in late:
        copy.start()

    def finish(i, carry):
        g_copy(i).wait_recv()
        g_copy(i).wait_send()
        t_copy(i).wait_recv()
        t_copy(i).wait_send()
        if direct:
            wide_copy(i, e).wait_send()
        return carry

    def finish_x(i, carry):
        x_copy(i).wait_recv()
        x_copy(i).wait_send()
        return carry

    lax.fori_loop(1, n, finish, 0)
    late.append(pltpu.make_async_copy(gr_ref, gr_out, outs.at[10]))
    late[-1].start()
    lax.fori_loop(1, early, finish_x, 0)
    w2_copy(0, far, far).wait_recv()
    late.append(pltpu.make_async_copy(wg2.at[far], w2_out.at[far], outs.at[15]))
    late[-1].start()
    w2_copy(0, m, far).wait_send()
    w2_copy(1, m, sib).wait_send()
    summed.drain(images)
    w_copy(0, m, far).wait_send()
    w_copy(1, m, sib).wait_send()
    w_copy(2, far, sib).wait_send()
    if direct:
        for j in range(1, NARROW):
            small_copy(j, m).wait_send()
        for d in range(nodes):
            pair_copy(d, e).wait_send()
            if d > 0:
                line_copy(d, e).wait_send()
    for copy in kept + late:
        copy.wait()


def forward(
    n, images, rows, capq, heads, direct, share, extra, params, x, g, routes, slots, noise, w, w2
):
    width = x.shape[1]
    count = images * rows
    lanes = round_up(count, 128)
    each = width // n
    half = width // 2
    group = min(4, n)
    sem = pltpu.SemaphoreType.DMA
    struct = jax.ShapeDtypeStruct
    moved = [
        ((lanes, width), BF),
        ((count, width), BF),
        ((count, width), BF),
        ((count, 256), BF),
        ((count, 256), BF),
        ((count, 256), BF),
        ((heads, count, rows), BF),
        ((count, 256), BF),
        ((2, count, half), F32),
        ((lanes, width), BF),
        ((width, 1024), BF),
        ((NARROW, *w.shape[1:]), BF),
        ((n, capq, width), BF),
        ((NARROW, *w2.shape[1:]), BF),
    ]
    held = [
        ((lanes, 128), F32),
        ((128, width), BF),
        ((8, width), F32),
        ((NARROW, 8, width), F32),
        ((n - n // 2, capq, width), BF),
        ((n // 2, capq, width), BF),
        ((n, 8, 128), F32),
    ]
    args = (*params, x, g, routes, slots, noise, w, w2)
    here, away = pl.BlockSpec(memory_space=pltpu.VMEM), pl.BlockSpec(memory_space=pl.ANY)
    return pl.pallas_call(
        functools.partial(forward_kernel, n, images, rows, capq, direct, share),
        name="forward",
        out_shape=tuple(struct(*shape) for shape in moved + held),
        in_specs=[here] * len(params) + [away] * 2 + [here] * 3 + [away] * 2,
        out_specs=(pl.BlockSpec(memory_space=pl.ANY),) * len(moved)
        + (pl.BlockSpec(memory_space=pltpu.VMEM),) * len(held),
        scratch_shapes=[pltpu.VMEM(*shape) for shape in moved]
        + [
            sem((len(moved) + 2,)),
            pltpu.VMEM(x.shape, BF),
            pltpu.VMEM(g.shape, F32),
            pltpu.VMEM(w.shape, F32),
            sem((4,)),
            pltpu.VMEM(x.shape, F32),
            pltpu.VMEM((n, each, width) if direct else (1, 16, 128), BF),
            pltpu.VMEM((128, width), F32),
            pltpu.VMEM((8, 256), F32),
            pltpu.VMEM((NARROW, 16, 128), F32),
            pltpu.VMEM((n, NARROW + 1, 8, 128), F32),
            pltpu.VMEM((256, 128), F32),
            pltpu.VMEM((8, lanes), jnp.int32),
            pltpu.VMEM((extra, lanes), F32),
            pltpu.VMEM((group * capq, lanes), BF),
            pltpu.VMEM((n, capq, width), BF),
            pltpu.VMEM((n, capq, width), BF),
            pltpu.VMEM((n, 8, 128), F32),
            pltpu.VMEM((128, 128), F32),
            pltpu.VMEM((2, count, half), BF),
            pltpu.VMEM((count, half), BF),
            pltpu.VMEM((count, half), BF),
            pltpu.VMEM((2, count, half), BF),
            sem((6, images)),
        ]
        + [sem((n // 2,))] * 4
        + [sem((NARROW,))] * 2
        + [sem((n,))] * 8
        + [sem((6,))] * 2,
        compiler_params=pltpu.CompilerParams(
            collective_id=1, has_side_effects=True, vmem_limit_bytes=LIMIT
        ),
    )(*args)


def expert_kernel(
    n,
    capq,
    lanes_each,
    xs_ref,
    x_early,
    gt,
    b1_ref,
    b2_ref,
    g_in,
    w1_in,
    w2_in,
    dxr_ref,
    dgr_ref,
    gy_out,
    db_ref,
    mine1_out,
    mine2_out,
    sum1_out,
    far2,
    far1,
    g_ref,
    w1_ref,
    gy_ref,
    io,
    wg,
    xr,
    gcol,
    dy,
    xt,
    yacc,
    dxacc,
    dxs,
    dgs,
    wt,
    s1,
    s2,
    r1,
    r2,
    wss,
    wsv,
    xss,
    xsv,
    ws,
    wv,
    dxss,
    dxsv,
    dgss,
    dgsv,
):
    e, m, c, y, sib, far = places()
    slots, width = g_ref.shape
    part = slots // 2
    load_g, load_w, load_far, load_own, load_sib = move(
        [(g_in, g_ref), (w1_in, w1_ref)] + [(w2_in.at[q], wg.at[q]) for q in (far, m, sib)], io
    )
    for copy in (load_far, load_g, load_w, load_own, load_sib):
        copy.start()
    greet(n, e, m, [sib, far])
    early = n // 2

    def x_copy(i):
        return remote(xs_ref.at[i - early], xr.at[i - early], xss.at[i], xsv.at[i], mate(e, i, n), m)

    def start_x(i, carry):
        x_copy(i).start()
        return carry

    def arrive_x(i, carry):
        x_copy(i).wait_recv()
        return carry

    lax.fori_loop(early, n, start_x, 0)
    to_sib = remote(wg.at[far], wg.at[far], wss, wsv, e, sib)
    from_sib = remote(wg.at[3 - m], wg.at[3 - m], wss, wsv, e, sib)
    load_far.wait()
    to_sib.start()

    def gate_col(i, carry):
        row = jnp.broadcast_to(gt[i, 0:1, :], (128, 128))
        gcol[pl.ds(pl.multiple_of(i * capq, 16), capq), :] = row.T[0:capq]
        return carry

    lax.fori_loop(0, n, gate_col, 0)
    gate = gcol[:, 0:1]
    load_g.wait()
    grad = (g_ref[...].astype(F32) * gate).astype(BF)
    dy[...] = grad
    db_ref[NARROW] = jnp.broadcast_to(jnp.sum(grad.astype(F32), axis=0, keepdims=True), (8, width))
    if lanes_each > capq:
        dxr_ref[:, capq:lanes_each, :] = jnp.zeros((n, lanes_each - capq, width), BF)

    cut = pl.ds(0, far1.shape[0])

    def d_copies(t, to):
        if t == 1:
            return [
                remote(s2.at[1], far2, ws.at[1, 1], wv.at[1, 1], e, to),
                remote(s1.at[1, cut], far1, ws.at[0, 1], wv.at[0, 1], e, to),
            ]
        return [
            remote(s1.at[t], r1.at[t], ws.at[0, t], wv.at[0, t], e, to),
            remote(s2.at[t], r2.at[t], ws.at[1, t], wv.at[1, t], e, to),
        ]

    def step(piece, t, q, fresh):
        at = pl.ds(piece * part, part)
        x = (x_early, xr)[piece][...].reshape(part, width)
        w1, w2 = w1_ref[q], wg[q]
        z = dot_nn(x, w1) + b1_ref[q, 0:1, :]
        cdf = 0.5 * (1.0 + lax.erf(z * (2.0**-0.5)))
        pdf = jnp.exp(-0.5 * z * z) * ((2.0 * jnp.pi) ** -0.5)
        u = (z * cdf).astype(BF)
        dz = dot_nt(dy[at, :], w2) * (cdf + z * pdf)
        db = jnp.broadcast_to(jnp.sum(dz, axis=0, keepdims=True), (8, dz.shape[1]))
        dz = dz.astype(BF)
        ypart, dxpart = dot_nn(u, w2), dot_nt(dz, w1)
        dw2, dw1 = dot_tn(u, dy[at, :]), dot_nn(xt[piece], dz)
        if fresh:
            yacc[at, :] = ypart
            dxacc[at, :] = dxpart
        else:
            yacc[at, :] += ypart
            dxacc[at, :] += dxpart
        if piece == 0:
            db_ref[q] = db
            s2[t] = dw2.astype(BF)
            s1[t] = dw1.astype(BF)
        else:
            db_ref[q] += db
            s2[t] = (s2[t].astype(F32) + dw2).astype(BF)
            s1[t] = (s1[t].astype(F32) + dw1).astype(BF)

    def dx_copy(i):
        return remote(
            dxs.at[i], dxr_ref.at[e, pl.ds(0, capq)], dxss.at[i], dxsv.at[i], mate(e, i, n), m
        )

    def dx_arrival(i):
        to = mate(e, i, n)
        return remote(dxs.at[i], dxr_ref.at[to, pl.ds(0, capq)], dxss.at[i], dxsv.at[i], to, m)

    def dg_copy(i, source):
        to = mate(e, i, n)
        return remote(dgs.at[i], dgr_ref.at[source], dgss.at[i], dgsv.at[i], to, m)

    def start_dx(i, carry):
        at = pl.ds(pl.multiple_of(i * capq, 16), capq)
        dxs[i] = dxacc[at, :].astype(BF)

        @pl.when(i > 0)
        def _():
            dx_copy(i).start()

        return carry

    xt[0] = x_early[...].reshape(part, width).T
    load_w.wait()
    load_own.wait()
    step(0, 3, m, True)
    load_sib.wait()
    step(0, 2, sib, False)
    step(0, 1, far, False)
    from_sib.wait_recv()
    step(0, 0, 3 - m, False)
    lax.fori_loop(0, n // 2, start_dx, 0)

    lax.fori_loop(early, n, arrive_x, 0)
    xt[1] = xr[...].reshape(part, width).T
    step(1, 0, 3 - m, True)
    for copy in d_copies(0, sib):
        copy.start()
    step(1, 1, far, False)
    for copy in d_copies(0, sib):
        copy.wait_recv()
    s2[1] = (s2[1].astype(F32) + r2[0].astype(F32)).astype(BF)
    across = d_copies(1, far)
    across[0].start()
    s1[1] = (s1[1].astype(F32) + r1[0].astype(F32)).astype(BF)
    across[1].start()
    keep = move([(s1.at[1], sum1_out), (s1.at[3], mine1_out), (s2.at[3], mine2_out), (gy_ref, gy_out)], io)
    keep[0].start()
    step(1, 2, sib, False)
    for copy in d_copies(2, sib):
        copy.start()
    step(1, 3, m, False)
    lax.fori_loop(n // 2, n, start_dx, 0)
    dxr_ref[e, 0:capq, :] = dxs[0]

    yv = yacc[...] + b2_ref[0:1, :]
    gy_ref[...] = (yv * gate).astype(BF)
    keep[3].start()
    gcol[...] = jnp.broadcast_to(
        jnp.sum(yv * g_ref[...].astype(F32), axis=1, keepdims=True), gcol.shape
    )
    wt[...] = jnp.zeros_like(wt)
    dgs[...] = jnp.zeros_like(dgs)
    per = max(1, 128 // lanes_each)

    def gate_row(i, carry):
        wt[0:capq, :] = gcol[pl.ds(pl.multiple_of(i * capq, 16), capq), :]
        row = wt[...].T[0:8, :]
        for k in range(per):

            @pl.when(lax.rem(e, per) == k)
            def _():
                dgs[i, :, k * lanes_each : (k + 1) * lanes_each] = row[:, 0:lanes_each]

        @pl.when(i > 0)
        def _():
            dg_copy(i, e).start()

        return carry

    lax.fori_loop(0, n, gate_row, 0)
    dgr_ref[e] = dgs[0]

    for copy in d_copies(2, sib):
        copy.wait_recv()
    s1[3] = (s1[3].astype(F32) + r1[2].astype(F32)).astype(BF)
    s2[3] = (s2[3].astype(F32) + r2[2].astype(F32)).astype(BF)
    keep[1].start()
    keep[2].start()

    def finish(i, carry):
        dx_arrival(i).wait_recv()
        dg_copy(i, mate(e, i, n)).wait_recv()
        dx_copy(i).wait_send()
        dg_copy(i, e).wait_send()
        return carry

    lax.fori_loop(1, n, finish, 0)

    def finish_x(i, carry):
        x_copy(i).wait_send()
        return carry

    lax.fori_loop(early, n, finish_x, 0)
    for copy in across:
        copy.wait_recv()
    for copy in keep:
        copy.wait()
    for t, to in ((0, sib), (1, far), (2, sib)):
        for copy in d_copies(t, to):
            copy.wait_send()
    to_sib.wait_send()


def experts(n, capq, lanes_each, xs, xr, gt, g, w1, w2, b1, b2):
    slots, width = g.shape
    hidden = w1.shape[2]
    struct = jax.ShapeDtypeStruct
    sem = pltpu.SemaphoreType.DMA
    one, two = (width, hidden), (hidden, width)
    outs = (
        struct((n, lanes_each, width), BF),
        struct((n, 8, 128), F32),
        struct((slots, width), BF),
        struct((NARROW + 1, 8, width), F32),
        struct(one, BF),
        struct(two, BF),
        struct(one, BF),
        struct(two, BF),
        struct((width // 4 * EARLY, hidden), BF),
    )
    args = (xs, xr, gt, b1, b2, g, w1, w2)
    here, away = pl.BlockSpec(memory_space=pltpu.VMEM), pl.BlockSpec(memory_space=pl.ANY)
    return pl.pallas_call(
        functools.partial(expert_kernel, n, capq, lanes_each),
        name="experts",
        out_shape=outs,
        in_specs=[here] * 5 + [away] * 3,
        out_specs=(here, here, away, here, away, away, away, here, here),
        scratch_shapes=[
            pltpu.VMEM(g.shape, BF),
            pltpu.VMEM(w1.shape, BF),
            pltpu.VMEM((slots, width), BF),
            sem((5,)),
            pltpu.VMEM((NARROW, *two), BF),
            pltpu.VMEM(xs.shape, BF),
            pltpu.VMEM((slots, 128), F32),
            pltpu.VMEM((slots, width), BF),
            pltpu.VMEM((2, width, slots // 2), BF),
            pltpu.VMEM((slots, width), F32),
            pltpu.VMEM((slots, width), F32),
            pltpu.VMEM((n, capq, width), BF),
            pltpu.VMEM((n, 8, 128), F32),
            pltpu.VMEM((128, 128), F32),
            pltpu.VMEM((4, *one), BF),
            pltpu.VMEM((4, *two), BF),
            pltpu.VMEM((3, *one), BF),
            pltpu.VMEM((3, *two), BF),
            sem,
            sem,
        ]
        + [sem((n,))] * 2
        + [sem((2, 3))] * 2
        + [sem((n,))] * 4,
        compiler_params=pltpu.CompilerParams(
            collective_id=3, has_side_effects=True, vmem_limit_bytes=LIMIT
        ),
    )(*args)


def backward_kernel(
    n,
    images,
    rows,
    capq,
    lanes_each,
    direct,
    share,
    owners,
    dxr_ref,
    dgr_ref,
    gy_ref,
    cols_ref,
    rpad_ref,
    vec_ref,
    db_ref,
    g_in,
    h_in,
    mats_in,
    q_in,
    k_in,
    v_in,
    p_in,
    x_in,
    o_in,
    a1_in,
    a2_in,
    sum1_in,
    fg_ref,
    po_ref,
    pgr,
    small_ref,
    router_ref,
    dbo_ref,
    far1,
    g_ref,
    h_ref,
    mats_ref,
    q_ref,
    k_ref,
    v_ref,
    p_ref,
    x_ref,
    o_ref,
    a1_ref,
    a2_ref,
    ins,
    gyr,
    oht,
    dlog,
    part,
    sa,
    sb,
    tot,
    dh,
    part2,
    tot2,
    sa2,
    sb2,
    dq,
    dk,
    dv,
    dr,
    acc,
    mine,
    mpv,
    exs,
    exv,
    dbm,
    dbv,
    pgs,
    ar,
    ar2,
    ppart,
    pin,
    pfar,
    fars,
    pss,
    gys,
    gyv,
    pgss,
    pgsr,
    mss,
    msr,
    dbs,
    dbr,
    ess,
    esr,
):
    e, m, c, y, sib, far = places()
    count, width = x_ref.shape
    half = width // 2
    heads = p_ref.shape[0]
    quarter = heads * HEAD
    each = width // n
    stride = NARROW * capq
    slots = n * lanes_each
    per = max(1, 128 // lanes_each)
    wide = acc.shape[0]
    here = pl.ds(0, capq)
    if lanes_each > capq:
        gyr[:, capq:lanes_each, :] = jnp.zeros((n, lanes_each - capq, width), BF)
    greet(n, e, m, [lax.rem(m + j, NARROW) for j in range(1, NARROW)])

    loads = move(
        [
            (g_in, g_ref),
            (h_in, h_ref),
            (mats_in, mats_ref),
            (q_in, q_ref),
            (k_in, k_ref),
            (v_in, v_ref),
            (p_in, p_ref),
            (x_in, x_ref),
            (o_in, o_ref),
            (a1_in, a1_ref),
            (a2_in, a2_ref),
        ],
        ins,
    )
    for copy in loads:
        copy.start()

    def gy_copy(i, source):
        to = mate(e, i, n)
        return remote(gy_ref.at[i], gyr.at[source, here], gys.at[i], gyv.at[i], to, m)

    def start_gy(i, carry):
        gy_copy(i, e).start()
        return carry

    lax.fori_loop(1, n, start_gy, 0)
    gyr[e, 0:capq, :] = gy_ref[0]
    dbm[...] = jnp.zeros_like(dbm)
    for j in range(NARROW + 1):
        dbm[j : j + 1, :] = db_ref[j, 0:1, :]

    def db_copy(j, source):
        return remote(dbm, dbv.at[source], dbs.at[j], dbr.at[j], e, lax.rem(m + j, NARROW))

    for j in range(1, NARROW):
        db_copy(j, m).start()
    dbv[m] = dbm[...]
    rest = far1.shape[0]
    first = rest // (4 - EARLY)
    far_copies = [
        remote(
            sum1_in.at[pl.ds(sum1_in.shape[0] - rest + lo, size)],
            far1.at[pl.ds(lo, size)],
            fars.at[i, 0],
            fars.at[i, 1],
            e,
            far,
        )
        for i, (lo, size) in enumerate([(0, first), (first, rest - first)])
    ]
    far_copies[0].start()

    gain0, gain1 = vec_ref[0:1, :], vec_ref[1:2, :]

    lane = lax.broadcasted_iota(jnp.int32, (1, slots), 1)
    place = lane % lanes_each
    want = (lane // lanes_each) * stride + place + m * capq
    want = jnp.where(place < capq, want, -2).astype(F32)
    pieces = []
    for block in range(n // per):
        piece = dgr_ref[block * per]
        for j in range(1, per):
            piece = piece + dgr_ref[block * per + j]
        pieces.append(piece[0:1, :])
    dgrow = jnp.concatenate(pieces, axis=1)
    acc[...] = jnp.zeros_like(acc)
    summed = Summed(rows, part, sa, sb, tot, ar)
    again = Summed(rows, part2, sa2, sb2, tot2, ar2)
    rfloor = lax.broadcasted_iota(jnp.int32, (1, 128), 1).astype(F32) * stride

    def returned(i):
        at = summed.at(i)
        key = [cols_ref[at, 0:1], cols_ref[at, 1:2]]
        gate = [cols_ref[at, 2:3], cols_ref[at, 3:4]]
        hits = [key[0] == want, key[1] == want]
        oht[at, :] = jnp.where(hits[0] | hits[1], 1.0, 0.0).astype(BF)
        dgate = [jnp.sum(jnp.where(hit, dgrow, 0.0), axis=1, keepdims=True) for hit in hits]
        mean = gate[0] * dgate[0] + gate[1] * dgate[1]
        dl = [
            jnp.where(
                (key[kk] >= rfloor) & (key[kk] < rfloor + stride), gate[kk] * (dgate[kk] - mean), 0.0
            )
            for kk in range(2)
        ]
        dl = (dl[0] + dl[1]).astype(BF)
        dlog[at, :] = dl
        for hh in range(2):
            cut = slice(hh * half, (hh + 1) * half)
            rowsum = dot_nn(oht[at, :], dxr_ref[:, :, cut].reshape(slots, half))
            part[hh, at] = (rowsum + dot_nn(dl, rpad_ref[:, cut])).astype(BF)

    in_b = head_masks(256, heads, BF)
    in_f = head_masks(256, heads, F32)
    scale = HEAD ** (-0.5)

    def attend(i):
        at = summed.at(i)
        da2 = summed.take(i)
        hidden = jnp.concatenate([h_ref[0, at], h_ref[1, at]], axis=1)
        normed, inverse = norm_parts(hidden)
        mixed = da2 * normed
        acc[1:2, :] += jnp.sum(mixed, axis=0, keepdims=True)
        acc[3:4, :] += jnp.sum(da2, axis=0, keepdims=True)
        mean_mixed = jnp.mean(mixed * gain1, axis=-1, keepdims=True)
        g2 = da2 * gain1
        mean_grad = jnp.mean(g2, axis=-1, keepdims=True)
        grad = g_ref[at, :].astype(F32) + inverse * (g2 - mean_grad - normed * mean_mixed)
        dh[at, :] = grad
        acc[6:7, :] += jnp.sum(grad, axis=0, keepdims=True)
        low = grad.astype(BF)
        dr[at, :] = low
        do = dot_nn(low, mats_ref[:, 768:1024]).astype(BF)
        q, k, v = q_ref[at, :], k_ref[at, :], v_ref[at, :]
        zero = jnp.zeros((rows, 256), F32)
        dqa, dka, dva = zero, zero, zero
        for h in range(heads):
            p = p_ref[h, at, :]
            dp = dot_nt(do * in_b[h], v)
            pf = p.astype(F32)
            t = pf * dp
            ds = (t - pf * jnp.sum(t, axis=-1, keepdims=True)).astype(BF)
            dqa = dqa + dot_nn(ds, k) * in_f[h]
            dka = dka + dot_tn(ds, q) * in_f[h]
            dva = dva + dot_tn(p, do) * in_f[h]
        dqb, dkb, dvb = (dqa * scale).astype(BF), (dka * scale).astype(BF), dva.astype(BF)
        dq[at, :], dk[at, :], dv[at, :] = dqb, dkb, dvb
        acc[4:5, 0:256] += jnp.sum(dqb.astype(F32), axis=0, keepdims=True)
        acc[5:6, 0:256] += jnp.sum(dvb.astype(F32), axis=0, keepdims=True)
        normed = norm_parts(x_ref[at, :].astype(F32))[0]
        for hh in range(2):
            r = slice(hh * half, (hh + 1) * half)
            da1 = (
                dot_nt(dqb, mats_ref[r, 0:256])
                + dot_nt(dkb, mats_ref[r, 256:512])
                + dot_nt(dvb, mats_ref[r, 512:768])
            )
            part2[hh, at] = da1.astype(BF)
            acc[0:1, r] += jnp.sum(da1 * normed[:, r], axis=0, keepdims=True)
            acc[2:3, r] += jnp.sum(da1, axis=0, keepdims=True)

    def last(i):
        at = again.at(i)
        da1 = again.take(i)
        normed, inverse = norm_parts(x_ref[at, :].astype(F32))
        g1 = da1 * gain0
        mean_mixed = jnp.mean(g1 * normed, axis=-1, keepdims=True)
        mean_grad = jnp.mean(g1, axis=-1, keepdims=True)
        dh[at, :] += inverse * (g1 - mean_grad - normed * mean_mixed)

    def tick(t, carry):
        @pl.when(t < images)
        def _():
            returned(t)
            summed.start_a(t)

        @pl.when((t >= 1) & (t <= images))
        def _():
            summed.step_b(t - 1)

        @pl.when((t >= 3) & (t <= images + 2))
        def _():
            summed.step_c(t - 3)

        @pl.when((t >= 4) & (t <= images + 3))
        def _():
            attend(t - 4)
            again.start_a(t - 4)

        @pl.when((t >= 5) & (t <= images + 4))
        def _():
            again.step_b(t - 5)

        @pl.when((t >= 7) & (t <= images + 6))
        def _():
            again.step_c(t - 7)

        @pl.when(t >= 8)
        def _():
            last(t - 8)

        return carry

    lax.fori_loop(0, 4, tick, 0)
    for copy in loads[0:8]:
        copy.wait()
    lax.fori_loop(4, images + 2, tick, 0)
    for copy in loads[8:]:
        copy.wait()
    lax.fori_loop(images + 2, images + 5, tick, 0)
    far_copies[1].start()

    acc[8:wide, :] = dot_tn(dlog[...], a2_ref[0:count, :])[0 : wide - 8]
    lane_w = lax.broadcasted_iota(jnp.int32, (1, width), 1)
    own_cols = (lane_w >= m * quarter) & (lane_w < (m + 1) * quarter)
    bias = acc[4:6, 0:quarter]
    acc[4:6, :] = jnp.zeros((2, width), F32)
    for row in (1, 3, 6):
        acc[row : row + 1, :] = jnp.where(own_cols, acc[row : row + 1, :], 0.0)
    for mm in range(NARROW):

        @pl.when(m == mm)
        def _():
            acc[4:6, mm * quarter : (mm + 1) * quarter] = bias

    def ex_copy(i):
        to = mate(e, i, n)
        return remote(exs.at[to], exv.at[i], ess.at[i], esr.at[i], to, m)

    def start_ex(i, carry):
        ex_copy(i).start()
        return carry

    def finish_ex(i, carry):
        ex_copy(i).wait_recv()
        return carry

    def narrow(j, source):
        return remote(mine, mpv.at[source], mss.at[j], msr.at[j], e, lax.rem(m + j, NARROW))

    if direct:
        exs[...] = jnp.zeros_like(exs)
        for i in range(n):
            exs[i, :, 0:each] = acc[:, i * each : (i + 1) * each]
        lax.fori_loop(1, n, start_ex, 0)
        exv[0] = exs[e]

    def pg_copy(b, i):
        to = mate(e, i, n)
        return remote(pgs.at[b, to], pgr.at[b, i], pgss.at[b, i], pgsr.at[b, i], to, m)

    pairs = [(dr, o_ref), (a1_ref, dq), (a1_ref, dk), (a1_ref, dv)]
    for b in range(2):
        for s in range(2):
            left, right = pairs[2 * b + s]
            grad = dot_tn(left[...], right[...])[:, :quarter]
            if direct:
                grad = grad.astype(BF)
                for i in range(n):
                    pgs[b, i, :, s * quarter : (s + 1) * quarter] = grad[i * each : (i + 1) * each]
            else:
                slot = 2 * b + s
                pgr[:, slot * quarter : (slot + 1) * quarter] = grad
        if direct:

            def start_pg(i, carry):
                pg_copy(b, i).start()
                return carry

            lax.fori_loop(1, n, start_pg, 0)
            pgr[b, 0] = pgs[b, e]

    def arrive_gy(i, carry):
        gy_copy(i, mate(e, i, n)).wait_recv()
        return carry

    lax.fori_loop(1, n, arrive_gy, 0)

    def combine(i, carry):
        at = summed.at(i)
        for hh in range(2):
            cut = slice(hh * half, (hh + 1) * half)
            ppart[hh, at] = dot_nn(oht[at, :], gyr[:, :, cut].reshape(slots, half)).astype(BF)
        return carry

    lax.fori_loop(0, images, combine, 0)
    both = count // 2
    own = pl.ds(pl.multiple_of(c * both, 16), both)
    other = pl.ds(pl.multiple_of((1 - c) * both, 16), both)
    copy_pa = [
        remote(
            ppart.at[hh, other], pin.at[pl.ds(hh * both, both)], pss.at[hh], pss.at[2 + hh], e, sib
        )
        for hh in range(2)
    ]
    for copy in copy_pa:
        copy.start()

    lax.fori_loop(images + 5, images + 6, tick, 0)
    if direct:
        lax.fori_loop(1, n, finish_ex, 0)
        total = exv[0]
        for i in range(1, n):
            total = total + exv[i]
        mine[...] = total
    else:
        mine[...] = acc[...]
    for j in range(1, NARROW):
        narrow(j, m).start()
    mpv[m] = mine[...]

    for copy in copy_pa:
        copy.wait_recv()
    for hh in range(2):
        pin[hh * both : (hh + 1) * both] = (
            ppart[hh, own].astype(F32) + pin[hh * both : (hh + 1) * both].astype(F32)
        ).astype(BF)
    send_to = pl.ds(pl.multiple_of((1 - y) * both, 16), both)
    keep_at = pl.ds(pl.multiple_of(y * both, 16), both)
    copy_pb = remote(pin.at[send_to], pfar, pss.at[4], pss.at[5], e, far)
    copy_pb.start()

    lax.fori_loop(images + 6, images + 8, tick, 0)
    summed.drain(images)
    again.drain(images)
    for i in range(images):
        fg_ref[i * SEQ : (i + 1) * SEQ, :] = dh[i * rows : i * rows + SEQ, :]

    for j in range(1, NARROW):
        narrow(j, lax.rem(m + NARROW - j, NARROW)).wait_recv()
    sums = mpv[0] + mpv[1] + mpv[2] + mpv[3]
    if direct:
        for mm in range(NARROW):

            @pl.when(m == mm)
            def _():
                small_ref[...] = sums[0:8, mm * share : (mm + 1) * share]

        router_ref[...] = sums[8 : 8 + owners, 0:each]
    else:
        small_ref[...] = sums[0:8]
        router_ref[...] = sums[8:wide]

    for j in range(1, NARROW):
        db_copy(j, lax.rem(m + NARROW - j, NARROW)).wait_recv()
    sums = dbv[0] + dbv[1] + dbv[2] + dbv[3]
    for mm in range(NARROW):

        @pl.when(m == mm)
        def _():
            dbo_ref[0:1, :] = sums[mm : mm + 1]

    dbo_ref[1:2, :] = sums[NARROW : NARROW + 1]

    copy_pb.wait_recv()
    total = pin[keep_at].astype(F32) + pfar[...].astype(F32) + h_ref[y, own]
    po_ref[own, :] = total.astype(BF)
    copy_pc = remote(po_ref.at[own], po_ref.at[own], pss.at[6], pss.at[7], e, sib)
    copy_pc.start()
    wait_pc = remote(po_ref.at[other], po_ref.at[other], pss.at[6], pss.at[7], e, sib)

    if direct:
        for b in range(2):

            def finish_pg(i, carry):
                pg_copy(b, i).wait_recv()
                return carry

            lax.fori_loop(1, n, finish_pg, 0)
    wait_pc.wait_recv()

    def drain(i, carry):
        gy_copy(i, e).wait_send()
        if direct:
            ex_copy(i).wait_send()
            pg_copy(0, i).wait_send()
            pg_copy(1, i).wait_send()
        return carry

    lax.fori_loop(1, n, drain, 0)
    for copy in copy_pa + [copy_pb, copy_pc] + far_copies + [
        each_copy(j, m) for each_copy in (narrow, db_copy) for j in range(1, NARROW)
    ]:
        copy.wait_send()
    for copy in far_copies:
        copy.wait_recv()


def backward(n, images, rows, capq, lanes_each, direct, share, owners, first, moved, sum1):
    x, p = moved[7], moved[6]
    count, width = x.shape
    half = width // 2
    heads = p.shape[0]
    quarter = heads * HEAD
    slots = n * lanes_each
    each = width // n
    sem = pltpu.SemaphoreType.DMA
    struct = jax.ShapeDtypeStruct
    extra = round_up(owners, 8)
    wide = 8 + extra
    block = (2, n, each, 2 * quarter)
    across = 128 if direct else width
    outs = (
        struct((images * SEQ, width), F32),
        struct((count, half), BF),
        struct(block, BF) if direct else struct((width, 4 * quarter), F32),
        struct((8, share if direct else width), F32),
        struct((owners, each) if direct else (extra, width), F32),
        struct((2, width), F32),
        struct((sum1.shape[0] // 4 * (4 - EARLY), sum1.shape[1]), BF),
    )
    args = (*first, *moved, sum1)
    here, away = pl.BlockSpec(memory_space=pltpu.VMEM), pl.BlockSpec(memory_space=pl.ANY)
    return pl.pallas_call(
        functools.partial(
            backward_kernel, n, images, rows, capq, lanes_each, direct, share, owners
        ),
        name="backward",
        out_shape=outs,
        in_specs=[here] * len(first) + [away] * len(moved) + [here],
        out_specs=(here,) * 7,
        scratch_shapes=[pltpu.VMEM(a.shape, a.dtype) for a in moved]
        + [
            sem((len(moved),)),
            pltpu.VMEM((n, lanes_each, width), BF),
            pltpu.VMEM((count, slots), BF),
            pltpu.VMEM((count, 128), BF),
            pltpu.VMEM((2, count, half), BF),
            pltpu.VMEM((count, half), BF),
            pltpu.VMEM((count, half), BF),
            pltpu.VMEM((2, count, half), BF),
            pltpu.VMEM((count, width), F32),
            pltpu.VMEM((2, count, half), BF),
            pltpu.VMEM((2, count, half), BF),
            pltpu.VMEM((count, half), BF),
            pltpu.VMEM((count, half), BF),
            pltpu.VMEM((count, 256), BF),
            pltpu.VMEM((count, 256), BF),
            pltpu.VMEM((count, 256), BF),
            pltpu.VMEM((count, width), BF),
            pltpu.VMEM((wide, width), F32),
            pltpu.VMEM((wide, across), F32),
            pltpu.VMEM((NARROW, wide, across), F32),
            pltpu.VMEM((n, wide, 128) if direct else (1, 8, 128), F32),
            pltpu.VMEM((n, wide, 128) if direct else (1, 8, 128), F32),
            pltpu.VMEM((8, width), F32),
            pltpu.VMEM((NARROW, 8, width), F32),
            pltpu.VMEM(block if direct else (1, 1, 16, 128), BF),
            sem((6, images)),
            sem((6, images)),
            pltpu.VMEM((2, count, half), BF),
            pltpu.VMEM((count, half), BF),
            pltpu.VMEM((count // 2, half), BF),
            sem((2, 2)),
            sem((8,)),
        ]
        + [sem((n,))] * 2
        + [sem((2, n))] * 2
        + [sem((NARROW,))] * 4
        + [sem((n,))] * 2,
        compiler_params=pltpu.CompilerParams(
            collective_id=2, has_side_effects=True, vmem_limit_bytes=LIMIT
        ),
    )(*args)


def finish_kernel(
    images,
    rows,
    fg_in,
    po_ref,
    pgr_ref,
    small_ref,
    router_in,
    dbo_ref,
    mine1,
    far1a,
    far1b,
    mine2,
    far2,
    out_ref,
    fg_ref,
    gain_ref,
    shift_ref,
    bias_ref,
    oshift_ref,
    pg_ref,
    mg_ref,
    router_ref,
    d1_ref,
    e1_ref,
    d2_ref,
    e2_ref,
    flat,
    tall,
    turn,
    sem,
):
    copy = pltpu.make_async_copy(fg_in, fg_ref, sem)
    copy.start()
    c = lax.rem(lax.axis_index("mp"), 2)
    quarter = out_ref.shape[0]
    for half in range(2):

        @pl.when(c == half)
        def _():
            flat[...] = po_ref[:, half * quarter : (half + 1) * quarter].astype(F32)

    for i in range(images):
        tall[i * SEQ : (i + 1) * SEQ, 0:quarter] = flat[i * rows : i * rows + SEQ, :]
    out_ref[...] = tall[...].T[0:quarter, 0 : images * SEQ].astype(BF)
    gain_ref[...] = small_ref[0:2]
    shift_ref[...] = small_ref[2:4]
    bias_ref[...] = small_ref[4:6]
    oshift_ref[...] = small_ref[6:7]
    router_ref[...] = router_in[...]
    e1_ref[...] = dbo_ref[0:1]
    e2_ref[...] = dbo_ref[1:2]
    totals = []
    for b in range(2):
        total = pgr_ref[b, 0].astype(F32)
        for i in range(1, pgr_ref.shape[1]):
            total = total + pgr_ref[b, i].astype(F32)
        totals.append(total)
    each = totals[0].shape[0]
    turn[0:each, 0:quarter] = totals[0][:, 0:quarter]
    mg_ref[...] = turn[...].T[0:quarter, 0:each]
    pg_ref[0] = totals[0][:, quarter:]
    pg_ref[1] = totals[1][:, 0:quarter]
    pg_ref[2] = totals[1][:, quarter:]
    cut = far1a.shape[0]
    d1_ref[0, 0:cut] = mine1[0:cut].astype(F32) + far1a[...].astype(F32)
    d1_ref[0, cut:] = mine1[cut:].astype(F32) + far1b[...].astype(F32)
    d2_ref[0] = mine2[...].astype(F32) + far2[...].astype(F32)
    copy.wait()


def finish(images, rows, quarter, args):
    fg, po, pgr, small, router, dbo, mine1 = args[:7]
    count, width = fg.shape
    each, share = pgr.shape[2], small.shape[1]
    struct = jax.ShapeDtypeStruct
    outs = (
        struct((quarter, count), BF),
        struct(fg.shape, F32),
        struct((2, share), F32),
        struct((2, share), F32),
        struct((2, share), F32),
        struct((1, share), F32),
        struct((3, each, quarter), F32),
        struct((quarter, each), F32),
        struct(router.shape, F32),
        struct((1, *mine1.shape), F32),
        struct((1, width), F32),
        struct((1, *args[9].shape), F32),
        struct((1, width), F32),
    )
    here, away = pl.BlockSpec(memory_space=pltpu.VMEM), pl.BlockSpec(memory_space=pl.ANY)
    return pl.pallas_call(
        functools.partial(finish_kernel, images, rows),
        name="finish",
        out_shape=outs,
        in_specs=[here] * len(args),
        out_specs=(here, away) + (here,) * (len(outs) - 2),
        scratch_shapes=[
            pltpu.VMEM((po.shape[0], quarter), F32),
            pltpu.VMEM((round_up(count, 128), 256), F32),
            pltpu.VMEM((128, 256), F32),
            pltpu.SemaphoreType.DMA,
        ],
        compiler_params=pltpu.CompilerParams(vmem_limit_bytes=LIMIT),
    )(*args)


def on_device(
    features,
    norm_gains,
    norm_shifts,
    attention_bias,
    output_bias,
    project_weight,
    merge_weight,
    router_weight,
    router_noise,
    routes,
    slot_numbers,
    expand_weight,
    expand_bias,
    contract_weight,
    contract_bias,
    cotangent,
):
    count, width = features.shape
    n = lax.axis_size("expert")
    e, m = lax.axis_index("expert"), lax.axis_index("mp")
    capacity = 3 * count // n
    quarter = project_weight.shape[2]
    heads = quarter // HEAD
    images = count // SEQ
    rows = round_up(SEQ, 16)
    capq = round_up(-(-capacity // NARROW), 16)
    lanes_each = 16
    while lanes_each < capq:
        lanes_each *= 2
    each = width // n
    direct = each % 16 == 0
    owners = router_weight.shape[1]
    extra = round_up(owners, 8)

    share = norm_gains.shape[1]
    if direct:
        params = (
            project_weight.transpose(1, 0, 2),
            merge_weight,
            router_weight.T,
            norm_gains,
            norm_shifts,
            attention_bias,
            output_bias[None],
            expand_bias,
        )
    else:
        low = project_weight.astype(BF)
        mat = jnp.concatenate([merge_weight.T.astype(BF), low[:, 0], low[:, 1], low[:, 2]], axis=1)
        packed = jnp.concatenate(
            [norm_gains, norm_shifts, attention_bias, output_bias[None], jnp.zeros((1, share), F32)]
        )
        rout = lax.all_gather(router_weight.astype(BF), "expert", axis=0, tiled=True).T
        first = lax.all_gather(expand_bias, "mp", axis=0)
        params = (
            lax.all_gather(mat, "expert", axis=0, tiled=True),
            lax.all_gather(packed, ("expert", "mp"), axis=1, tiled=True),
            jnp.pad(rout, ((0, 128 - owners), (0, 0))),
            jnp.broadcast_to(first, (NARROW, 8, width)),
        )
    g, x, a1, q, k, v, p, o, h, a2, mats, w1, gr, w2, cols, rpad, vecs, b1, xs, xr, gt = forward(
        n,
        images,
        rows,
        capq,
        heads,
        direct,
        share,
        extra,
        params,
        features,
        cotangent,
        routes.T,
        slot_numbers.T,
        router_noise.T,
        expand_weight,
        contract_weight,
    )
    slots = n * capq
    dxr, dgr, gy, db, mine1, mine2, sum1, far2, far1a = experts(
        n, capq, lanes_each, xs, xr, gt, gr.reshape(slots, width), w1, w2, b1, contract_bias
    )
    fg, po, pgr, small, router_share, dbo, far1b = backward(
        n,
        images,
        rows,
        capq,
        lanes_each,
        direct,
        share,
        owners,
        (dxr, dgr, gy.reshape(n, capq, width), cols, rpad, vecs, db),
        (g, h, mats, q, k, v, p, x, o, a1, a2),
        sum1,
    )
    if not direct:
        small = lax.psum_scatter(small, "expert", scatter_dimension=1, tiled=True)
        small = lax.dynamic_slice_in_dim(small, m * share, share, 1)
        pg = lax.psum_scatter(pgr, "expert", scatter_dimension=0, tiled=True)
        pgr = jnp.stack([pg[:, : 2 * quarter], pg[:, 2 * quarter :]])[:, None]
        router_share = lax.psum_scatter(
            router_share[:owners].T, "expert", scatter_dimension=0, tiled=True
        ).T
    done = finish(
        images,
        rows,
        quarter,
        (fg, po, pgr, small, router_share, dbo, mine1, far1a, far1b, mine2, far2),
    )
    out, fg, gain, shift, bias, oshift, pg, mg, router_share, d1, e1, d2, e2 = done
    return (
        out.T,
        fg,
        gain,
        shift,
        bias,
        oshift[0],
        pg.transpose(1, 0, 2),
        mg,
        router_share.T,
        d1,
        e1,
        d2,
        e2,
    )


def solution(mesh):
    placed = (
        P("expert", None),
        P(None, ("expert", "mp")),
        P(None, ("expert", "mp")),
        P(None, ("expert", "mp")),
        P(("expert", "mp")),
        P("expert", None, "mp"),
        P("mp", "expert"),
        P("expert", None),
        P("expert", None),
        P("expert", None),
        P("expert", None),
        P("expert", None, "mp"),
        P("expert", "mp"),
        P("expert", "mp", None),
        P("expert", None),
        P("expert", None),
    )
    return jax.shard_map(
        on_device,
        mesh=mesh,
        in_specs=placed,
        out_specs=(
            P("expert", "mp"),
            P("expert", None),
            P(None, ("expert", "mp")),
            P(None, ("expert", "mp")),
            P(None, ("expert", "mp")),
            P(("expert", "mp")),
            P("expert", None, "mp"),
            P("mp", "expert"),
            P("expert", None),
            P("expert", None, "mp"),
            P("expert", "mp"),
            P("expert", "mp", None),
            P("expert", None),
        ),
        check_vma=False,
    )
```
